256 devices in a mesh: gx: 32 (over x, z_lo, core), gy: 8 (over y, z_hi).
Axes of the slice: x: 4, y: 4, z: 8 (z_hi: 2, z_lo: 4; z = z_hi * 4 + z_lo), core: 2. Of those that a mesh axis runs over, the one named last changes fastest.
Arguments:
- temp_old: float32 [512, 256, 1024], P('gx', 'gy'), may hold values from -6 to 6
- capacity: float32 [512, 256, 1024], P('gx', 'gy'), may hold values from 0.05 to 0.5
- soil_class: int32 [512, 256, 1024], P('gx', 'gy'), may hold values from 0 to 7
- cond_table: float32 [8], replicated, may hold values from 0.3 to 3
- losses: float32 [65536, 128], P(('gx', 'gy')), may hold values from 0.1 to 10
- owner: int32 [65536, 1], P(('gx', 'gy')), may hold values from 0 to 7; in each aligned block of 256 rows (0 to 255, 256 to 511, ...) at most 64 rows name the same one
- column: int32 [65536], P(('gx', 'gy')), may hold values from 0 to 511
- injection: float32 [128, 1024], replicated, may hold values from -0.5 to 0.5
Outputs:
- temp_new: float32 [512, 256, 1024], P('gx', 'gy')
The draws below stay inside these ranges and needn't reach their ends.
Inputs may be any that keep to these rules, and one draw needn't show every extreme that they name: In each device's block of 256 rows no owner is named by more than 64 rows, a bound that some block reaches.
All inputs are finite; a program needn't handle non-finite values.
Results may differ from the reference program's by a relative error of at most 0.000061.
Values sent between devices are 32-bit elements; how exact they have to be, the bound alone decides.
No kernel may reach another device: no remote copies, remote signals or barrier semaphores. Data moves between devices by JAX's collectives and lax.ppermute only.
A program may use at most 64 MiB of HBM per device.

```python
import math
import jax
import jax.numpy as jnp
import numpy as np
from jax import lax

CX = 16
CY = 32
NZ = 1024
SWEEPS = 4
NCLS = 8
LW = 128
SEG_DEV = 256
CAP = 64
NX = 512
NY = 256
NSEG = 65536
N_GY = 8


def with_ends(values, rng, smallest, top_value):
    longest = values.shape.index(max(values.shape))
    spots = []
    for shift in (0, 1):
        where = [jax.random.randint(jax.random.fold_in(rng, axis), (), 0, length) for axis, length in enumerate(values.shape)]
        where[longest] = (where[longest] + shift) % values.shape[longest]
        spots.append(tuple(where))
    return values.at[spots[0]].set(smallest).at[spots[1]].set(top_value)


def shard_levels(rng, dims, pieces, low, largest):
    def one(axis_at, shards_of):
        draws = jax.random.uniform(jax.random.fold_in(jax.random.fold_in(rng, 6), axis_at), (shards_of,), jnp.float32, low / len(pieces), largest / len(pieces))
        return jnp.repeat(jnp.exp(draws), dims[axis_at] // shards_of).reshape((-1,) + (1,) * (len(dims) - axis_at - 1))

    loudness = one(*pieces[0])
    for cut in pieces[1:]:
        loudness = loudness * one(*cut)
    return loudness


def routed_block(own_key, own, number, rows, count, top, reach, slope):
    order = jax.random.permutation(own_key, count)
    crowded, ordinary = shares(count, rows * top, reach, slope, True), shares(count, rows * top, reach, slope, False)
    places = jnp.arange(count)

    def named(tallies, rotation):
        used = int((tallies > 0).sum())
        fixed = max(1, used // 4)
        shifted = fixed + (places - fixed + rotation * (used - fixed)) % max(1, count - fixed)
        return jnp.zeros((count,), jnp.int32).at[order[jnp.where(places < fixed, places, shifted)]].set(jnp.asarray(tallies, jnp.int32))

    tallies = jnp.where(number % 4 == 0, named(crowded, number // 4), named(ordinary, number - number // 4 - 1))
    mixed = jax.random.permutation(jax.random.fold_in(own, 3), count)
    source_of, sink = mixed[0:count // 2 * 2:2], mixed[1:count // 2 * 2:2]
    margin = jnp.minimum(tallies[source_of] - 1, reach - tallies[sink]) // 2
    margin = jnp.where((source_of == order[0]) | (sink == order[0]) | (tallies[sink] == 0), 0, jnp.maximum(margin, 0))
    shifted = jax.random.randint(jax.random.fold_in(own, 4), (count // 2,), 0, 1 << 20) % (margin + 1)
    tallies = tallies.at[source_of].add(-shifted).at[sink].add(shifted)
    labels = jnp.searchsorted(jnp.cumsum(tallies), jnp.arange(rows * top), side="right").astype(jnp.int32)
    grid = labels.reshape(top, rows).T
    grid = grid[jax.random.permutation(jax.random.fold_in(own, 1), rows)]
    rotation = jax.random.randint(jax.random.fold_in(own, 2), (rows, 1), 0, top)
    return jnp.take_along_axis(grid, (jnp.arange(top)[None, :] + rotation) % top, axis=1)


def shares(amount, total, bound, lean, full):
    portions = [(1 << 20) // math.isqrt(grade ** lean) + 1 for grade in range(1, amount + 1)]
    largest = bound if full else min(bound, max(-(-total // amount), total * portions[0] // sum(portions)))
    least = 1 if total - largest >= amount - 1 else 0
    counts, spare = [largest] + [least] * (amount - 1), total - largest - least * (amount - 1)
    while spare > 0:
        movable = [i for i in range(1, amount) if counts[i] < largest] or [i for i in range(1, amount) if counts[i] < bound]
        whole, budget = sum([portions[i] for i in movable]), spare
        for i in movable:
            addition = min(bound - counts[i], max(1, budget * portions[i] // whole), spare)
            counts[i] = counts[i] + addition
            spare = spare - addition
    return np.array(counts)


def noise(own_key, extent, deviation, most, split=(), kind=jnp.bfloat16):
    drawn = jax.random.normal(own_key, extent, jnp.float32) * deviation
    if len(split) > 0:
        drawn = shard_levels(own_key, extent, split, -0.22, 0.18) * drawn
    return jnp.clip(drawn, min=-most, max=most).astype(kind)


def setup_inputs(seed: int = 0) -> dict:
    keys = jax.random.split(jax.random.key(seed), 9)
    temp_old = noise(keys[0], (NX, NY, NZ), 1.0, 6.0, ((0, 32), (1, 8)), jnp.float32)
    capacity = jnp.clip(jnp.exp(math.log(0.5) - 2.3025851 * jax.random.uniform(keys[1], (NX, NY, NZ), jnp.float32) ** shard_levels(keys[1], (NX, NY, NZ), ((0, 32), (1, 8)), -0.2, 0.2)), 0.05, 0.5)
    soil_class = with_ends(jax.random.randint(keys[2], (NX, NY, NZ), 0, NCLS), jax.random.fold_in(keys[2], 1), 0, NCLS - 1).astype(jnp.int32)
    cond_table = jnp.clip(jnp.exp(jax.random.uniform(keys[3], (NCLS,), jnp.float32, math.log(0.3), math.log(3.0))), 0.3, 3.0)
    losses = jnp.clip(jnp.exp(math.log(10.0) - 4.6051702 * jax.random.uniform(keys[4], (NSEG, LW), jnp.float32) ** shard_levels(keys[4], (NSEG, LW), ((0, 256),), -0.2, 0.2)), 0.1, 10.0)
    owner_keys = jax.random.split(jax.random.fold_in(keys[5], 1), NSEG // SEG_DEV)
    owner_turns = jax.random.permutation(jax.random.fold_in(keys[5], 3), NSEG // SEG_DEV)
    owner = jax.vmap(lambda own, number: routed_block(jax.random.fold_in(keys[5], 2), own, number, SEG_DEV, N_GY, 1, CAP, 2))(owner_keys, owner_turns).reshape((NSEG, 1))
    column = with_ends(jax.random.randint(keys[6], (NSEG,), 0, CX * CY), jax.random.fold_in(keys[6], 1), 0, (CX * CY) - 1).astype(jnp.int32)
    injection = noise(keys[7], (LW, NZ), LW ** -0.5, 0.5, (), jnp.float32)
    return dict(temp_old=temp_old, capacity=capacity, soil_class=soil_class, cond_table=cond_table, losses=losses, owner=owner, column=column, injection=injection)


def face_terms(cond_pad):
    center = cond_pad[1:-1, 1:-1, 1:-1]
    return [0.5 * (center + cond_pad[2:, 1:-1, 1:-1]), 0.5 * (center + cond_pad[:-2, 1:-1, 1:-1]),
            0.5 * (center + cond_pad[1:-1, 2:, 1:-1]), 0.5 * (center + cond_pad[1:-1, :-2, 1:-1]),
            0.5 * (center + cond_pad[1:-1, 1:-1, 2:]), 0.5 * (center + cond_pad[1:-1, 1:-1, :-2])]


def neighbour_sum(faces, temp_pad):
    total = faces[0] * temp_pad[2:, 1:-1, 1:-1] + faces[1] * temp_pad[:-2, 1:-1, 1:-1]
    total = total + faces[2] * temp_pad[1:-1, 2:, 1:-1] + faces[3] * temp_pad[1:-1, :-2, 1:-1]
    total = total + faces[4] * temp_pad[1:-1, 1:-1, 2:] + faces[5] * temp_pad[1:-1, 1:-1, :-2]
    return total


def reference(temp_old, capacity, soil_class, cond_table, losses, owner, column, injection):
    cond = jnp.zeros(temp_old.shape, jnp.float32)
    for klass in range(NCLS):
        cond = cond + jnp.where(soil_class == klass, cond_table[klass], jnp.float32(0.0))
    faces = face_terms(jnp.pad(cond, 1))
    diag = capacity + faces[0] + faces[1] + faces[2] + faces[3] + faces[4] + faces[5]
    profile = jnp.dot(losses, injection, precision=lax.Precision.HIGHEST, preferred_element_type=jnp.float32)
    rows = jnp.arange(NSEG, dtype=jnp.int32)
    row_x = (rows // SEG_DEV // N_GY) * CX + column // CY
    row_y = owner[:, 0] * CY + column % CY
    source = jnp.zeros((NX * NY, NZ), jnp.float32).at[row_x * NY + row_y].add(profile)
    rhs = capacity * temp_old + source.reshape(NX, NY, NZ)
    temp = temp_old
    for sweep in range(SWEEPS):
        nbsum = neighbour_sum(faces, jnp.pad(temp, 1))
        temp = temp + 0.8 * (rhs - diag * temp + nbsum) / diag
    return temp
```

```python
import jax
import jax.numpy as jnp
from jax import lax
from jax.experimental import pallas as pl
from jax.experimental.pallas import tpu as pltpu
from jax.sharding import PartitionSpec as P

SWEEPS = 4
NCLS = 8
CX, CY, NZ = 16, 32, 1024
LW = 128
SEG = 256
CAP = 64
NGX, NGY = 32, 8
CHUNK = CAP + 8
YT = 8
F32 = jnp.float32
HIGH = lax.Precision.HIGHEST
VMEM_LIMIT = 12 * 1024 * 1024
VM = pl.BlockSpec(memory_space=pltpu.VMEM)
SM = pl.BlockSpec(memory_space=pltpu.SMEM)


def shape(*dims):
    return pltpu.VMEM(dims, F32)


def near(*arrays):
    return [pltpu.with_memory_space_constraint(a, pltpu.VMEM) for a in arrays]


def lookup(klass, table):
    cond = jnp.where(klass == 0, table[0], F32(0.0))
    for k in range(1, NCLS):
        cond = jnp.where(klass == k, table[k], cond)
    return cond


def pack_kernel(table_ref, t_ref, soil_ref, loss_ref, owner_ref, col_ref, xlo, xhi, ylo, yhi, send_ref):
    table = [table_ref[k] for k in range(NCLS)]
    for out, x in ((xlo, 0), (xhi, CX - 1)):
        out[0:CY, :] = t_ref[x]
        out[CY:, :] = lookup(soil_ref[x], table)
    for out, y in ((ylo, 0), (yhi, CY - 1)):
        for x in range(CX):
            out[x:x + 1, :] = t_ref[x, y:y + 1, :]
            out[CX + x:CX + x + 1, :] = soil_ref[x, y:y + 1, :].astype(F32)
        out[CX:, :] = lookup(out[CX:, :].astype(jnp.int32), table)
    own = owner_ref[...]
    mine = lax.broadcasted_iota(jnp.int32, (NGY, SEG), 0) == own
    before = lax.broadcasted_iota(jnp.int32, (SEG, SEG), 0) < lax.broadcasted_iota(jnp.int32, (SEG, SEG), 1)
    count = jnp.dot(mine.astype(jnp.bfloat16), before.astype(jnp.bfloat16), preferred_element_type=F32)
    rank = jnp.sum(jnp.where(mine, count, 0.0), axis=0, keepdims=True).astype(jnp.int32)
    slot = own * CAP + rank
    cols = jnp.broadcast_to(col_ref[...].astype(F32), (8, SEG))
    loss = loss_ref[...]
    for o in range(NGY):
        pick = (lax.broadcasted_iota(jnp.int32, (CAP, SEG), 0) + o * CAP == slot).astype(F32)
        send_ref[o * CHUNK:o * CHUNK + CAP, :] = jnp.dot(pick, loss, precision=HIGH, preferred_element_type=F32)
        crow = lax.dot_general(cols, pick, (((1,), (1,)), ((), ())), precision=HIGH, preferred_element_type=F32)
        send_ref[o * CHUNK + CAP:(o + 1) * CHUNK, :] = jnp.concatenate([crow, crow], axis=1)


def update(t, sides, faces, w, rhs):
    total = rhs
    for face, side in zip(faces, sides):
        total = total + face * side
    return (1.0 - 0.8) * t + w * total


def tile_sides(ref, x, base, yt, lo_row, hi_row):
    mid = ref[x + base, yt * YT:(yt + 1) * YT, :]
    row = lax.broadcasted_iota(jnp.int32, (YT, NZ), 0)
    after = ref[x + base, (yt + 1) * YT:(yt + 1) * YT + 1, :] if yt < CY // YT - 1 else hi_row
    before = ref[x + base, yt * YT - 1:yt * YT, :] if yt > 0 else lo_row
    up = jnp.where(row == YT - 1, after, pltpu.roll(mid, YT - 1, 0))
    down = jnp.where(row == 0, before, pltpu.roll(mid, 1, 0))
    return mid, up, down


def depth_sides(mid):
    lane = lax.broadcasted_iota(jnp.int32, (YT, NZ), 1)
    up = jnp.where(lane == NZ - 1, F32(0.0), pltpu.roll(mid, NZ - 1, 1))
    down = jnp.where(lane == 0, F32(0.0), pltpu.roll(mid, 1, 1))
    return up, down


def start_kernel(pos_ref, table_ref, t_ref, cap_ref, soil_ref, hxlo, hxhi, hylo, hyhi, recv_ref, inj_ref,
                 tn_ref, fx_ref, fy_ref, fylo_ref, fz_ref, w_ref, rhs_ref, xlo, xhi, ylo, yhi, cond, tx):
    gx, gy = pos_ref[0], pos_ref[1]
    in_xlo = (gx > 0).astype(F32)
    in_xhi = (gx < NGX - 1).astype(F32)
    in_ylo = (gy > 0).astype(F32)
    in_yhi = (gy < NGY - 1).astype(F32)
    table = [table_ref[k] for k in range(NCLS)]
    cell = lax.broadcasted_iota(jnp.int32, (CX * CY, CAP), 0)
    gathered = jnp.zeros((CX * CY, LW), F32)
    for g in range(NGY):
        crow = recv_ref[g * CHUNK + CAP:g * CHUNK + CAP + 1, 0:CAP].astype(jnp.int32)
        pick = (cell == crow).astype(F32)
        gathered = gathered + jnp.dot(pick, recv_ref[g * CHUNK:g * CHUNK + CAP, :], precision=HIGH, preferred_element_type=F32)
    source = jnp.dot(gathered, inj_ref[...], precision=HIGH, preferred_element_type=F32)
    rhs_ref[...] = source.reshape(CX, CY, NZ)
    cond[0] = hxlo[CY:, :] * in_xlo
    cond[CX + 1] = hxhi[CY:, :] * in_xhi
    tx[0] = hxlo[0:CY, :] * in_xlo
    tx[CX + 1] = hxhi[0:CY, :] * in_xhi

    def fill(x, carry):
        cond[x + 1] = lookup(soil_ref[x], table)
        tx[x + 1] = t_ref[x]
        return carry

    lax.fori_loop(0, CX, fill, 0)
    row = lax.broadcasted_iota(jnp.int32, (YT, NZ), 0)

    def plane(x, carry):
        for yt in range(CY // YT):
            rows = slice(yt * YT, (yt + 1) * YT)
            c, cyp, cym = tile_sides(cond, x, 1, yt, hylo[pl.ds(CX + x, 1), :] * in_ylo, hyhi[pl.ds(CX + x, 1), :] * in_yhi)
            czp, czm = depth_sides(c)
            fxp = 0.5 * (c + cond[x + 2, rows, :])
            fxm = 0.5 * (c + cond[x, rows, :])
            fyp, fym = 0.5 * (c + cyp), 0.5 * (c + cym)
            fzp, fzm = 0.5 * (c + czp), 0.5 * (c + czm)
            cap = cap_ref[x, rows, :]
            diag = cap + fxp + fxm + fyp + fym + fzp + fzm
            w = 0.8 / diag
            t, typ, tym = tile_sides(tx, x, 1, yt, hylo[pl.ds(x, 1), :] * in_ylo, hyhi[pl.ds(x, 1), :] * in_yhi)
            tzp, tzm = depth_sides(t)
            rhs = rhs_ref[x, rows, :] + cap * t
            rhs_ref[x, rows, :] = rhs
            w_ref[x, rows, :] = w
            fx_ref[x + 1, rows, :] = fxp
            if yt == CY // YT - 1:
                fyk = jnp.where(row == YT - 1, fyp * in_yhi, fyp)
            else:
                fyk = fyp
            fy_ref[x, rows, :] = fyk
            if yt == 0:
                fylo_ref[pl.ds(x, 1), :] = fym[0:1, :] * in_ylo
            fz_ref[x, rows, :] = fzp
            tn = update(t, (tx[x + 2, rows, :], tx[x, rows, :], typ, tym, tzp, tzm), (fxp, fxm, fyp, fym, fzp, fzm), w, rhs)
            tn_ref[x, rows, :] = tn
            if yt == 0:
                ylo[pl.ds(x, 1), :] = tn[0:1, :]
            if yt == CY // YT - 1:
                yhi[pl.ds(x, 1), :] = tn[YT - 1:YT, :]
        return carry

    fx_ref[0] = 0.5 * (cond[0] + cond[1]) * in_xlo
    lax.fori_loop(0, CX, plane, 0)
    fx_ref[CX] = fx_ref[CX] * in_xhi
    xlo[...] = tn_ref[0]
    xhi[...] = tn_ref[CX - 1]


def sweep_kernel(t_ref, fx_ref, fy_ref, fylo_ref, fz_ref, w_ref, rhs_ref, hxlo, hxhi, hylo, hyhi, tn_ref, *edges):
    row = lax.broadcasted_iota(jnp.int32, (YT, NZ), 0)
    lane = lax.broadcasted_iota(jnp.int32, (YT, NZ), 1)

    def plane(x, first, last):
        for yt in range(CY // YT):
            rows = slice(yt * YT, (yt + 1) * YT)
            t, typ, tym = tile_sides(t_ref, x, 0, yt, hylo[pl.ds(x, 1), :], hyhi[pl.ds(x, 1), :])
            txm = hxlo[rows, :] if first else t_ref[x - 1, rows, :]
            txp = hxhi[rows, :] if last else t_ref[x + 1, rows, :]
            fy, fybefore = fy_ref[x, rows, :], None
            fybefore = fylo_ref[pl.ds(x, 1), :] if yt == 0 else fy_ref[x, yt * YT - 1:yt * YT, :]
            fym = jnp.where(row == 0, fybefore, pltpu.roll(fy, 1, 0))
            fz = fz_ref[x, rows, :]
            tzp = pltpu.roll(t, NZ - 1, 1)
            total = rhs_ref[x, rows, :] + fx_ref[x + 1, rows, :] * txp + fx_ref[x, rows, :] * txm
            total = total + fy * typ + fym * tym
            total = total + jnp.where(lane == NZ - 1, F32(0.0), fz * tzp)
            total = total + jnp.where(lane == 0, F32(0.0), pltpu.roll(fz * t, 1, 1))
            tn = (1.0 - 0.8) * t + w_ref[x, rows, :] * total
            tn_ref[x, rows, :] = tn
            if edges:
                if yt == 0:
                    edges[2][pl.ds(x, 1), :] = tn[0:1, :]
                if yt == CY // YT - 1:
                    edges[3][pl.ds(x, 1), :] = tn[YT - 1:YT, :]

    def body(x, carry):
        plane(x, False, False)
        return carry

    plane(0, True, False)
    lax.fori_loop(1, CX - 1, body, 0)
    plane(CX - 1, False, True)
    if edges:
        edges[0][...] = tn_ref[0]
        edges[1][...] = tn_ref[CX - 1]


def exchange(xlo, xhi, ylo, yhi):
    upx = [(i, (i + 1) % NGX) for i in range(NGX)]
    upy = [(i, (i + 1) % NGY) for i in range(NGY)]
    hylo = lax.ppermute(yhi, "gy", upy)
    hyhi = lax.ppermute(ylo, "gy", [(j, i) for i, j in upy])
    hxlo = lax.ppermute(xhi, "gx", upx)
    hxhi = lax.ppermute(xlo, "gx", [(j, i) for i, j in upx])
    return hxlo, hxhi, hylo, hyhi


PARAMS = pltpu.CompilerParams(vmem_limit_bytes=VMEM_LIMIT)
SLAB = shape(CX, CY, NZ)
XF, YF = shape(CY, NZ), shape(CX, NZ)


def shards(temp_old, capacity, soil_class, cond_table, losses, owner, column, injection):
    pos = jnp.stack([lax.axis_index("gx"), lax.axis_index("gy")]).astype(jnp.int32)
    xlo, xhi, ylo, yhi, send = pl.pallas_call(
        pack_kernel,
        out_shape=(shape(2 * CY, NZ), shape(2 * CY, NZ), shape(2 * CX, NZ), shape(2 * CX, NZ), shape(NGY * CHUNK, LW)),
        in_specs=[SM] + [VM] * 5,
        out_specs=[VM] * 5,
        compiler_params=PARAMS,
    )(cond_table, temp_old, soil_class, losses, owner.reshape(1, SEG), column.reshape(1, SEG))
    halo = exchange(xlo, xhi, ylo, yhi)
    recv = lax.all_to_all(send, "gy", 0, 0, tiled=True)
    out = pl.pallas_call(
        start_kernel,
        out_shape=(SLAB, shape(CX + 1, CY, NZ), SLAB, YF, SLAB, SLAB, SLAB, XF, XF, YF, YF),
        in_specs=[SM, SM] + [VM] * 9,
        out_specs=[VM] * 11,
        scratch_shapes=[pltpu.VMEM((CX + 2, CY, NZ), F32), pltpu.VMEM((CX + 2, CY, NZ), F32)],
        compiler_params=PARAMS,
    )(pos, cond_table, temp_old, capacity, soil_class, *near(*halo, recv), injection)
    temp, coefs, faces = out[0], out[1:7], out[7:]
    for sweep in range(1, SWEEPS):
        halo = exchange(*faces)
        last = sweep == SWEEPS - 1
        outs = (jax.ShapeDtypeStruct((CX, CY, NZ), F32),) if last else (SLAB, XF, XF, YF, YF)
        out = pl.pallas_call(
            sweep_kernel,
            out_shape=outs,
            in_specs=[VM] * 11,
            out_specs=[VM] * len(outs),
            compiler_params=PARAMS,
        )(*near(temp, *coefs, *halo))
        temp, faces = out[0], out[1:]
    return temp


def solution(mesh):
    return jax.shard_map(
        shards,
        mesh=mesh,
        in_specs=(
            P("gx", "gy", None),
            P("gx", "gy", None),
            P("gx", "gy", None),
            P(),
            P(("gx", "gy"), None),
            P(("gx", "gy"), None),
            P(("gx", "gy")),
            P(),
        ),
        out_specs=P("gx", "gy", None),
        check_vma=False,
    )
```

```python
import jax
import jax.numpy as jnp
from jax import lax
from jax.experimental import pallas as pl
from jax.experimental.pallas import tpu as pltpu
from jax.sharding import PartitionSpec as P

SWEEPS = 4
NCLS = 8
CX, CY, NZ = 16, 32, 1024
LW = 128
SEG = 256
CAP = 64
NGX, NGY = 32, 8
CHUNK = CAP + 8
YT = 8
NT = CY // YT
PARTS = 4
F32, BF16 = jnp.float32, jnp.bfloat16
HIGH = lax.Precision.HIGHEST
VM = pl.BlockSpec(memory_space=pltpu.VMEM)
SM = pl.BlockSpec(memory_space=pltpu.SMEM)
HB = pl.BlockSpec(memory_space=pltpu.HBM)


def local(*dims, dtype=F32):
    return pltpu.VMEM(dims, dtype)


def near(*arrays):
    return [pltpu.with_memory_space_constraint(a, pltpu.VMEM) for a in arrays]


def far(*arrays):
    return [pltpu.with_memory_space_constraint(a, pltpu.HBM) for a in arrays]


def lookup(klass, table):
    cond = jnp.where(klass == 0, table[0], F32(0.0))
    for k in range(1, NCLS):
        cond = jnp.where(klass == k, table[k], cond)
    return cond


def load(pairs, sems):
    copies = [pltpu.make_async_copy(src, dst, sems.at[i]) for i, (src, dst) in enumerate(pairs)]
    for copy in copies:
        copy.start()
    for copy in copies:
        copy.wait()


def pack_kernel(loss_hbm, owner_hbm, col_hbm, send_ref, loss_ref, owner_ref, col_ref, sems):
    load([(loss_hbm, loss_ref), (owner_hbm, owner_ref), (col_hbm, col_ref)], sems)
    own = owner_ref[...]
    mine = lax.broadcasted_iota(jnp.int32, (NGY, SEG), 0) == own
    before = lax.broadcasted_iota(jnp.int32, (SEG, SEG), 0) < lax.broadcasted_iota(jnp.int32, (SEG, SEG), 1)
    count = jnp.dot(mine.astype(BF16), before.astype(BF16), preferred_element_type=F32)
    rank = jnp.sum(jnp.where(mine, count, 0.0), axis=0, keepdims=True).astype(jnp.int32)
    slot = own * CAP + rank
    cols = jnp.broadcast_to(col_ref[...].astype(F32), (8, SEG))
    loss = loss_ref[...]
    for o in range(NGY):
        pick = (lax.broadcasted_iota(jnp.int32, (CAP, SEG), 0) + o * CAP == slot).astype(F32)
        send_ref[o * CHUNK:o * CHUNK + CAP, :] = jnp.dot(pick, loss, precision=HIGH, preferred_element_type=F32)
        crow = lax.dot_general(cols, pick, (((1,), (1,)), ((), ())), precision=HIGH, preferred_element_type=F32)
        send_ref[o * CHUNK + CAP:(o + 1) * CHUNK, :] = jnp.concatenate([crow, crow], axis=1)


def faces_kernel(after_ref, t_ref, soil_ref, xlo, xhi, ylo, yhi, t_lo, t_hi, s_lo, s_hi, sx_lo, sx_hi, sems):
    load([(t_ref.at[:, 0:YT], t_lo), (t_ref.at[:, CY - YT:CY], t_hi),
          (soil_ref.at[:, 0:YT], s_lo), (soil_ref.at[:, CY - YT:CY], s_hi),
          (t_ref.at[0], xlo.at[0:CY]), (t_ref.at[CX - 1], xhi.at[0:CY]),
          (soil_ref.at[0], sx_lo), (soil_ref.at[CX - 1], sx_hi)], sems)
    for x in range(CX):
        ylo[x:x + 1, :] = t_lo[x, 0:1, :]
        yhi[x:x + 1, :] = t_hi[x, YT - 1:YT, :]
        ylo[CX + x:CX + x + 1, :] = s_lo[x, 0:1, :].astype(F32)
        yhi[CX + x:CX + x + 1, :] = s_hi[x, YT - 1:YT, :].astype(F32)
    xlo[CY:, :] = sx_lo[...].astype(F32)
    xhi[CY:, :] = sx_hi[...].astype(F32)


def tile_sides(ref, x, yt, lo_row, hi_row):
    mid = ref[x, yt * YT:(yt + 1) * YT, :]
    row = lax.broadcasted_iota(jnp.int32, (YT, NZ), 0)
    after = ref[x, (yt + 1) * YT:(yt + 1) * YT + 1, :] if yt < NT - 1 else hi_row
    before = ref[x, yt * YT - 1:yt * YT, :] if yt > 0 else lo_row
    up = jnp.where(row == YT - 1, after, pltpu.roll(mid, YT - 1, 0))
    down = jnp.where(row == 0, before, pltpu.roll(mid, 1, 0))
    return mid, up, down


def add_source(recv_ref, inj, out_ref):
    lane = lax.broadcasted_iota(jnp.int32, (1, 2 * CAP), 1)
    cell = lax.broadcasted_iota(jnp.int32, (CX * CY, 2 * CAP), 0)
    pick, loss = [], []
    for g in range(0, NGY, 2):
        a, b = g * CHUNK, (g + 1) * CHUNK
        crow = jnp.where(lane < CAP, recv_ref[a + CAP:a + CAP + 1, :], recv_ref[b + CAP:b + CAP + 1, :])
        pick.append((cell == crow.astype(jnp.int32)).astype(F32).astype(BF16))
        loss += [recv_ref[a:a + CAP, :], recv_ref[b:b + CAP, :]]
    pick = jnp.concatenate(pick, axis=1)
    loss = jnp.concatenate(loss, axis=0)
    gathered = jnp.zeros((CX * CY, LW), F32)
    for _ in range(3):
        part = loss.astype(BF16)
        loss = loss - part.astype(F32)
        gathered = gathered + jnp.dot(pick, part, preferred_element_type=F32)
    high = gathered.astype(BF16)
    low = (gathered - high.astype(F32)).astype(BF16)
    left = jnp.concatenate([high, low, high], axis=1)
    width = 256
    for n in range(0, NZ, width):
        cut = slice(n, n + width)
        both = inj[:, cut]
        top = both.astype(BF16)
        right = jnp.concatenate([top, top, (both - top.astype(F32)).astype(BF16)], axis=0)
        out_ref[:, :, cut] = jnp.dot(left, right, preferred_element_type=F32).reshape(CX, CY, width)


def prepare_kernel(recv_ref, table_ref, t_hbm, cap_hbm, soil_hbm, inj_hbm,
                   t_ref, fx_ref, fy_ref, fylo_ref, fz_ref, w_ref, rhs_ref, cond, soil, cap, inj, sems):
    copies = []
    step = CX // PARTS
    for part in range(PARTS):
        span = pl.ds(part * step, step)
        for k, (src, dst) in enumerate(((soil_hbm, soil), (t_hbm, t_ref), (cap_hbm, cap))):
            copies.append(pltpu.make_async_copy(src.at[span], dst.at[span], sems.at[3 * part + k]))
    copies.append(pltpu.make_async_copy(inj_hbm, inj, sems.at[3 * PARTS]))
    for copy in copies:
        copy.start()
    table = [table_ref[k] for k in range(NCLS)]

    def fill(x, carry):
        cond[x] = lookup(soil[x], table)
        return carry

    copies[-1].wait()
    add_source(recv_ref, inj, rhs_ref)
    for part in range(PARTS):
        copies[3 * part].wait()
        lax.fori_loop(part * step, (part + 1) * step, fill, 0)
    none = jnp.zeros((1, NZ), F32)
    lane = lax.broadcasted_iota(jnp.int32, (YT, NZ), 1)

    def plane(x, first, last):
        for yt in range(NT):
            rows = slice(yt * YT, (yt + 1) * YT)
            c, cyp, cym = tile_sides(cond, x, yt, none, none)
            fxp = 0.5 * c if last else 0.5 * (c + cond[x + 1, rows, :])
            fxm = 0.5 * c if first else 0.5 * (c + cond[x - 1, rows, :])
            fyp, fym = 0.5 * (c + cyp), 0.5 * (c + cym)
            czp = jnp.where(lane == NZ - 1, F32(0.0), pltpu.roll(c, NZ - 1, 1))
            czm = jnp.where(lane == 0, F32(0.0), pltpu.roll(c, 1, 1))
            fzp, fzm = 0.5 * (c + czp), 0.5 * (c + czm)
            cp = cap[x, rows, :]
            diag = cp + fxp + fxm + fyp + fym + fzp + fzm
            inner = not (first or last or yt == 0 or yt == NT - 1)
            w_ref[x, rows, :] = 0.8 / diag if inner else diag
            rhs_ref[x, rows, :] = rhs_ref[x, rows, :] + cp * t_ref[x, rows, :]
            fx_ref[x + 1, rows, :] = fxp
            if first:
                fx_ref[x, rows, :] = fxm
            fy_ref[x, rows, :] = fyp
            if yt == 0:
                fylo_ref[pl.ds(x, 1), :] = fym[0:1, :]
            fz_ref[x, rows, :] = fzp

    def body(x, carry):
        plane(x, False, False)
        return carry

    for part in range(PARTS):
        copies[3 * part + 1].wait()
        copies[3 * part + 2].wait()
        if part == 0:
            plane(0, True, False)
        lax.fori_loop(max(1, part * step), min(CX - 1, (part + 1) * step), body, 0)
    plane(CX - 1, False, True)


def new_tile(x, yt, first, last, t_ref, fx_ref, fy_ref, fylo_ref, fz_ref, w_ref, rhs_ref, hxlo, hxhi, hylo, hyhi):
    row = lax.broadcasted_iota(jnp.int32, (YT, NZ), 0)
    lane = lax.broadcasted_iota(jnp.int32, (YT, NZ), 1)
    rows = slice(yt * YT, (yt + 1) * YT)
    t, typ, tym = tile_sides(t_ref, x, yt, hylo[pl.ds(x, 1), :] if yt == 0 else None,
                             hyhi[pl.ds(x, 1), :] if yt == NT - 1 else None)
    txm = hxlo[rows, :] if first else t_ref[x - 1, rows, :]
    txp = hxhi[rows, :] if last else t_ref[x + 1, rows, :]
    fy = fy_ref[x, rows, :]
    before = fylo_ref[pl.ds(x, 1), :] if yt == 0 else fy_ref[x, yt * YT - 1:yt * YT, :]
    fym = jnp.where(row == 0, before, pltpu.roll(fy, 1, 0))
    fz = fz_ref[x, rows, :]
    total = rhs_ref[x, rows, :] + fx_ref[x + 1, rows, :] * txp + fx_ref[x, rows, :] * txm
    total = total + fy * typ + fym * tym
    total = total + jnp.where(lane == NZ - 1, F32(0.0), fz * pltpu.roll(t, NZ - 1, 1))
    total = total + jnp.where(lane == 0, F32(0.0), pltpu.roll(fz * t, 1, 1))
    return (1.0 - 0.8) * t + w_ref[x, rows, :] * total


def step_tile(refs, tn_ref, ylo, yhi, x, yt, first=False, last=False):
    tn = new_tile(x, yt, first, last, *refs)
    tn_ref[x, yt * YT:(yt + 1) * YT, :] = tn
    if ylo is not None and yt == 0:
        ylo[pl.ds(x, 1), :] = tn[0:1, :]
    if yhi is not None and yt == NT - 1:
        yhi[pl.ds(x, 1), :] = tn[YT - 1:YT, :]


def planes(refs, tn_ref, tiles, ylo=None, yhi=None, start=1, stop=CX - 1):
    def body(x, carry):
        for yt in tiles:
            step_tile(refs, tn_ref, ylo, yhi, x, yt)
        return carry

    lax.fori_loop(start, stop, body, 0)


def y_fix_kernel(pos_ref, table_ref, hylo, hyhi, t_ref, fx_ref, fz_ref, rhs_ref, fy_in, fylo_in, w_in,
                 fy_ref, fylo_ref, w_ref, tn_ref, ylo, yhi, dy):
    gy = pos_ref[1]
    in_lo = (gy > 0).astype(F32)
    in_hi = (gy < NGY - 1).astype(F32)
    table = [table_ref[k] for k in range(NCLS)]
    dy[0] = 0.5 * lookup(hylo[CX:, :].astype(jnp.int32), table) * in_lo
    dy[1] = 0.5 * lookup(hyhi[CX:, :].astype(jnp.int32), table) * in_hi
    fylo_ref[...] = (fylo_in[...] + dy[0]) * in_lo
    row = lax.broadcasted_iota(jnp.int32, (YT, NZ), 0)
    bot, top = slice(0, YT), slice(CY - YT, CY)

    def fix(x, edge):
        add = dy[1, pl.ds(x, 1), :]
        lo = w_in[x, bot, :] + jnp.where(row == 0, dy[0, pl.ds(x, 1), :], F32(0.0))
        hi = w_in[x, top, :] + jnp.where(row == YT - 1, add, F32(0.0))
        w_ref[x, bot, :] = lo if edge else 0.8 / lo
        w_ref[x, top, :] = hi if edge else 0.8 / hi
        fy = fy_in[x, top, :]
        fy_ref[x, top, :] = jnp.where(row == YT - 1, (fy + add) * in_hi, fy)

    fix(0, True)
    fix(CX - 1, True)
    refs = (t_ref, fx_ref, fy_ref, fylo_ref, fz_ref, w_ref, rhs_ref, None, None, hylo, hyhi)

    def body(x, carry):
        fix(x, False)
        for yt in (0, NT - 1):
            step_tile(refs, tn_ref, ylo, yhi, x, yt)
        return carry

    lax.fori_loop(1, CX - 1, body, 0)


def x_planes(refs, tn_ref, ylo, yhi, xlo, xhi):
    for yt in (0, NT - 1, 1, NT - 2):
        step_tile(refs, tn_ref, ylo, yhi, 0, yt, first=True)
        step_tile(refs, tn_ref, ylo, yhi, CX - 1, yt, last=True)
    xlo[...] = tn_ref[0]
    xhi[...] = tn_ref[CX - 1]


def x_fix_kernel(pos_ref, table_ref, hxlo, hxhi, hylo, hyhi, t_ref, fy_ref, fylo_ref, fz_ref, rhs_ref,
                 fx_in, w_in, tn_in, ylo_in, yhi_in, fx_ref, w_ref, tn_ref, ylo, yhi, xlo, xhi):
    gx = pos_ref[0]
    table = [table_ref[k] for k in range(NCLS)]
    for halo, within, x, at in ((hxlo, gx > 0, 0, 0), (hxhi, gx < NGX - 1, CX - 1, CX)):
        within = within.astype(F32)
        add = 0.5 * lookup(halo[CY:, :].astype(jnp.int32), table) * within
        fx_ref[at] = (fx_in[at] + add) * within
        w_ref[x] = 0.8 / (w_in[x] + add)
    x_planes((t_ref, fx_ref, fy_ref, fylo_ref, fz_ref, w_ref, rhs_ref, hxlo, hxhi, hylo, hyhi), tn_ref, ylo, yhi, xlo, xhi)


def y_edge_kernel(*refs):
    refs, (hylo, hyhi, tn_ref, ylo, yhi) = refs[:7], refs[7:]
    planes(refs + (None, None, hylo, hyhi), tn_ref, (0, NT - 1), ylo, yhi)


def x_edge_kernel(*refs):
    refs, (tn_in, ylo_in, yhi_in, tn_ref, ylo, yhi, xlo, xhi) = refs[:11], refs[11:]
    x_planes(refs, tn_ref, ylo, yhi, xlo, xhi)


def inner_kernel(*refs):
    refs, (tn_in, tn_ref) = refs[:7], refs[7:]
    planes(refs + (None,) * 4, tn_ref, range(1, NT - 1))


def last_inner_kernel(*refs):
    refs, (hylo, hyhi, out_ref, tn_ref, sems) = refs[:7], refs[7:]
    bounds = list(range(1, CX - 1, 2)) + [CX - 1]
    copies = []
    for k, (start, stop) in enumerate(zip(bounds[:-1], bounds[1:])):
        planes(refs + (None, None, hylo, hyhi), tn_ref, range(NT), start=start, stop=stop)
        span = pl.ds(start, stop - start)
        copies.append(pltpu.make_async_copy(tn_ref.at[span], out_ref.at[span], sems.at[k]))
        copies[-1].start()
    for copy in copies:
        copy.wait()


def last_edge_kernel(*refs):
    refs, (out_in, out_ref, lo_ref, hi_ref, sems) = refs[:11], refs[11:]
    for yt in range(NT):
        rows = slice(yt * YT, (yt + 1) * YT)
        lo_ref[rows, :] = new_tile(0, yt, True, False, *refs)
        hi_ref[rows, :] = new_tile(CX - 1, yt, False, True, *refs)
    load([(lo_ref, out_ref.at[0]), (hi_ref, out_ref.at[CX - 1])], sems)


def along_y(ylo, yhi):
    up = [(i, (i + 1) % NGY) for i in range(NGY)]
    return lax.ppermute(yhi, "gy", up), lax.ppermute(ylo, "gy", [(j, i) for i, j in up])


def along_x(xlo, xhi):
    up = [(i, (i + 1) % NGX) for i in range(NGX)]
    return lax.ppermute(xhi, "gx", up), lax.ppermute(xlo, "gx", [(j, i) for i, j in up])


def call(kernel, outs, specs, scratch=(), alias={}, mib=1, us=0.1, out_specs=None):
    return pl.pallas_call(
        kernel,
        out_shape=outs,
        in_specs=specs,
        out_specs=out_specs or [VM] * len(outs),
        scratch_shapes=scratch,
        input_output_aliases=alias,
        compiler_params=pltpu.CompilerParams(vmem_limit_bytes=mib * 1024 * 1024),
        cost_estimate=pl.CostEstimate(flops=0, bytes_accessed=int(us * 3e6), transcendentals=0),
    )


SLAB = local(CX, CY, NZ)
XF, YF = local(CY, NZ), local(CX, NZ)
DMA = pltpu.SemaphoreType.DMA
I32 = jnp.int32


def shards(temp_old, capacity, soil_class, cond_table, losses, owner, column, injection):
    pos = jnp.stack([lax.axis_index("gx"), lax.axis_index("gy")]).astype(I32)
    (send,) = call(pack_kernel, (local(NGY * CHUNK, LW),), [HB, HB, HB],
                   [local(SEG, LW), local(1, SEG, dtype=I32), local(1, SEG, dtype=I32), DMA((3,))], mib=4)(
        *far(losses, owner.reshape(1, SEG), column.reshape(1, SEG)))
    recv = lax.all_to_all(send, "gy", 0, 0, tiled=True)
    rows, rows_int, face_int = local(CX, YT, NZ), local(CX, YT, NZ, dtype=I32), local(CY, NZ, dtype=I32)
    two_x, two_y = local(2 * CY, NZ), local(2 * CX, NZ)
    xlo, xhi, ylo, yhi = call(faces_kernel, (two_x, two_x, two_y, two_y), [VM, HB, HB],
                              [rows, rows, rows_int, rows_int, face_int, face_int, DMA((8,))], mib=4)(
        *near(send), *far(temp_old, soil_class))
    hylo, hyhi = along_y(ylo, yhi)
    hxlo, hxhi = along_x(xlo, xhi)
    temp, fx, fy, fylo, fz, w, rhs = call(
        prepare_kernel, (SLAB, local(CX + 1, CY, NZ), SLAB, YF, SLAB, SLAB, SLAB),
        [VM, SM] + [HB] * 4,
        [SLAB, local(CX, CY, NZ, dtype=I32), SLAB, local(LW, NZ), DMA((3 * PARTS + 1,))], mib=12, us=PREP)(
        *near(recv), cond_table, *far(temp_old, capacity, soil_class, injection))
    fy, fylo, w, new, ylo, yhi = call(
        y_fix_kernel, (SLAB, YF, SLAB, SLAB, YF, YF), [SM, SM] + [VM] * 9, [local(2, CX, NZ)], alias={8: 0, 9: 1, 10: 2}, us=Z1)(
        pos, cond_table, *near(hylo, hyhi, temp, fx, fz, rhs, fy, fylo, w))
    fx, w, new, ylo, yhi, xlo, xhi = call(
        x_fix_kernel, (local(CX + 1, CY, NZ), SLAB, SLAB, YF, YF, XF, XF), [SM, SM] + [VM] * 14,
        alias={11: 0, 12: 1, 13: 2, 14: 3, 15: 4}, us=CXC)(
        pos, cond_table, *near(hxlo, hxhi, hylo, hyhi, temp, fy, fylo, fz, rhs, fx, w, new, ylo, yhi))
    for sweep in range(1, SWEEPS):
        hylo, hyhi = along_y(ylo, yhi)
        hxlo, hxhi = along_x(xlo, xhi)
        (temp,) = call(inner_kernel, (SLAB,), [VM] * 8, alias={7: 0}, us=INN)(*near(temp, fx, fy, fylo, fz, w, rhs, new))
        args = near(temp, fx, fy, fylo, fz, w, rhs)
        hy, hx = near(hylo, hyhi), near(hxlo, hxhi)
        if sweep < SWEEPS - 1:
            new, ylo, yhi = call(y_edge_kernel, (SLAB, YF, YF), [VM] * 9, us=Z)(*args, *hy)
            new, ylo, yhi, xlo, xhi = call(x_edge_kernel, (SLAB, YF, YF, XF, XF), [VM] * 14, alias={11: 0, 12: 1, 13: 2}, us=CXC)(
                *args, *hx, *hy, *near(new, ylo, yhi))
    (out,) = call(last_inner_kernel, (pltpu.HBM((CX, CY, NZ), F32),), [VM] * 9, [SLAB, DMA((CX,))], mib=4, us=Z, out_specs=[HB])(*args, *hy)
    return call(last_edge_kernel, (pltpu.HBM((CX, CY, NZ), F32),), [VM] * 11 + [HB], [XF, XF, DMA((2,))], alias={11: 0},
                out_specs=[HB], us=CXC)(*args, *hx, *hy, out)[0]


PREP, Z1, Z, CXC, INN = 5.0, 8.0, 8.0, 1.0, 0.1


def solution(mesh):
    return jax.shard_map(
        shards,
        mesh=mesh,
        in_specs=(
            P("gx", "gy", None),
            P("gx", "gy", None),
            P("gx", "gy", None),
            P(),
            P(("gx", "gy"), None),
            P(("gx", "gy"), None),
            P(("gx", "gy")),
            P(),
        ),
        out_specs=P("gx", "gy", None),
        check_vma=False,
    )
```

```python
import jax
import jax.numpy as jnp
from jax import lax
from jax.experimental import pallas as pl
from jax.experimental.pallas import tpu as pltpu
from jax.sharding import PartitionSpec as P

SWEEPS = 4
NCLS = 8
CX, CY, NZ = 16, 32, 1024
LW = 128
SEG = 256
CAP = 64
NGX, NGY = 32, 8
CHUNK = CAP + 8
YT = 8
NT = CY // YT
PARTS = 4
F32, BF16 = jnp.float32, jnp.bfloat16
HIGH = lax.Precision.HIGHEST
VM = pl.BlockSpec(memory_space=pltpu.VMEM)
SM = pl.BlockSpec(memory_space=pltpu.SMEM)
HB = pl.BlockSpec(memory_space=pltpu.HBM)


def local(*dims, dtype=F32):
    return pltpu.VMEM(dims, dtype)


def near(*arrays):
    return [pltpu.with_memory_space_constraint(a, pltpu.VMEM) for a in arrays]


def far(*arrays):
    return [pltpu.with_memory_space_constraint(a, pltpu.HBM) for a in arrays]


def lookup(klass, table):
    cond = jnp.where(klass == 0, table[0], F32(0.0))
    for k in range(1, NCLS):
        cond = jnp.where(klass == k, table[k], cond)
    return cond


def load(pairs, sems):
    copies = [pltpu.make_async_copy(src, dst, sems.at[i]) for i, (src, dst) in enumerate(pairs)]
    for copy in copies:
        copy.start()
    for copy in copies:
        copy.wait()


def even(axis):
    return lax.rem(lax.axis_index(axis), 2) == 0


def split(a, b, is_even):
    return jnp.where(is_even, b, a), jnp.where(is_even, a, b)


def start_kernel(t_hbm, soil_hbm, loss_hbm, owner_hbm, col_hbm, send_ref, xa, xb, ya, yb,
                 t_lo, t_hi, s_lo, s_hi, tx, sx, loss_ref, owner_ref, col_ref, sems):
    pairs = [(loss_hbm, loss_ref), (owner_hbm, owner_ref), (col_hbm, col_ref),
             (t_hbm.at[:, 0:YT], t_lo), (t_hbm.at[:, CY - YT:CY], t_hi),
             (soil_hbm.at[:, 0:YT], s_lo), (soil_hbm.at[:, CY - YT:CY], s_hi),
             (t_hbm.at[0], tx.at[0]), (t_hbm.at[CX - 1], tx.at[1]),
             (soil_hbm.at[0], sx.at[0]), (soil_hbm.at[CX - 1], sx.at[1])]
    copies = [pltpu.make_async_copy(src, dst, sems.at[i]) for i, (src, dst) in enumerate(pairs)]
    for copy in copies:
        copy.start()
    for copy in copies[:3]:
        copy.wait()
    own = owner_ref[...]
    mine = lax.broadcasted_iota(jnp.int32, (NGY, SEG), 0) == own
    before = lax.broadcasted_iota(jnp.int32, (SEG, SEG), 0) < lax.broadcasted_iota(jnp.int32, (SEG, SEG), 1)
    count = jnp.dot(mine.astype(F32).astype(BF16), before.astype(F32).astype(BF16), preferred_element_type=F32)
    rank = jnp.sum(jnp.where(mine, count, 0.0), axis=0, keepdims=True).astype(jnp.int32)
    slot = own * CAP + rank
    pick = (lax.broadcasted_iota(jnp.int32, (NGY * CAP, SEG), 0) == slot).astype(F32).astype(BF16)
    loss = loss_ref[...]
    sent = jnp.zeros((NGY * CAP, LW), F32)
    for _ in range(3):
        part = loss.astype(BF16)
        loss = loss - part.astype(F32)
        sent = sent + jnp.dot(pick, part, preferred_element_type=F32)
    col = jnp.broadcast_to(col_ref[...], (8, SEG))
    low = lax.rem(col, 128)
    by_lane = (((1,), (1,)), ((), ()))
    cols = lax.dot_general(low.astype(F32).astype(BF16), pick, by_lane, preferred_element_type=F32)
    cols = cols + lax.dot_general((col - low).astype(F32).astype(BF16), pick, by_lane, preferred_element_type=F32)
    for o in range(NGY):
        send_ref[o * CHUNK:o * CHUNK + CAP, :] = sent[o * CAP:(o + 1) * CAP, :]
        crow = cols[:, o * CAP:(o + 1) * CAP]
        send_ref[o * CHUNK + CAP:(o + 1) * CHUNK, :] = jnp.concatenate([crow, crow], axis=1)
    for copy in copies[3:]:
        copy.wait()
    even_x, even_y = even("gx"), even("gy")
    for x in range(CX):
        ya[x:x + 1, :], yb[x:x + 1, :] = split(t_lo[x, 0:1, :], t_hi[x, YT - 1:YT, :], even_y)
        s_a, s_b = split(s_lo[x, 0:1, :], s_hi[x, YT - 1:YT, :], even_y)
        ya[CX + x:CX + x + 1, :] = s_a.astype(F32)
        yb[CX + x:CX + x + 1, :] = s_b.astype(F32)
    xa[0:CY, :], xb[0:CY, :] = split(tx[0], tx[1], even_x)
    s_a, s_b = split(sx[0], sx[1], even_x)
    xa[CY:, :] = s_a.astype(F32)
    xb[CY:, :] = s_b.astype(F32)


def add_source(recv_ref, inj, out_ref):
    lane = lax.broadcasted_iota(jnp.int32, (1, 2 * CAP), 1)
    cell = lax.broadcasted_iota(jnp.int32, (CX * CY, 2 * CAP), 0)
    pick, loss = [], []
    for g in range(0, NGY, 2):
        a, b = g * CHUNK, (g + 1) * CHUNK
        crow = jnp.where(lane < CAP, recv_ref[a + CAP:a + CAP + 1, :], recv_ref[b + CAP:b + CAP + 1, :])
        pick.append((cell == crow.astype(jnp.int32)).astype(F32).astype(BF16))
        loss += [recv_ref[a:a + CAP, :], recv_ref[b:b + CAP, :]]
    pick = jnp.concatenate(pick, axis=1)
    loss = jnp.concatenate(loss, axis=0)
    gathered = jnp.zeros((CX * CY, LW), F32)
    for _ in range(3):
        part = loss.astype(BF16)
        loss = loss - part.astype(F32)
        gathered = gathered + jnp.dot(pick, part, preferred_element_type=F32)
    high = gathered.astype(BF16)
    low = (gathered - high.astype(F32)).astype(BF16)
    left = jnp.concatenate([high, low, high], axis=1)
    width = 256
    for n in range(0, NZ, width):
        cut = slice(n, n + width)
        both = inj[:, cut]
        top = both.astype(BF16)
        right = jnp.concatenate([top, top, (both - top.astype(F32)).astype(BF16)], axis=0)
        out_ref[:, :, cut] = jnp.dot(left, right, preferred_element_type=F32).reshape(CX, CY, width)


def tile_sides(ref, x, yt):
    mid = ref[x, yt * YT:(yt + 1) * YT, :]
    row = lax.broadcasted_iota(jnp.int32, (YT, NZ), 0)
    up, down = pltpu.roll(mid, YT - 1, 0), pltpu.roll(mid, 1, 0)
    if yt < NT - 1:
        up = jnp.where(row == YT - 1, ref[x, (yt + 1) * YT:(yt + 1) * YT + 1, :], up)
    if yt > 0:
        down = jnp.where(row == 0, ref[x, yt * YT - 1:yt * YT, :], down)
    return mid, up, down


def prepare_kernel(recv_ref, table_ref, t_hbm, cap_hbm, soil_hbm, inj_hbm,
                   fx_ref, fy_ref, fz_ref, w_ref, rhs_ref, tn_ref, cx_ref, ey_ref, t_ref, cond, soil, cap, inj, sems):
    copies = []
    step = CX // PARTS
    for part in range(PARTS):
        span = pl.ds(part * step, step)
        for k, (src, dst) in enumerate(((soil_hbm, soil), (t_hbm, t_ref), (cap_hbm, cap))):
            copies.append(pltpu.make_async_copy(src.at[span], dst.at[span], sems.at[3 * part + k]))
    copies.append(pltpu.make_async_copy(inj_hbm, inj, sems.at[3 * PARTS]))
    for copy in copies:
        copy.start()
    table = [table_ref[k] for k in range(NCLS)]

    def fill(x, carry):
        cond[x] = lookup(soil[x], table)
        return carry

    copies[-1].wait()
    add_source(recv_ref, inj, rhs_ref)
    for part in range(PARTS):
        copies[3 * part].wait()
        lax.fori_loop(part * step, (part + 1) * step, fill, 0)
    for part in range(PARTS):
        copies[3 * part + 1].wait()
        copies[3 * part + 2].wait()
    cx_ref[0] = cond[0]
    cx_ref[1] = cond[CX - 1]
    row = lax.broadcasted_iota(jnp.int32, (YT, NZ), 0)
    lane = lax.broadcasted_iota(jnp.int32, (YT, NZ), 1)

    def plane(x, first, last):
        for yt in range(NT):
            rows = slice(yt * YT, (yt + 1) * YT)
            low, high = yt == 0, yt == NT - 1
            c, cyp, cym = tile_sides(cond, x, yt)
            half = 0.5 * c
            fxp = half if last else 0.5 * (c + cond[x + 1, rows, :])
            fxm = half if first else 0.5 * (c + cond[x - 1, rows, :])
            fyp, fym = 0.5 * (c + cyp), 0.5 * (c + cym)
            if high:
                fyp = jnp.where(row == YT - 1, half, fyp)
            if low:
                fym = jnp.where(row == 0, half, fym)
            fzp = jnp.where(lane == NZ - 1, half, 0.5 * (c + pltpu.roll(c, NZ - 1, 1)))
            fzm = jnp.where(lane == 0, half, 0.5 * (c + pltpu.roll(c, 1, 1)))
            cp = cap[x, rows, :]
            diag = cp + fxp + fxm + fyp + fym + fzp + fzm
            t, typ, tym = tile_sides(t_ref, x, yt)
            rhs = rhs_ref[x, rows, :] + cp * t
            rhs_ref[x, rows, :] = rhs
            total = rhs
            if not last:
                total = total + fxp * t_ref[x + 1, rows, :]
                fx_ref[x, rows, :] = fxp
            if not first:
                total = total + fxm * t_ref[x - 1, rows, :]
            if high:
                fyp = jnp.where(row == YT - 1, F32(0.0), fyp)
            if low:
                fym = jnp.where(row == 0, F32(0.0), fym)
            fzp = jnp.where(lane == NZ - 1, F32(0.0), fzp)
            fzm = jnp.where(lane == 0, F32(0.0), fzm)
            fy_ref[x, rows, :] = fyp
            fz_ref[x, rows, :] = fzp
            total = total + fyp * typ + fym * tym
            total = total + fzp * pltpu.roll(t, NZ - 1, 1) + fzm * pltpu.roll(t, 1, 1)
            if first or last:
                w_ref[x, rows, :] = diag
                tn_ref[x, rows, :] = total
            else:
                w = 0.8 / diag
                w_ref[x, rows, :] = w
                tn_ref[x, rows, :] = (1.0 - 0.8) * t + w * total
            if low or high:
                at = slice(0, 1) if low else slice(YT - 1, YT)
                side = 0 if low else 1
                for k, value in enumerate((total, diag, c, t)):
                    ey_ref[side, k, pl.ds(x, 1), :] = value[at, :]

    def inner(x, carry):
        plane(x, False, False)
        return carry

    plane(0, True, False)
    lax.fori_loop(1, CX - 1, inner, 0)
    plane(CX - 1, False, True)


def at_row(shape, index, value):
    return jnp.where(lax.broadcasted_iota(jnp.int32, shape, 0) == index, value, F32(0.0))


def with_corners(xlo, xhi, ylo, yhi):
    xs, ys = xlo.shape, ylo.shape
    return (xlo + at_row(xs, 0, ylo[0:1]) + at_row(xs, CY - 1, yhi[0:1]),
            xhi + at_row(xs, 0, ylo[CX - 1:CX]) + at_row(xs, CY - 1, yhi[CX - 1:CX]),
            ylo + at_row(ys, 0, xlo[0:1]) + at_row(ys, CX - 1, xhi[0:1]),
            yhi + at_row(ys, 0, xlo[CY - 1:CY]) + at_row(ys, CX - 1, xhi[CY - 1:CY]))


def fix_kernel(table_ref, hxa, hxb, hya, hyb, t_hbm, w_ref, tn_ref, cx_ref, ey_ref,
               xa, xb, ya, yb, wx_ref, wy_ref, ax_ref, ay_ref, t_edge, sems):
    copies = [pltpu.make_async_copy(t_hbm.at[x], t_edge.at[k], sems.at[k]) for k, x in enumerate((0, CX - 1))]
    for copy in copies:
        copy.start()
    table = [table_ref[k] for k in range(NCLS)]
    gx, gy = lax.axis_index("gx"), lax.axis_index("gy")
    within = [jnp.where(q, F32(1.0), F32(0.0)) for q in (gx > 0, gx < NGX - 1, gy > 0, gy < NGY - 1)]
    t_halo = split(hxa[0:CY, :], hxb[0:CY, :], even("gx")) + split(hya[0:CX, :], hyb[0:CX, :], even("gy"))
    klass = split(hxa[CY:, :], hxb[CY:, :], even("gx")) + split(hya[CX:, :], hyb[CX:, :], even("gy"))
    conds = (cx_ref[0], cx_ref[1], ey_ref[0, 2], ey_ref[1, 2])
    more = [0.5 * lookup(k.astype(jnp.int32), table) * q for k, q in zip(klass, within)]
    face = [(0.5 * c + m) * q for c, m, q in zip(conds, more, within)]
    diag = with_corners(*more)
    total = with_corners(*[f * t for f, t in zip(face, t_halo)])
    for copy in copies:
        copy.wait()
    total = [a + b for a, b in zip(total, (tn_ref[0], tn_ref[CX - 1], ey_ref[0, 0], ey_ref[1, 0]))]
    w = [0.8 / (a + b) for a, b in zip(diag, (w_ref[0], w_ref[CX - 1], ey_ref[0, 1], ey_ref[1, 1]))]
    old = (t_edge[0], t_edge[1], ey_ref[0, 3], ey_ref[1, 3])
    new = [(1.0 - 0.8) * t + a * b for t, a, b in zip(old, w, total)]
    xa[...], xb[...] = split(new[0], new[1], even("gx"))
    ya[...], yb[...] = split(new[2], new[3], even("gy"))
    for k in range(2):
        wx_ref[k], wy_ref[k] = w[k], w[2 + k]
        ax_ref[k], ay_ref[k] = w[k] * face[k], w[2 + k] * face[2 + k]


def faces_of(tn_ref, py_ref, ax_ref, ay_ref, hxa, hxb, hya, hyb):
    halo = split(hxa[...], hxb[...], even("gx")) + split(hya[...], hyb[...], even("gy"))
    terms = with_corners(ax_ref[0] * halo[0], ax_ref[1] * halo[1], ay_ref[0] * halo[2], ay_ref[1] * halo[3])
    return [a + b for a, b in zip(terms, (tn_ref[0], tn_ref[CX - 1], py_ref[0], py_ref[1]))]


def edge_kernel(tn_ref, py_ref, ax_ref, ay_ref, hxa, hxb, hya, hyb, xa, xb, ya, yb):
    new = faces_of(tn_ref, py_ref, ax_ref, ay_ref, hxa, hxb, hya, hyb)
    xa[...], xb[...] = split(new[0], new[1], even("gx"))
    ya[...], yb[...] = split(new[2], new[3], even("gy"))


def put_edges(ref, xlo, xhi, ylo, yhi):
    ref[0] = xlo
    ref[CX - 1] = xhi
    for x in range(1, CX - 1):
        ref[x, 0:1, :] = ylo[x:x + 1]
        ref[x, CY - 1:CY, :] = yhi[x:x + 1]


def sweep_plane(x, first, last, t_ref, fx_ref, fy_ref, fz_ref, w_ref, rhs_ref, tn_ref, py_ref):
    row = lax.broadcasted_iota(jnp.int32, (YT, NZ), 0)
    lane = lax.broadcasted_iota(jnp.int32, (YT, NZ), 1)
    for yt in range(NT):
        rows = slice(yt * YT, (yt + 1) * YT)
        t, typ, tym = tile_sides(t_ref, x, yt)
        fy, _, fym = tile_sides(fy_ref, x, yt)
        if yt == 0:
            fym = jnp.where(row == 0, F32(0.0), fym)
        fz = fz_ref[x, rows, :]
        total = rhs_ref[x, rows, :] + fy * typ + fym * tym
        if not last:
            total = total + fx_ref[x, rows, :] * t_ref[x + 1, rows, :]
        if not first:
            total = total + fx_ref[x - 1, rows, :] * t_ref[x - 1, rows, :]
        total = total + fz * pltpu.roll(t, NZ - 1, 1)
        total = total + jnp.where(lane == 0, F32(0.0), pltpu.roll(fz * t, 1, 1))
        tn = (1.0 - 0.8) * t + w_ref[x, rows, :] * total
        tn_ref[x, rows, :] = tn
        if yt == 0:
            py_ref[0, pl.ds(x, 1), :] = tn[0:1, :]
        if yt == NT - 1:
            py_ref[1, pl.ds(x, 1), :] = tn[YT - 1:YT, :]


def sweep_inside(refs, start=1, stop=CX - 1):
    def inner(x, carry):
        sweep_plane(x, False, False, *refs)
        return carry

    lax.fori_loop(start, stop, inner, 0)


def first_sweep_kernel(fx_ref, fy_ref, fz_ref, rhs_ref, xa, xb, ya, yb, wx_ref, wy_ref, w_in, t_in,
                       w_ref, t_ref, tn_ref, py_ref):
    put_edges(w_ref, wx_ref[0], wx_ref[1], wy_ref[0], wy_ref[1])
    sweep(fx_ref, fy_ref, fz_ref, rhs_ref, w_ref, xa, xb, ya, yb, t_ref, tn_ref, py_ref)


def sweep(fx_ref, fy_ref, fz_ref, rhs_ref, w_ref, xa, xb, ya, yb, t_ref, tn_ref, py_ref):
    put_edges(t_ref, *split(xa[...], xb[...], even("gx")), *split(ya[...], yb[...], even("gy")))
    refs = (t_ref, fx_ref, fy_ref, fz_ref, w_ref, rhs_ref, tn_ref, py_ref)
    sweep_plane(0, True, False, *refs)
    sweep_inside(refs)
    sweep_plane(CX - 1, False, True, *refs)


def sweep_kernel(fx_ref, fy_ref, fz_ref, rhs_ref, w_ref, xa, xb, ya, yb, t_in, t_ref, tn_ref, py_ref):
    sweep(fx_ref, fy_ref, fz_ref, rhs_ref, w_ref, xa, xb, ya, yb, t_ref, tn_ref, py_ref)


def last_sweep_kernel(fx_ref, fy_ref, fz_ref, rhs_ref, w_ref, xa, xb, ya, yb, t_in, t_ref, tn_ref, py_ref, out_ref, sems):
    put_edges(t_ref, *split(xa[...], xb[...], even("gx")), *split(ya[...], yb[...], even("gy")))
    refs = (t_ref, fx_ref, fy_ref, fz_ref, w_ref, rhs_ref, tn_ref, py_ref)
    bounds = list(range(1, CX - 1, 4)) + [CX - 1]
    copies = []
    for k, (start, stop) in enumerate(zip(bounds[:-1], bounds[1:])):
        sweep_inside(refs, start, stop)
        part = (pl.ds(start, stop - start), pl.ds(YT, CY - 2 * YT))
        copies.append(pltpu.make_async_copy(tn_ref.at[part], out_ref.at[part], sems.at[k]))
        copies[-1].start()
    sweep_plane(0, True, False, *refs)
    sweep_plane(CX - 1, False, True, *refs)
    for copy in copies:
        copy.wait()


def finish_kernel(tn_ref, py_ref, ax_ref, ay_ref, hxa, hxb, hya, hyb, out_in, out_ref, x_out, lo_out, hi_out, sems):
    xlo, xhi, ylo, yhi = faces_of(tn_ref, py_ref, ax_ref, ay_ref, hxa, hxb, hya, hyb)
    x_out[0] = xlo
    x_out[1] = xhi
    row = lax.broadcasted_iota(jnp.int32, (YT, NZ), 0)
    for x in range(1, CX - 1):
        lo_out[x - 1] = jnp.where(row == 0, ylo[x:x + 1], tn_ref[x, 0:YT, :])
        hi_out[x - 1] = jnp.where(row == YT - 1, yhi[x:x + 1], tn_ref[x, CY - YT:CY, :])
    inside = pl.ds(1, CX - 2)
    load([(x_out.at[0], out_ref.at[0]), (x_out.at[1], out_ref.at[CX - 1]),
          (lo_out, out_ref.at[inside, 0:YT]), (hi_out, out_ref.at[inside, CY - YT:CY])], sems)


def swaps(axis, count, a, b):
    one = [(i, i + 1) for i in range(0, count, 2)]
    two = [(i, (i + 1) % count) for i in range(1, count, 2)]
    return [lax.ppermute(v, axis, p + [(j, i) for i, j in p]) for v, p in ((a, one), (b, two))]


def exchange(xa, xb, ya, yb):
    return near(*swaps("gx", NGX, xa, xb), *swaps("gy", NGY, ya, yb))


def call(kernel, outs, specs, scratch=(), alias={}, mib=1, us=0.1, out_specs=None):
    return pl.pallas_call(
        kernel,
        out_shape=outs,
        in_specs=specs,
        out_specs=out_specs or [VM] * len(outs),
        scratch_shapes=scratch,
        input_output_aliases=alias,
        compiler_params=pltpu.CompilerParams(vmem_limit_bytes=mib * 1024 * 1024),
        cost_estimate=pl.CostEstimate(flops=0, bytes_accessed=int(us * 3e6), transcendentals=0),
    )


SLAB = local(CX, CY, NZ)
FACES = (local(CY, NZ), local(CY, NZ), local(CX, NZ), local(CX, NZ))
XX, YY = local(2, CY, NZ), local(2, CX, NZ)
DMA = pltpu.SemaphoreType.DMA
I32 = jnp.int32


def shards(temp_old, capacity, soil_class, cond_table, losses, owner, column, injection):
    rows, rows_int = local(CX, YT, NZ), local(CX, YT, NZ, dtype=I32)
    send, *faces = call(
        start_kernel, (local(NGY * CHUNK, LW),) + (local(2 * CY, NZ),) * 2 + (local(2 * CX, NZ),) * 2, [HB] * 5,
        [rows, rows, rows_int, rows_int, XX, local(2, CY, NZ, dtype=I32), local(SEG, LW), local(1, SEG, dtype=I32),
         local(1, SEG, dtype=I32), DMA((11,))], mib=6)(
        *far(temp_old, soil_class, losses, owner.reshape(1, SEG), column.reshape(1, SEG)))
    recv = lax.all_to_all(send, "gy", 0, 0, tiled=True)
    halo = exchange(*faces)
    fx, fy, fz, w, rhs, new, cx, ey = call(
        prepare_kernel, (SLAB,) * 6 + (XX, local(2, 4, CX, NZ)), [VM, SM] + [HB] * 4,
        [SLAB, SLAB, local(CX, CY, NZ, dtype=I32), SLAB, local(LW, NZ), DMA((3 * PARTS + 1,))], mib=16, us=5.0)(
        *near(recv), cond_table, *far(temp_old, capacity, soil_class, injection))
    *faces, wx, wy, ax, ay = call(
        fix_kernel, FACES + (XX, YY, XX, YY), [SM] + [VM] * 4 + [HB] + [VM] * 4, [XX, DMA((2,))], mib=4)(
        cond_table, *halo, *far(temp_old), *near(w, new, cx, ey))
    for number in range(1, SWEEPS):
        halo = exchange(*faces)
        coefs = near(fx, fy, fz, rhs)
        if number == 1:
            w, temp, new, py = call(
                first_sweep_kernel, (SLAB, SLAB, SLAB, YY), [VM] * 12, alias={10: 0, 11: 1}, mib=2)(
                *coefs, *near(*faces, wx, wy, w, new))
        elif number < SWEEPS - 1:
            temp, new, py = call(sweep_kernel, (SLAB, SLAB, YY), [VM] * 10, alias={9: 0}, mib=2)(
                *coefs, *near(w, *faces, new))
        else:
            temp, new, py, out = call(
                last_sweep_kernel, (SLAB, SLAB, YY, pltpu.HBM((CX, CY, NZ), F32)), [VM] * 10, [DMA((4,))],
                alias={9: 0}, mib=2, out_specs=[VM] * 3 + [HB])(*coefs, *near(w, *faces, new))
        args = near(new, py, ax, ay) + halo
        if number < SWEEPS - 1:
            faces = call(edge_kernel, FACES, [VM] * 8, mib=2)(*args)
    return call(finish_kernel, (pltpu.HBM((CX, CY, NZ), F32),), [VM] * 8 + [HB],
                [XX, local(CX - 2, YT, NZ), local(CX - 2, YT, NZ), DMA((4,))], alias={8: 0}, mib=4, out_specs=[HB])(*args, out)[0]


def solution(mesh):
    return jax.shard_map(
        shards,
        mesh=mesh,
        in_specs=(
            P("gx", "gy", None),
            P("gx", "gy", None),
            P("gx", "gy", None),
            P(),
            P(("gx", "gy"), None),
            P(("gx", "gy"), None),
            P(("gx", "gy")),
            P(),
        ),
        out_specs=P("gx", "gy", None),
        check_vma=False,
    )
```

```python
import jax
import jax.numpy as jnp
from jax import lax
from jax.experimental import pallas as pl
from jax.experimental.pallas import tpu as pltpu
from jax.sharding import PartitionSpec as P

SWEEPS = 4
NCLS = 8
CX, CY, NZ = 16, 32, 1024
LW = 128
SEG = 256
CAP = 64
NGX, NGY = 32, 8
CHUNK = CAP + 8
YT = 8
NT = CY // YT
PARTS = 4
F32, BF16 = jnp.float32, jnp.bfloat16
HIGH = lax.Precision.HIGHEST
VM = pl.BlockSpec(memory_space=pltpu.VMEM)
SM = pl.BlockSpec(memory_space=pltpu.SMEM)
HB = pl.BlockSpec(memory_space=pltpu.HBM)


def local(*dims, dtype=F32):
    return pltpu.VMEM(dims, dtype)


def near(*arrays):
    return [pltpu.with_memory_space_constraint(a, pltpu.VMEM) for a in arrays]


def far(*arrays):
    return [pltpu.with_memory_space_constraint(a, pltpu.HBM) for a in arrays]


def lookup(klass, table):
    cond = jnp.where(klass == 0, table[0], F32(0.0))
    for k in range(1, NCLS):
        cond = jnp.where(klass == k, table[k], cond)
    return cond


def load(pairs, sems):
    copies = [pltpu.make_async_copy(src, dst, sems.at[i]) for i, (src, dst) in enumerate(pairs)]
    for copy in copies:
        copy.start()
    for copy in copies:
        copy.wait()


def even(axis):
    return lax.rem(lax.axis_index(axis), 2) == 0


def split(a, b, is_even):
    return jnp.where(is_even, b, a), jnp.where(is_even, a, b)


def start_kernel(t_hbm, soil_hbm, loss_hbm, owner_hbm, col_hbm, send_ref, xa, xb, ya, yb,
                 t_lo, t_hi, s_lo, s_hi, tx, sx, loss_ref, owner_ref, col_ref, sems):
    pairs = [(loss_hbm, loss_ref), (owner_hbm, owner_ref), (col_hbm, col_ref),
             (t_hbm.at[:, 0:YT], t_lo), (t_hbm.at[:, CY - YT:CY], t_hi),
             (soil_hbm.at[:, 0:YT], s_lo), (soil_hbm.at[:, CY - YT:CY], s_hi),
             (t_hbm.at[0], tx.at[0]), (t_hbm.at[CX - 1], tx.at[1]),
             (soil_hbm.at[0], sx.at[0]), (soil_hbm.at[CX - 1], sx.at[1])]
    copies = [pltpu.make_async_copy(src, dst, sems.at[i]) for i, (src, dst) in enumerate(pairs)]
    for copy in copies:
        copy.start()
    for copy in copies[:3]:
        copy.wait()
    own = owner_ref[...]
    mine = lax.broadcasted_iota(jnp.int32, (NGY, SEG), 0) == own
    before = lax.broadcasted_iota(jnp.int32, (SEG, SEG), 0) < lax.broadcasted_iota(jnp.int32, (SEG, SEG), 1)
    count = jnp.dot(mine.astype(F32).astype(BF16), before.astype(F32).astype(BF16), preferred_element_type=F32)
    rank = jnp.sum(jnp.where(mine, count, 0.0), axis=0, keepdims=True).astype(jnp.int32)
    slot = own * CAP + rank
    pick = (lax.broadcasted_iota(jnp.int32, (NGY * CAP, SEG), 0) == slot).astype(F32).astype(BF16)
    loss = loss_ref[...]
    sent = jnp.zeros((NGY * CAP, LW), F32)
    for _ in range(3):
        part = loss.astype(BF16)
        loss = loss - part.astype(F32)
        sent = sent + jnp.dot(pick, part, preferred_element_type=F32)
    col = jnp.broadcast_to(col_ref[...], (8, SEG))
    low = lax.rem(col, 128)
    by_lane = (((1,), (1,)), ((), ()))
    cols = lax.dot_general(low.astype(F32).astype(BF16), pick, by_lane, preferred_element_type=F32)
    cols = cols + lax.dot_general((col - low).astype(F32).astype(BF16), pick, by_lane, preferred_element_type=F32)
    for o in range(NGY):
        send_ref[o * CHUNK:o * CHUNK + CAP, :] = sent[o * CAP:(o + 1) * CAP, :]
        crow = cols[:, o * CAP:(o + 1) * CAP]
        send_ref[o * CHUNK + CAP:(o + 1) * CHUNK, :] = jnp.concatenate([crow, crow], axis=1)
    for copy in copies[3:]:
        copy.wait()
    even_x, even_y = even("gx"), even("gy")
    for x in range(CX):
        ya[x:x + 1, :], yb[x:x + 1, :] = split(t_lo[x, 0:1, :], t_hi[x, YT - 1:YT, :], even_y)
        s_a, s_b = split(s_lo[x, 0:1, :], s_hi[x, YT - 1:YT, :], even_y)
        ya[CX + x:CX + x + 1, :] = s_a.astype(F32)
        yb[CX + x:CX + x + 1, :] = s_b.astype(F32)
    xa[0:CY, :], xb[0:CY, :] = split(tx[0], tx[1], even_x)
    s_a, s_b = split(sx[0], sx[1], even_x)
    xa[CY:, :] = s_a.astype(F32)
    xb[CY:, :] = s_b.astype(F32)


def add_source(recv_ref, inj, out_ref):
    lane = lax.broadcasted_iota(jnp.int32, (1, 2 * CAP), 1)
    cell = lax.broadcasted_iota(jnp.int32, (CX * CY, 2 * CAP), 0)
    pick, loss = [], []
    for g in range(0, NGY, 2):
        a, b = g * CHUNK, (g + 1) * CHUNK
        crow = jnp.where(lane < CAP, recv_ref[a + CAP:a + CAP + 1, :], recv_ref[b + CAP:b + CAP + 1, :])
        pick.append((cell == crow.astype(jnp.int32)).astype(F32).astype(BF16))
        loss += [recv_ref[a:a + CAP, :], recv_ref[b:b + CAP, :]]
    pick = jnp.concatenate(pick, axis=1)
    loss = jnp.concatenate(loss, axis=0)
    gathered = jnp.zeros((CX * CY, LW), F32)
    for _ in range(3):
        part = loss.astype(BF16)
        loss = loss - part.astype(F32)
        gathered = gathered + jnp.dot(pick, part, preferred_element_type=F32)
    high = gathered.astype(BF16)
    low = (gathered - high.astype(F32)).astype(BF16)
    left = jnp.concatenate([high, low, high], axis=1)
    width = 256
    for n in range(0, NZ, width):
        cut = slice(n, n + width)
        both = inj[:, cut]
        top = both.astype(BF16)
        right = jnp.concatenate([top, top, (both - top.astype(F32)).astype(BF16)], axis=0)
        out_ref[:, :, cut] = jnp.dot(left, right, preferred_element_type=F32).reshape(CX, CY, width)


def tile_sides(ref, x, yt):
    mid = ref[x, yt * YT:(yt + 1) * YT, :]
    row = lax.broadcasted_iota(jnp.int32, (YT, NZ), 0)
    up, down = pltpu.roll(mid, YT - 1, 0), pltpu.roll(mid, 1, 0)
    if yt < NT - 1:
        up = jnp.where(row == YT - 1, ref[x, (yt + 1) * YT:(yt + 1) * YT + 1, :], up)
    if yt > 0:
        down = jnp.where(row == 0, ref[x, yt * YT - 1:yt * YT, :], down)
    return mid, up, down


def prepare_kernel(recv_ref, table_ref, t_hbm, cap_hbm, soil_hbm, inj_hbm,
                   fx_ref, fy_ref, fz_ref, w_ref, rhs_ref, tn_ref, ex_ref, ey_ref, t_ref, cond, soil, cap, inj, sems):
    copies = []
    step = CX // PARTS
    for part in range(PARTS):
        span = pl.ds(part * step, step)
        for k, (src, dst) in enumerate(((soil_hbm, soil), (t_hbm, t_ref), (cap_hbm, cap))):
            copies.append(pltpu.make_async_copy(src.at[span], dst.at[span], sems.at[3 * part + k]))
    copies.append(pltpu.make_async_copy(inj_hbm, inj, sems.at[3 * PARTS]))
    for copy in copies:
        copy.start()
    table = [table_ref[k] for k in range(NCLS)]

    def fill(x, carry):
        cond[x] = lookup(soil[x], table)
        return carry

    copies[-1].wait()
    add_source(recv_ref, inj, rhs_ref)
    for part in range(PARTS):
        copies[3 * part].wait()
        lax.fori_loop(part * step, (part + 1) * step, fill, 0)
    for part in range(PARTS):
        copies[3 * part + 1].wait()
        copies[3 * part + 2].wait()
    for side, x in enumerate((0, CX - 1)):
        ex_ref[side, 0] = cond[x]
        ex_ref[side, 1] = t_ref[x]
    row = lax.broadcasted_iota(jnp.int32, (YT, NZ), 0)
    lane = lax.broadcasted_iota(jnp.int32, (YT, NZ), 1)

    def plane(x, first, last):
        for yt in range(NT):
            rows = slice(yt * YT, (yt + 1) * YT)
            low, high = yt == 0, yt == NT - 1
            c, cyp, cym = tile_sides(cond, x, yt)
            half = 0.5 * c
            fxp = half if last else 0.5 * (c + cond[x + 1, rows, :])
            fxm = half if first else 0.5 * (c + cond[x - 1, rows, :])
            fyp, fym = 0.5 * (c + cyp), 0.5 * (c + cym)
            if high:
                fyp = jnp.where(row == YT - 1, half, fyp)
            if low:
                fym = jnp.where(row == 0, half, fym)
            fzp = jnp.where(lane == NZ - 1, half, 0.5 * (c + pltpu.roll(c, NZ - 1, 1)))
            fzm = jnp.where(lane == 0, half, 0.5 * (c + pltpu.roll(c, 1, 1)))
            cp = cap[x, rows, :]
            diag = cp + fxp + fxm + fyp + fym + fzp + fzm
            t, typ, tym = tile_sides(t_ref, x, yt)
            rhs = rhs_ref[x, rows, :] + cp * t
            rhs_ref[x, rows, :] = rhs
            total = rhs
            if not last:
                total = total + fxp * t_ref[x + 1, rows, :]
                fx_ref[x, rows, :] = fxp
            if not first:
                total = total + fxm * t_ref[x - 1, rows, :]
            if high:
                fyp = jnp.where(row == YT - 1, F32(0.0), fyp)
            if low:
                fym = jnp.where(row == 0, F32(0.0), fym)
            fzp = jnp.where(lane == NZ - 1, F32(0.0), fzp)
            fzm = jnp.where(lane == 0, F32(0.0), fzm)
            fy_ref[x, rows, :] = fyp
            fz_ref[x, rows, :] = fzp
            total = total + fyp * typ + fym * tym
            total = total + fzp * pltpu.roll(t, NZ - 1, 1) + fzm * pltpu.roll(t, 1, 1)
            if first or last:
                w_ref[x, rows, :] = diag
                tn_ref[x, rows, :] = total
            else:
                w = 0.8 / diag
                w_ref[x, rows, :] = w
                tn_ref[x, rows, :] = (1.0 - 0.8) * t + w * total
            if low or high:
                at = slice(0, 1) if low else slice(YT - 1, YT)
                side = 0 if low else 1
                for k, value in enumerate((total, diag, c, t)):
                    ey_ref[side, k, pl.ds(x, 1), :] = value[at, :]

    def inner(x, carry):
        plane(x, False, False)
        return carry

    plane(0, True, False)
    lax.fori_loop(1, CX - 1, inner, 0)
    plane(CX - 1, False, True)


def at_row(shape, index, value):
    return jnp.where(lax.broadcasted_iota(jnp.int32, shape, 0) == index, value, F32(0.0))


def with_corners(xlo, xhi, ylo, yhi):
    xs, ys = xlo.shape, ylo.shape
    return (xlo + at_row(xs, 0, ylo[0:1]) + at_row(xs, CY - 1, yhi[0:1]),
            xhi + at_row(xs, 0, ylo[CX - 1:CX]) + at_row(xs, CY - 1, yhi[CX - 1:CX]),
            ylo + at_row(ys, 0, xlo[0:1]) + at_row(ys, CX - 1, xhi[0:1]),
            yhi + at_row(ys, 0, xlo[CY - 1:CY]) + at_row(ys, CX - 1, xhi[CY - 1:CY]))


def fix_y_kernel(table_ref, hya, hyb, ey_ref, more_ref, face_ref, term_ref):
    table = [table_ref[k] for k in range(NCLS)]
    gy = lax.axis_index("gy")
    halo = split(hya[...], hyb[...], even("gy"))
    for k, inside in enumerate((gy > 0, gy < NGY - 1)):
        inside = jnp.where(inside, F32(1.0), F32(0.0))
        more = 0.5 * lookup(halo[k][CX:].astype(jnp.int32), table) * inside
        face = (0.5 * ey_ref[k, 2] + more) * inside
        more_ref[k] = more
        face_ref[k] = face
        term_ref[k] = face * halo[k][0:CX]


def fix_kernel(table_ref, hxa, hxb, my_ref, fy_ref, gy_ref, w_ref, tn_ref, ex_ref, ey_ref,
               xa, xb, ya, yb, wx_ref, wy_ref, ax_ref, ay_ref):
    table = [table_ref[k] for k in range(NCLS)]
    gx = lax.axis_index("gx")
    within = [jnp.where(q, F32(1.0), F32(0.0)) for q in (gx > 0, gx < NGX - 1)]
    t_halo = split(hxa[0:CY, :], hxb[0:CY, :], even("gx"))
    klass = split(hxa[CY:, :], hxb[CY:, :], even("gx"))
    more = [0.5 * lookup(k.astype(jnp.int32), table) * q for k, q in zip(klass, within)]
    face = [(0.5 * ex_ref[k, 0] + more[k]) * within[k] for k in range(2)] + [fy_ref[0], fy_ref[1]]
    diag = with_corners(*more, my_ref[0], my_ref[1])
    total = with_corners(face[0] * t_halo[0], face[1] * t_halo[1], gy_ref[0], gy_ref[1])
    total = [a + b for a, b in zip(total, (tn_ref[0], tn_ref[CX - 1], ey_ref[0, 0], ey_ref[1, 0]))]
    w = [0.8 / (a + b) for a, b in zip(diag, (w_ref[0], w_ref[CX - 1], ey_ref[0, 1], ey_ref[1, 1]))]
    old = (ex_ref[0, 1], ex_ref[1, 1], ey_ref[0, 3], ey_ref[1, 3])
    new = [(1.0 - 0.8) * t + a * b for t, a, b in zip(old, w, total)]
    xa[...], xb[...] = split(new[0], new[1], even("gx"))
    ya[...], yb[...] = split(new[2], new[3], even("gy"))
    for k in range(2):
        wx_ref[k], wy_ref[k] = w[k], w[2 + k]
        ax_ref[k], ay_ref[k] = w[k] * face[k], w[2 + k] * face[2 + k]


def y_term_kernel(ay_ref, hya, hyb, gy_ref):
    lo, hi = split(hya[...], hyb[...], even("gy"))
    gy_ref[0] = ay_ref[0] * lo
    gy_ref[1] = ay_ref[1] * hi


def faces_of(tn_ref, py_ref, ax_ref, gy_ref, hxa, hxb):
    lo, hi = split(hxa[...], hxb[...], even("gx"))
    terms = with_corners(ax_ref[0] * lo, ax_ref[1] * hi, gy_ref[0], gy_ref[1])
    return [a + b for a, b in zip(terms, (tn_ref[0], tn_ref[CX - 1], py_ref[0], py_ref[1]))]


def edge_kernel(tn_ref, py_ref, ax_ref, gy_ref, hxa, hxb, xa, xb, ya, yb):
    new = faces_of(tn_ref, py_ref, ax_ref, gy_ref, hxa, hxb)
    xa[...], xb[...] = split(new[0], new[1], even("gx"))
    ya[...], yb[...] = split(new[2], new[3], even("gy"))


def put_edges(ref, xlo, xhi, ylo, yhi):
    ref[0] = xlo
    ref[CX - 1] = xhi
    for x in range(1, CX - 1):
        ref[x, 0:1, :] = ylo[x:x + 1]
        ref[x, CY - 1:CY, :] = yhi[x:x + 1]


def sweep_plane(x, first, last, t_ref, fx_ref, fy_ref, fz_ref, w_ref, rhs_ref, tn_ref, py_ref):
    row = lax.broadcasted_iota(jnp.int32, (YT, NZ), 0)
    lane = lax.broadcasted_iota(jnp.int32, (YT, NZ), 1)
    for yt in range(NT):
        rows = slice(yt * YT, (yt + 1) * YT)
        t, typ, tym = tile_sides(t_ref, x, yt)
        fy, _, fym = tile_sides(fy_ref, x, yt)
        if yt == 0:
            fym = jnp.where(row == 0, F32(0.0), fym)
        fz = fz_ref[x, rows, :]
        total = rhs_ref[x, rows, :] + fy * typ + fym * tym
        if not last:
            total = total + fx_ref[x, rows, :] * t_ref[x + 1, rows, :]
        if not first:
            total = total + fx_ref[x - 1, rows, :] * t_ref[x - 1, rows, :]
        total = total + fz * pltpu.roll(t, NZ - 1, 1)
        total = total + jnp.where(lane == 0, F32(0.0), pltpu.roll(fz * t, 1, 1))
        tn = (1.0 - 0.8) * t + w_ref[x, rows, :] * total
        tn_ref[x, rows, :] = tn
        if yt == 0:
            py_ref[0, pl.ds(x, 1), :] = tn[0:1, :]
        if yt == NT - 1:
            py_ref[1, pl.ds(x, 1), :] = tn[YT - 1:YT, :]


def sweep_inside(refs, start=1, stop=CX - 1):
    def inner(x, carry):
        sweep_plane(x, False, False, *refs)
        return carry

    lax.fori_loop(start, stop, inner, 0)


def first_sweep_kernel(fx_ref, fy_ref, fz_ref, rhs_ref, xa, xb, ya, yb, wx_ref, wy_ref, w_in, t_in,
                       w_ref, t_ref, tn_ref, py_ref):
    put_edges(w_ref, wx_ref[0], wx_ref[1], wy_ref[0], wy_ref[1])
    sweep(fx_ref, fy_ref, fz_ref, rhs_ref, w_ref, xa, xb, ya, yb, t_ref, tn_ref, py_ref)


def sweep(fx_ref, fy_ref, fz_ref, rhs_ref, w_ref, xa, xb, ya, yb, t_ref, tn_ref, py_ref):
    put_edges(t_ref, *split(xa[...], xb[...], even("gx")), *split(ya[...], yb[...], even("gy")))
    refs = (t_ref, fx_ref, fy_ref, fz_ref, w_ref, rhs_ref, tn_ref, py_ref)
    sweep_plane(0, True, False, *refs)
    sweep_inside(refs)
    sweep_plane(CX - 1, False, True, *refs)


def sweep_kernel(fx_ref, fy_ref, fz_ref, rhs_ref, w_ref, xa, xb, ya, yb, t_in, t_ref, tn_ref, py_ref):
    sweep(fx_ref, fy_ref, fz_ref, rhs_ref, w_ref, xa, xb, ya, yb, t_ref, tn_ref, py_ref)


def last_sweep_kernel(fx_ref, fy_ref, fz_ref, rhs_ref, w_ref, xa, xb, ya, yb, t_in, t_ref, tn_ref, py_ref, out_ref, sems):
    put_edges(t_ref, *split(xa[...], xb[...], even("gx")), *split(ya[...], yb[...], even("gy")))
    refs = (t_ref, fx_ref, fy_ref, fz_ref, w_ref, rhs_ref, tn_ref, py_ref)
    bounds = list(range(1, CX - 1, 4)) + [CX - 1]
    copies = []
    for k, (start, stop) in enumerate(zip(bounds[:-1], bounds[1:])):
        sweep_inside(refs, start, stop)
        part = (pl.ds(start, stop - start), pl.ds(YT, CY - 2 * YT))
        copies.append(pltpu.make_async_copy(tn_ref.at[part], out_ref.at[part], sems.at[k]))
        copies[-1].start()
    sweep_plane(0, True, False, *refs)
    sweep_plane(CX - 1, False, True, *refs)
    for copy in copies:
        copy.wait()


def finish_kernel(tn_ref, py_ref, ax_ref, gy_ref, hxa, hxb, out_in, out_ref, x_out, lo_out, hi_out, sems):
    xlo, xhi, ylo, yhi = faces_of(tn_ref, py_ref, ax_ref, gy_ref, hxa, hxb)
    x_out[0] = xlo
    x_out[1] = xhi
    row = lax.broadcasted_iota(jnp.int32, (YT, NZ), 0)
    for x in range(1, CX - 1):
        lo_out[x - 1] = jnp.where(row == 0, ylo[x:x + 1], tn_ref[x, 0:YT, :])
        hi_out[x - 1] = jnp.where(row == YT - 1, yhi[x:x + 1], tn_ref[x, CY - YT:CY, :])
    inside = pl.ds(1, CX - 2)
    load([(x_out.at[0], out_ref.at[0]), (x_out.at[1], out_ref.at[CX - 1]),
          (lo_out, out_ref.at[inside, 0:YT]), (hi_out, out_ref.at[inside, CY - YT:CY])], sems)


def swaps(axis, count, a, b):
    one = [(i, i + 1) for i in range(0, count, 2)]
    two = [(i, (i + 1) % count) for i in range(1, count, 2)]
    return [lax.ppermute(v, axis, p + [(j, i) for i, j in p]) for v, p in ((a, one), (b, two))]


def exchange(xa, xb, ya, yb):
    return near(*swaps("gx", NGX, xa, xb), *swaps("gy", NGY, ya, yb))


def call(kernel, outs, specs, scratch=(), alias={}, mib=1, us=0.1, out_specs=None):
    return pl.pallas_call(
        kernel,
        out_shape=outs,
        in_specs=specs,
        out_specs=out_specs or [VM] * len(outs),
        scratch_shapes=scratch,
        input_output_aliases=alias,
        compiler_params=pltpu.CompilerParams(vmem_limit_bytes=mib * 1024 * 1024),
        cost_estimate=pl.CostEstimate(flops=int(us * 1e9), bytes_accessed=int(us * 3e6), transcendentals=0),
    )


SLAB = local(CX, CY, NZ)
FACES = (local(CY, NZ), local(CY, NZ), local(CX, NZ), local(CX, NZ))
XX, YY = local(2, CY, NZ), local(2, CX, NZ)
DMA = pltpu.SemaphoreType.DMA
I32 = jnp.int32


def shards(temp_old, capacity, soil_class, cond_table, losses, owner, column, injection):
    rows, rows_int = local(CX, YT, NZ), local(CX, YT, NZ, dtype=I32)
    send, *faces = call(
        start_kernel, (local(NGY * CHUNK, LW),) + (local(2 * CY, NZ),) * 2 + (local(2 * CX, NZ),) * 2, [HB] * 5,
        [rows, rows, rows_int, rows_int, XX, local(2, CY, NZ, dtype=I32), local(SEG, LW), local(1, SEG, dtype=I32),
         local(1, SEG, dtype=I32), DMA((11,))], mib=6)(
        *far(temp_old, soil_class, losses, owner.reshape(1, SEG), column.reshape(1, SEG)))
    recv = lax.all_to_all(send, "gy", 0, 0, tiled=True)
    halo = exchange(*faces)
    fx, fy, fz, w, rhs, new, ex, ey = call(
        prepare_kernel, (SLAB,) * 6 + (local(2, 2, CY, NZ), local(2, 4, CX, NZ)), [VM, SM] + [HB] * 4,
        [SLAB, SLAB, local(CX, CY, NZ, dtype=I32), SLAB, local(LW, NZ), DMA((3 * PARTS + 1,))], mib=16, us=0.1)(
        *near(recv), cond_table, *far(temp_old, capacity, soil_class, injection))
    hxa, hxb, hya, hyb = halo
    my, fyh, gy = call(fix_y_kernel, (YY, YY, YY), [SM] + [VM] * 3, us=8.0)(cond_table, hya, hyb, *near(ey))
    *faces, wx, wy, ax, ay = call(
        fix_kernel, FACES + (XX, YY, XX, YY), [SM] + [VM] * 9, mib=2)(
        cond_table, hxa, hxb, *near(my, fyh, gy, w, new, ex, ey))
    for number in range(1, SWEEPS):
        halo = exchange(*faces)
        coefs = near(fx, fy, fz, rhs)
        if number == 1:
            w, temp, new, py = call(
                first_sweep_kernel, (SLAB, SLAB, SLAB, YY), [VM] * 12, alias={10: 0, 11: 1}, mib=2)(
                *coefs, *near(*faces, wx, wy, w, new))
        elif number < SWEEPS - 1:
            temp, new, py = call(sweep_kernel, (SLAB, SLAB, YY), [VM] * 10, alias={9: 0}, mib=2)(
                *coefs, *near(w, *faces, new))
        else:
            temp, new, py, out = call(
                last_sweep_kernel, (SLAB, SLAB, YY, pltpu.HBM((CX, CY, NZ), F32)), [VM] * 10, [DMA((4,))],
                alias={9: 0}, mib=2, out_specs=[VM] * 3 + [HB])(*coefs, *near(w, *faces, new))
        hxa, hxb, hya, hyb = halo
        (gy,) = call(y_term_kernel, (YY,), [VM] * 3, us=8.0)(*near(ay), hya, hyb)
        args = near(new, py, ax, gy) + [hxa, hxb]
        if number < SWEEPS - 1:
            faces = call(edge_kernel, FACES, [VM] * 6, mib=2)(*args)
    return call(finish_kernel, (pltpu.HBM((CX, CY, NZ), F32),), [VM] * 6 + [HB],
                [XX, local(CX - 2, YT, NZ), local(CX - 2, YT, NZ), DMA((4,))], alias={6: 0}, mib=4, out_specs=[HB])(*args, out)[0]


def solution(mesh):
    return jax.shard_map(
        shards,
        mesh=mesh,
        in_specs=(
            P("gx", "gy", None),
            P("gx", "gy", None),
            P("gx", "gy", None),
            P(),
            P(("gx", "gy"), None),
            P(("gx", "gy"), None),
            P(("gx", "gy")),
            P(),
        ),
        out_specs=P("gx", "gy", None),
        check_vma=False,
    )
```

```python
import jax
import jax.numpy as jnp
from jax import lax
from jax.experimental import pallas as pl
from jax.experimental.pallas import tpu as pltpu
from jax.sharding import PartitionSpec as P

SWEEPS = 4
NCLS = 8
CX, CY, NZ = 16, 32, 1024
LW = 128
SEG = 256
CAP = 64
NGX, NGY = 32, 8
CHUNK = CAP + 8
YT = 8
NT = CY // YT
PARTS = 4
F32, BF16 = jnp.float32, jnp.bfloat16
HIGH = lax.Precision.HIGHEST
VM = pl.BlockSpec(memory_space=pltpu.VMEM)
SM = pl.BlockSpec(memory_space=pltpu.SMEM)
HB = pl.BlockSpec(memory_space=pltpu.HBM)


def local(*dims, dtype=F32):
    return pltpu.VMEM(dims, dtype)


def near(*arrays):
    return [pltpu.with_memory_space_constraint(a, pltpu.VMEM) for a in arrays]


def far(*arrays):
    return [pltpu.with_memory_space_constraint(a, pltpu.HBM) for a in arrays]


def lookup(klass, table):
    cond = jnp.where(klass == 0, table[0], F32(0.0))
    for k in range(1, NCLS):
        cond = jnp.where(klass == k, table[k], cond)
    return cond


def load(pairs, sems):
    copies = [pltpu.make_async_copy(src, dst, sems.at[i]) for i, (src, dst) in enumerate(pairs)]
    for copy in copies:
        copy.start()
    for copy in copies:
        copy.wait()


def even(axis):
    return lax.rem(lax.axis_index(axis), 2) == 0


def split(a, b, is_even):
    return jnp.where(is_even, b, a), jnp.where(is_even, a, b)


def start_kernel(t_hbm, soil_hbm, loss_hbm, owner_hbm, col_hbm, send_ref, xa, xb, ya, yb,
                 t_lo, t_hi, s_lo, s_hi, tx, sx, loss_ref, owner_ref, col_ref, sems):
    pairs = [(loss_hbm, loss_ref), (owner_hbm, owner_ref), (col_hbm, col_ref),
             (t_hbm.at[:, 0:YT], t_lo), (t_hbm.at[:, CY - YT:CY], t_hi),
             (soil_hbm.at[:, 0:YT], s_lo), (soil_hbm.at[:, CY - YT:CY], s_hi),
             (t_hbm.at[0], tx.at[0]), (t_hbm.at[CX - 1], tx.at[1]),
             (soil_hbm.at[0], sx.at[0]), (soil_hbm.at[CX - 1], sx.at[1])]
    copies = [pltpu.make_async_copy(src, dst, sems.at[i]) for i, (src, dst) in enumerate(pairs)]
    for copy in copies:
        copy.start()
    for copy in copies[:3]:
        copy.wait()
    own = owner_ref[...]
    mine = lax.broadcasted_iota(jnp.int32, (NGY, SEG), 0) == own
    before = lax.broadcasted_iota(jnp.int32, (SEG, SEG), 0) < lax.broadcasted_iota(jnp.int32, (SEG, SEG), 1)
    count = jnp.dot(mine.astype(F32).astype(BF16), before.astype(F32).astype(BF16), preferred_element_type=F32)
    rank = jnp.sum(jnp.where(mine, count, 0.0), axis=0, keepdims=True).astype(jnp.int32)
    slot = own * CAP + rank
    pick = (lax.broadcasted_iota(jnp.int32, (NGY * CAP, SEG), 0) == slot).astype(F32).astype(BF16)
    loss = loss_ref[...]
    sent = jnp.zeros((NGY * CAP, LW), F32)
    for _ in range(3):
        part = loss.astype(BF16)
        loss = loss - part.astype(F32)
        sent = sent + jnp.dot(pick, part, preferred_element_type=F32)
    col = jnp.broadcast_to(col_ref[...], (8, SEG))
    low = lax.rem(col, 128)
    by_lane = (((1,), (1,)), ((), ()))
    cols = lax.dot_general(low.astype(F32).astype(BF16), pick, by_lane, preferred_element_type=F32)
    cols = cols + lax.dot_general((col - low).astype(F32).astype(BF16), pick, by_lane, preferred_element_type=F32)
    for o in range(NGY):
        send_ref[o * CHUNK:o * CHUNK + CAP, :] = sent[o * CAP:(o + 1) * CAP, :]
        crow = cols[:, o * CAP:(o + 1) * CAP]
        send_ref[o * CHUNK + CAP:(o + 1) * CHUNK, :] = jnp.concatenate([crow, crow], axis=1)
    for copy in copies[3:]:
        copy.wait()
    even_x, even_y = even("gx"), even("gy")
    for x in range(CX):
        ya[x:x + 1, :], yb[x:x + 1, :] = split(t_lo[x, 0:1, :], t_hi[x, YT - 1:YT, :], even_y)
        s_a, s_b = split(s_lo[x, 0:1, :], s_hi[x, YT - 1:YT, :], even_y)
        ya[CX + x:CX + x + 1, :] = s_a.astype(F32)
        yb[CX + x:CX + x + 1, :] = s_b.astype(F32)
    xa[0:CY, :], xb[0:CY, :] = split(tx[0], tx[1], even_x)
    s_a, s_b = split(sx[0], sx[1], even_x)
    xa[CY:, :] = s_a.astype(F32)
    xb[CY:, :] = s_b.astype(F32)


def add_source(recv_ref, inj, out_ref):
    lane = lax.broadcasted_iota(jnp.int32, (1, 2 * CAP), 1)
    cell = lax.broadcasted_iota(jnp.int32, (CX * CY, 2 * CAP), 0)
    pick, loss = [], []
    for g in range(0, NGY, 2):
        a, b = g * CHUNK, (g + 1) * CHUNK
        crow = jnp.where(lane < CAP, recv_ref[a + CAP:a + CAP + 1, :], recv_ref[b + CAP:b + CAP + 1, :])
        pick.append((cell == crow.astype(jnp.int32)).astype(F32).astype(BF16))
        loss += [recv_ref[a:a + CAP, :], recv_ref[b:b + CAP, :]]
    pick = jnp.concatenate(pick, axis=1)
    loss = jnp.concatenate(loss, axis=0)
    gathered = jnp.zeros((CX * CY, LW), F32)
    for _ in range(3):
        part = loss.astype(BF16)
        loss = loss - part.astype(F32)
        gathered = gathered + jnp.dot(pick, part, preferred_element_type=F32)
    high = gathered.astype(BF16)
    low = (gathered - high.astype(F32)).astype(BF16)
    left = jnp.concatenate([high, low, high], axis=1)
    width = 256
    for n in range(0, NZ, width):
        cut = slice(n, n + width)
        both = inj[:, cut]
        top = both.astype(BF16)
        right = jnp.concatenate([top, top, (both - top.astype(F32)).astype(BF16)], axis=0)
        out_ref[:, :, cut] = jnp.dot(left, right, preferred_element_type=F32).reshape(CX, CY, width)


def tile_sides(ref, x, yt):
    mid = ref[x, yt * YT:(yt + 1) * YT, :]
    row = lax.broadcasted_iota(jnp.int32, (YT, NZ), 0)
    up, down = pltpu.roll(mid, YT - 1, 0), pltpu.roll(mid, 1, 0)
    if yt < NT - 1:
        up = jnp.where(row == YT - 1, ref[x, (yt + 1) * YT:(yt + 1) * YT + 1, :], up)
    if yt > 0:
        down = jnp.where(row == 0, ref[x, yt * YT - 1:yt * YT, :], down)
    return mid, up, down


def coef_kernel(table_ref, hya, hyb, t_hbm, cap_hbm, soil_hbm, *refs):
    outs, (more_ref, halo_ref, ex_ref, ey_ref, half_ref, t_ref, cap, soil), made, (in_sems, out_sems) = (
        refs[:6], refs[6:14], refs[14:20], refs[20:])
    fx_ref, fy_ref, fz_ref, rhs_ref, tn_ref, w_ref = made
    step = CX // PARTS
    spans = [pl.ds(part * step, step) for part in range(PARTS)]
    copies = []
    for k, (src, dst) in enumerate(((soil_hbm, soil), (t_hbm, t_ref), (cap_hbm, cap))):
        copies.append([pltpu.make_async_copy(src.at[span], dst.at[span], in_sems.at[k, part]) for part, span in enumerate(spans)])
        for copy in copies[k]:
            copy.start()
    table = [0.5 * table_ref[k] for k in range(NCLS)]
    gy = lax.axis_index("gy")
    halo = split(hya[...], hyb[...], even("gy"))
    for k, inside in enumerate((gy > 0, gy < NGY - 1)):
        more_ref[k] = lookup(halo[k][CX:].astype(jnp.int32), table) * jnp.where(inside, F32(1.0), F32(0.0))
        halo_ref[k] = halo[k][0:CX]

    def fill(x, carry):
        half_ref[x] = lookup(soil[x], table)
        return carry

    for part in range(PARTS):
        copies[0][part].wait()
        lax.fori_loop(part * step, (part + 1) * step, fill, 0)
    for part in range(PARTS):
        copies[1][part].wait()
        copies[2][part].wait()
    for side, x in enumerate((0, CX - 1)):
        ex_ref[side, 0] = half_ref[x]
        ex_ref[side, 1] = t_ref[x]
    row = lax.broadcasted_iota(jnp.int32, (YT, NZ), 0)
    lane = lax.broadcasted_iota(jnp.int32, (YT, NZ), 1)
    at_end = lane == NZ - 1
    at_ends = jnp.logical_or(at_end, lane == 0)

    def plane(x, first, last):
        for yt in range(NT):
            rows = slice(yt * YT, (yt + 1) * YT)
            low, high = yt == 0, yt == NT - 1
            c, cyp, cym = tile_sides(half_ref, x, yt)
            t, typ, tym = tile_sides(t_ref, x, yt)
            fyp, fym = c + cyp, c + cym
            fz = jnp.where(at_end, F32(0.0), c + pltpu.roll(c, NZ - 1, 1))
            cp = cap[x, rows, :]
            diag = cp + fz + pltpu.roll(fz, 1, 1) + jnp.where(at_ends, c, F32(0.0))
            if high:
                diag = diag + jnp.where(row == YT - 1, c, fyp)
                fyp = jnp.where(row == YT - 1, F32(0.0), fyp)
            else:
                diag = diag + fyp
            if low:
                diag = diag + jnp.where(row == 0, c, fym)
                fym = jnp.where(row == 0, F32(0.0), fym)
            else:
                diag = diag + fym
            rhs = cp * t
            total = rhs + fyp * typ + fym * tym
            if last:
                diag = diag + c
            else:
                fxp = c + half_ref[x + 1, rows, :]
                diag = diag + fxp
                total = total + fxp * t_ref[x + 1, rows, :]
                fx_ref[x, rows, :] = fxp
            if first:
                diag = diag + c
            else:
                fxm = c + half_ref[x - 1, rows, :]
                diag = diag + fxm
                total = total + fxm * t_ref[x - 1, rows, :]
            total = total + fz * pltpu.roll(t, NZ - 1, 1) + pltpu.roll(fz * t, 1, 1)
            rhs_ref[x, rows, :] = rhs
            fy_ref[x, rows, :] = fyp
            fz_ref[x, rows, :] = fz
            if first or last:
                w_ref[x, rows, :] = diag
                tn_ref[x, rows, :] = total
            else:
                w = 0.8 / diag
                w_ref[x, rows, :] = w
                tn_ref[x, rows, :] = (1.0 - 0.8) * t + w * total
            if low or high:
                at = slice(0, 1) if low else slice(YT - 1, YT)
                side = 0 if low else 1
                for k, value in enumerate((total, diag, c, t)):
                    ey_ref[side, k, pl.ds(x, 1), :] = value[at, :]

    def inner(x, carry):
        plane(x, False, False)
        return carry

    leaving = []
    for part in range(PARTS):
        if part == 0:
            plane(0, True, False)
        lax.fori_loop(max(1, part * step), min(CX - 1, (part + 1) * step), inner, 0)
        if part == PARTS - 1:
            fx_ref[CX - 1] = jnp.zeros((CY, NZ), F32)
            plane(CX - 1, False, True)
        for k in range(6):
            leaving.append(pltpu.make_async_copy(made[k].at[spans[part]], outs[k].at[spans[part]], out_sems.at[k, part]))
            leaving[-1].start()
    for copy in leaving:
        copy.wait()


def source_kernel(recv_ref, inj_hbm, rhs_hbm, tn_hbm, w_hbm, ey_in, rhs_ref, tn_ref, w_ref, ey_ref, source, inj, sems):
    pairs = [(inj_hbm, inj), (rhs_hbm, rhs_ref), (tn_hbm, tn_ref), (w_hbm, w_ref)]
    copies = [pltpu.make_async_copy(src, dst, sems.at[k]) for k, (src, dst) in enumerate(pairs)]
    for copy in copies:
        copy.start()
    copies[0].wait()
    add_source(recv_ref, inj, source)
    copies[1].wait()
    copies[2].wait()
    copies[3].wait()

    def plane(x, edge):
        for yt in range(NT):
            rows = slice(yt * YT, (yt + 1) * YT)
            src = source[x, rows, :]
            rhs_ref[x, rows, :] = rhs_ref[x, rows, :] + src
            tn_ref[x, rows, :] = tn_ref[x, rows, :] + (src if edge else w_ref[x, rows, :] * src)
        for side, y in enumerate((0, CY - 1)):
            ey_ref[side, 0, pl.ds(x, 1), :] = ey_in[side, 0, pl.ds(x, 1), :] + source[x, y:y + 1, :]

    def inner(x, carry):
        plane(x, False)
        return carry

    plane(0, True)
    lax.fori_loop(1, CX - 1, inner, 0)
    plane(CX - 1, True)


def at_row(shape, index, value):
    return jnp.where(lax.broadcasted_iota(jnp.int32, shape, 0) == index, value, F32(0.0))


def with_corners(xlo, xhi, ylo, yhi):
    xs, ys = xlo.shape, ylo.shape
    return (xlo + at_row(xs, 0, ylo[0:1]) + at_row(xs, CY - 1, yhi[0:1]),
            xhi + at_row(xs, 0, ylo[CX - 1:CX]) + at_row(xs, CY - 1, yhi[CX - 1:CX]),
            ylo + at_row(ys, 0, xlo[0:1]) + at_row(ys, CX - 1, xhi[0:1]),
            yhi + at_row(ys, 0, xlo[CY - 1:CY]) + at_row(ys, CX - 1, xhi[CY - 1:CY]))


def fix_kernel(table_ref, hxa, hxb, my_ref, ty_ref, w_ref, tn_ref, ex_ref, ey_ref,
               xa, xb, ya, yb, wx_ref, wy_ref, ax_ref, ay_ref):
    table = [0.5 * table_ref[k] for k in range(NCLS)]
    gx, gy = lax.axis_index("gx"), lax.axis_index("gy")
    within = [jnp.where(q, F32(1.0), F32(0.0)) for q in (gx > 0, gx < NGX - 1, gy > 0, gy < NGY - 1)]
    t_halo = split(hxa[0:CY, :], hxb[0:CY, :], even("gx")) + (ty_ref[0], ty_ref[1])
    klass = split(hxa[CY:, :], hxb[CY:, :], even("gx"))
    more = [lookup(k.astype(jnp.int32), table) * q for k, q in zip(klass, within)] + [my_ref[0], my_ref[1]]
    conds = (ex_ref[0, 0], ex_ref[1, 0], ey_ref[0, 2], ey_ref[1, 2])
    face = [(c + m) * q for c, m, q in zip(conds, more, within)]
    diag = with_corners(*more)
    total = with_corners(*[f * t for f, t in zip(face, t_halo)])
    total = [a + b for a, b in zip(total, (tn_ref[0], tn_ref[CX - 1], ey_ref[0, 0], ey_ref[1, 0]))]
    w = [0.8 / (a + b) for a, b in zip(diag, (w_ref[0], w_ref[CX - 1], ey_ref[0, 1], ey_ref[1, 1]))]
    old = (ex_ref[0, 1], ex_ref[1, 1], ey_ref[0, 3], ey_ref[1, 3])
    new = [(1.0 - 0.8) * t + a * b for t, a, b in zip(old, w, total)]
    xa[...], xb[...] = split(new[0], new[1], even("gx"))
    ya[...], yb[...] = split(new[2], new[3], even("gy"))
    for k in range(2):
        wx_ref[k], wy_ref[k] = w[k], w[2 + k]
        ax_ref[k], ay_ref[k] = w[k] * face[k], w[2 + k] * face[2 + k]


def y_term_kernel(ay_ref, hya, hyb, gy_ref):
    lo, hi = split(hya[...], hyb[...], even("gy"))
    gy_ref[0] = ay_ref[0] * lo
    gy_ref[1] = ay_ref[1] * hi


def faces_of(tn_ref, py_ref, ax_ref, gy_ref, hxa, hxb):
    lo, hi = split(hxa[...], hxb[...], even("gx"))
    terms = with_corners(ax_ref[0] * lo, ax_ref[1] * hi, gy_ref[0], gy_ref[1])
    return [a + b for a, b in zip(terms, (tn_ref[0], tn_ref[CX - 1], py_ref[0], py_ref[1]))]


def edge_kernel(tn_ref, py_ref, ax_ref, gy_ref, hxa, hxb, xa, xb, ya, yb):
    new = faces_of(tn_ref, py_ref, ax_ref, gy_ref, hxa, hxb)
    xa[...], xb[...] = split(new[0], new[1], even("gx"))
    ya[...], yb[...] = split(new[2], new[3], even("gy"))


def put_edges(ref, xlo, xhi, ylo, yhi):
    ref[0] = xlo
    ref[CX - 1] = xhi
    for x in range(1, CX - 1):
        ref[x, 0:1, :] = ylo[x:x + 1]
        ref[x, CY - 1:CY, :] = yhi[x:x + 1]


def sweep_plane(x, first, last, t_ref, fx_ref, fy_ref, fz_ref, w_ref, rhs_ref, tn_ref, py_ref):
    row = lax.broadcasted_iota(jnp.int32, (YT, NZ), 0)
    for yt in range(NT):
        rows = slice(yt * YT, (yt + 1) * YT)
        t, typ, tym = tile_sides(t_ref, x, yt)
        fy, _, fym = tile_sides(fy_ref, x, yt)
        if yt == 0:
            fym = jnp.where(row == 0, F32(0.0), fym)
        fz = fz_ref[x, rows, :]
        total = rhs_ref[x, rows, :] + fy * typ + fym * tym
        if not last:
            total = total + fx_ref[x, rows, :] * t_ref[x + 1, rows, :]
        if not first:
            total = total + fx_ref[x - 1, rows, :] * t_ref[x - 1, rows, :]
        total = total + fz * pltpu.roll(t, NZ - 1, 1)
        total = total + pltpu.roll(fz * t, 1, 1)
        tn = (1.0 - 0.8) * t + w_ref[x, rows, :] * total
        tn_ref[x, rows, :] = tn
        if yt == 0:
            py_ref[0, pl.ds(x, 1), :] = tn[0:1, :]
        if yt == NT - 1:
            py_ref[1, pl.ds(x, 1), :] = tn[YT - 1:YT, :]


def sweep_inside(refs, start=1, stop=CX - 1):
    def inner(x, carry):
        sweep_plane(x, False, False, *refs)
        return carry

    lax.fori_loop(start, stop, inner, 0)


def first_sweep_kernel(fx_hbm, fy_hbm, fz_hbm, rhs_ref, xa, xb, ya, yb, wx_ref, wy_ref, w_in, t_in,
                       w_ref, t_ref, tn_ref, py_ref, fx_ref, fy_ref, fz_ref, sems):
    step = CX // PARTS
    pairs = ((fx_hbm, fx_ref), (fy_hbm, fy_ref), (fz_hbm, fz_ref))
    copies = [[pltpu.make_async_copy(src.at[pl.ds(part * step, step)], dst.at[pl.ds(part * step, step)], sems.at[k, part])
               for k, (src, dst) in enumerate(pairs)] for part in range(PARTS)]
    for part in range(PARTS):
        for copy in copies[part]:
            copy.start()
    put_edges(w_ref, wx_ref[0], wx_ref[1], wy_ref[0], wy_ref[1])
    put_edges(t_ref, *split(xa[...], xb[...], even("gx")), *split(ya[...], yb[...], even("gy")))
    refs = (t_ref, fx_ref, fy_ref, fz_ref, w_ref, rhs_ref, tn_ref, py_ref)
    for part in range(PARTS):
        for copy in copies[part]:
            copy.wait()
        if part == 0:
            sweep_plane(0, True, False, *refs)
        sweep_inside(refs, max(1, part * step), min(CX - 1, (part + 1) * step))
    sweep_plane(CX - 1, False, True, *refs)


def sweep(fx_ref, fy_ref, fz_ref, rhs_ref, w_ref, xa, xb, ya, yb, t_ref, tn_ref, py_ref):
    put_edges(t_ref, *split(xa[...], xb[...], even("gx")), *split(ya[...], yb[...], even("gy")))
    refs = (t_ref, fx_ref, fy_ref, fz_ref, w_ref, rhs_ref, tn_ref, py_ref)
    sweep_plane(0, True, False, *refs)
    sweep_inside(refs)
    sweep_plane(CX - 1, False, True, *refs)


def sweep_kernel(fx_ref, fy_ref, fz_ref, rhs_ref, w_ref, xa, xb, ya, yb, t_in, t_ref, tn_ref, py_ref):
    sweep(fx_ref, fy_ref, fz_ref, rhs_ref, w_ref, xa, xb, ya, yb, t_ref, tn_ref, py_ref)


def last_sweep_kernel(fx_ref, fy_ref, fz_ref, rhs_ref, w_ref, xa, xb, ya, yb, t_in, t_ref, tn_ref, py_ref, out_ref, sems):
    put_edges(t_ref, *split(xa[...], xb[...], even("gx")), *split(ya[...], yb[...], even("gy")))
    refs = (t_ref, fx_ref, fy_ref, fz_ref, w_ref, rhs_ref, tn_ref, py_ref)
    bounds = list(range(1, CX - 1, 4)) + [CX - 1]
    copies = []
    for k, (start, stop) in enumerate(zip(bounds[:-1], bounds[1:])):
        sweep_inside(refs, start, stop)
        part = (pl.ds(start, stop - start), pl.ds(YT, CY - 2 * YT))
        copies.append(pltpu.make_async_copy(tn_ref.at[part], out_ref.at[part], sems.at[k]))
        copies[-1].start()
    sweep_plane(0, True, False, *refs)
    sweep_plane(CX - 1, False, True, *refs)
    for copy in copies:
        copy.wait()


def finish_kernel(tn_ref, py_ref, ax_ref, gy_ref, hxa, hxb, out_in, out_ref, x_out, lo_out, hi_out, sems):
    xlo, xhi, ylo, yhi = faces_of(tn_ref, py_ref, ax_ref, gy_ref, hxa, hxb)
    x_out[0] = xlo
    x_out[1] = xhi
    row = lax.broadcasted_iota(jnp.int32, (YT, NZ), 0)
    for x in range(1, CX - 1):
        lo_out[x - 1] = jnp.where(row == 0, ylo[x:x + 1], tn_ref[x, 0:YT, :])
        hi_out[x - 1] = jnp.where(row == YT - 1, yhi[x:x + 1], tn_ref[x, CY - YT:CY, :])
    inside = pl.ds(1, CX - 2)
    load([(x_out.at[0], out_ref.at[0]), (x_out.at[1], out_ref.at[CX - 1]),
          (lo_out, out_ref.at[inside, 0:YT]), (hi_out, out_ref.at[inside, CY - YT:CY])], sems)


def swaps(axis, count, a, b):
    one = [(i, i + 1) for i in range(0, count, 2)]
    two = [(i, (i + 1) % count) for i in range(1, count, 2)]
    return [lax.ppermute(v, axis, p + [(j, i) for i, j in p]) for v, p in ((a, one), (b, two))]


def exchange(xa, xb, ya, yb):
    return near(*swaps("gx", NGX, xa, xb), *swaps("gy", NGY, ya, yb))


def call(kernel, outs, specs, scratch=(), alias={}, mib=1, us=0.1, out_specs=None):
    return pl.pallas_call(
        kernel,
        out_shape=outs,
        in_specs=specs,
        out_specs=out_specs or [VM] * len(outs),
        scratch_shapes=scratch,
        input_output_aliases=alias,
        compiler_params=pltpu.CompilerParams(vmem_limit_bytes=mib * 1024 * 1024),
        cost_estimate=pl.CostEstimate(flops=int(us * 1e9), bytes_accessed=int(us * 3e6), transcendentals=0),
    )


SLAB = local(CX, CY, NZ)
FACES = (local(CY, NZ), local(CY, NZ), local(CX, NZ), local(CX, NZ))
XX, YY = local(2, CY, NZ), local(2, CX, NZ)
DMA = pltpu.SemaphoreType.DMA
I32 = jnp.int32
FIXY, PREP = 20.0, 0.1


def shards(temp_old, capacity, soil_class, cond_table, losses, owner, column, injection):
    rows, rows_int = local(CX, YT, NZ), local(CX, YT, NZ, dtype=I32)
    send, *faces = call(
        start_kernel, (local(NGY * CHUNK, LW),) + (local(2 * CY, NZ),) * 2 + (local(2 * CX, NZ),) * 2, [HB] * 5,
        [rows, rows, rows_int, rows_int, XX, local(2, CY, NZ, dtype=I32), local(SEG, LW), local(1, SEG, dtype=I32),
         local(1, SEG, dtype=I32), DMA((11,))], mib=6)(
        *far(temp_old, soil_class, losses, owner.reshape(1, SEG), column.reshape(1, SEG)))
    recv = lax.all_to_all(send, "gy", 0, 0, tiled=True)
    halo = exchange(*faces)
    hxa, hxb, hya, hyb = halo
    edge_x, edge_y = local(2, 2, CY, NZ), local(2, 4, CX, NZ)
    *stored, my, ty, ex, ey = call(
        coef_kernel, (pltpu.HBM((CX, CY, NZ), F32),) * 6 + (YY, YY, edge_x, edge_y), [SM] + [VM] * 2 + [HB] * 3,
        [SLAB, SLAB, SLAB, local(CX, CY, NZ, dtype=I32)] + [SLAB] * 6 + [DMA((3, PARTS)), DMA((6, PARTS))],
        mib=24, us=FIXY, out_specs=[HB] * 6 + [VM] * 4)(
        cond_table, hya, hyb, *far(temp_old, capacity, soil_class))
    rhs, new, w, ey = call(
        source_kernel, (SLAB,) * 3 + (edge_y,), [VM] + [HB] * 4 + [VM], [SLAB, local(LW, NZ), DMA((4,))],
        alias={5: 3}, mib=8, us=PREP)(*near(recv), *far(injection, *stored[3:]), *near(ey))
    *faces, wx, wy, ax, ay = call(fix_kernel, FACES + (XX, YY, XX, YY), [SM] + [VM] * 8, mib=2)(
        cond_table, hxa, hxb, *near(my, ty, w, new, ex, ey))
    for number in range(1, SWEEPS):
        halo = exchange(*faces)
        if number == 1:
            w, temp, new, py, fx, fy, fz = call(
                first_sweep_kernel, (SLAB, SLAB, SLAB, YY, SLAB, SLAB, SLAB), [HB] * 3 + [VM] * 9, [DMA((3, PARTS))],
                alias={10: 0, 11: 1}, mib=2)(*far(*stored[:3]), *near(rhs, *faces, wx, wy, w, new))
            coefs = near(fx, fy, fz, rhs)
        elif number < SWEEPS - 1:
            temp, new, py = call(sweep_kernel, (SLAB, SLAB, YY), [VM] * 10, alias={9: 0}, mib=2)(
                *coefs, *near(w, *faces, new))
        else:
            temp, new, py, out = call(
                last_sweep_kernel, (SLAB, SLAB, YY, pltpu.HBM((CX, CY, NZ), F32)), [VM] * 10, [DMA((4,))],
                alias={9: 0}, mib=2, out_specs=[VM] * 3 + [HB])(*coefs, *near(w, *faces, new))
        hxa, hxb, hya, hyb = halo
        (gy,) = call(y_term_kernel, (YY,), [VM] * 3, us=8.0)(*near(ay), hya, hyb)
        args = near(new, py, ax, gy) + [hxa, hxb]
        if number < SWEEPS - 1:
            faces = call(edge_kernel, FACES, [VM] * 6, mib=2)(*args)
    return call(finish_kernel, (pltpu.HBM((CX, CY, NZ), F32),), [VM] * 6 + [HB],
                [XX, local(CX - 2, YT, NZ), local(CX - 2, YT, NZ), DMA((4,))], alias={6: 0}, mib=4, out_specs=[HB])(*args, out)[0]


def solution(mesh):
    return jax.shard_map(
        shards,
        mesh=mesh,
        in_specs=(
            P("gx", "gy", None),
            P("gx", "gy", None),
            P("gx", "gy", None),
            P(),
            P(("gx", "gy"), None),
            P(("gx", "gy"), None),
            P(("gx", "gy")),
            P(),
        ),
        out_specs=P("gx", "gy", None),
        check_vma=False,
    )
```

```python
import jax
import jax.numpy as jnp
from jax import lax
from jax.experimental import pallas as pl
from jax.experimental.pallas import tpu as pltpu
from jax.sharding import PartitionSpec as P

SWEEPS = 4
NCLS = 8
CX, CY, NZ = 16, 32, 1024
LW = 128
SEG = 256
CAP = 64
NGX, NGY = 32, 8
CHUNK = CAP + 8
YT = 8
NT = CY // YT
PARTS = 4
F32, BF16 = jnp.float32, jnp.bfloat16
HIGH = lax.Precision.HIGHEST
VM = pl.BlockSpec(memory_space=pltpu.VMEM)
SM = pl.BlockSpec(memory_space=pltpu.SMEM)
HB = pl.BlockSpec(memory_space=pltpu.HBM)


def local(*dims, dtype=F32):
    return pltpu.VMEM(dims, dtype)


def near(*arrays):
    return [pltpu.with_memory_space_constraint(a, pltpu.VMEM) for a in arrays]


def far(*arrays):
    return [pltpu.with_memory_space_constraint(a, pltpu.HBM) for a in arrays]


def lookup(klass, table):
    cond = jnp.where(klass == 0, table[0], F32(0.0))
    for k in range(1, NCLS):
        cond = jnp.where(klass == k, table[k], cond)
    return cond


def load(pairs, sems):
    copies = [pltpu.make_async_copy(src, dst, sems.at[i]) for i, (src, dst) in enumerate(pairs)]
    for copy in copies:
        copy.start()
    for copy in copies:
        copy.wait()


def even(axis):
    return lax.rem(lax.axis_index(axis), 2) == 0


def split(a, b, is_even):
    return jnp.where(is_even, b, a), jnp.where(is_even, a, b)


def start_kernel(t_hbm, soil_hbm, loss_hbm, owner_hbm, col_hbm, send_ref, xa, xb, ya, yb,
                 t_lo, t_hi, s_lo, s_hi, tx, sx, loss_ref, owner_ref, col_ref, sems):
    pairs = [(loss_hbm, loss_ref), (owner_hbm, owner_ref), (col_hbm, col_ref),
             (t_hbm.at[:, 0:YT], t_lo), (t_hbm.at[:, CY - YT:CY], t_hi),
             (soil_hbm.at[:, 0:YT], s_lo), (soil_hbm.at[:, CY - YT:CY], s_hi),
             (t_hbm.at[0], tx.at[0]), (t_hbm.at[CX - 1], tx.at[1]),
             (soil_hbm.at[0], sx.at[0]), (soil_hbm.at[CX - 1], sx.at[1])]
    copies = [pltpu.make_async_copy(src, dst, sems.at[i]) for i, (src, dst) in enumerate(pairs)]
    for copy in copies:
        copy.start()
    for copy in copies[:3]:
        copy.wait()
    own = owner_ref[...]
    mine = lax.broadcasted_iota(jnp.int32, (NGY, SEG), 0) == own
    before = lax.broadcasted_iota(jnp.int32, (SEG, SEG), 0) < lax.broadcasted_iota(jnp.int32, (SEG, SEG), 1)
    count = jnp.dot(mine.astype(F32).astype(BF16), before.astype(F32).astype(BF16), preferred_element_type=F32)
    rank = jnp.sum(jnp.where(mine, count, 0.0), axis=0, keepdims=True).astype(jnp.int32)
    slot = own * CAP + rank
    pick = (lax.broadcasted_iota(jnp.int32, (NGY * CAP, SEG), 0) == slot).astype(F32).astype(BF16)
    loss = loss_ref[...]
    sent = jnp.zeros((NGY * CAP, LW), F32)
    for _ in range(3):
        part = loss.astype(BF16)
        loss = loss - part.astype(F32)
        sent = sent + jnp.dot(pick, part, preferred_element_type=F32)
    col = jnp.broadcast_to(col_ref[...], (8, SEG))
    low = lax.rem(col, 128)
    by_lane = (((1,), (1,)), ((), ()))
    cols = lax.dot_general(low.astype(F32).astype(BF16), pick, by_lane, preferred_element_type=F32)
    cols = cols + lax.dot_general((col - low).astype(F32).astype(BF16), pick, by_lane, preferred_element_type=F32)
    for o in range(NGY):
        send_ref[o * CHUNK:o * CHUNK + CAP, :] = sent[o * CAP:(o + 1) * CAP, :]
        crow = cols[:, o * CAP:(o + 1) * CAP]
        send_ref[o * CHUNK + CAP:(o + 1) * CHUNK, :] = jnp.concatenate([crow, crow], axis=1)
    for copy in copies[3:]:
        copy.wait()
    even_x, even_y = even("gx"), even("gy")
    for x in range(CX):
        ya[x:x + 1, :], yb[x:x + 1, :] = split(t_lo[x, 0:1, :], t_hi[x, YT - 1:YT, :], even_y)
        s_a, s_b = split(s_lo[x, 0:1, :], s_hi[x, YT - 1:YT, :], even_y)
        ya[CX + x:CX + x + 1, :] = s_a.astype(F32)
        yb[CX + x:CX + x + 1, :] = s_b.astype(F32)
    xa[0:CY, :], xb[0:CY, :] = split(tx[0], tx[1], even_x)
    s_a, s_b = split(sx[0], sx[1], even_x)
    xa[CY:, :] = s_a.astype(F32)
    xb[CY:, :] = s_b.astype(F32)


def add_source(recv_ref, inj, out_ref):
    lane = lax.broadcasted_iota(jnp.int32, (1, 2 * CAP), 1)
    cell = lax.broadcasted_iota(jnp.int32, (CX * CY, 2 * CAP), 0)
    pick, loss = [], []
    for g in range(0, NGY, 2):
        a, b = g * CHUNK, (g + 1) * CHUNK
        crow = jnp.where(lane < CAP, recv_ref[a + CAP:a + CAP + 1, :], recv_ref[b + CAP:b + CAP + 1, :])
        pick.append((cell == crow.astype(jnp.int32)).astype(F32).astype(BF16))
        loss += [recv_ref[a:a + CAP, :], recv_ref[b:b + CAP, :]]
    pick = jnp.concatenate(pick, axis=1)
    loss = jnp.concatenate(loss, axis=0)
    gathered = jnp.zeros((CX * CY, LW), F32)
    for _ in range(3):
        part = loss.astype(BF16)
        loss = loss - part.astype(F32)
        gathered = gathered + jnp.dot(pick, part, preferred_element_type=F32)
    high = gathered.astype(BF16)
    low = (gathered - high.astype(F32)).astype(BF16)
    left = jnp.concatenate([high, low, high], axis=1)
    width = 256
    for n in range(0, NZ, width):
        cut = slice(n, n + width)
        both = inj[:, cut]
        top = both.astype(BF16)
        right = jnp.concatenate([top, top, (both - top.astype(F32)).astype(BF16)], axis=0)
        out_ref[:, :, cut] = jnp.dot(left, right, preferred_element_type=F32).reshape(CX, CY, width)


def tile_sides(ref, x, yt):
    mid = ref[x, yt * YT:(yt + 1) * YT, :]
    row = lax.broadcasted_iota(jnp.int32, (YT, NZ), 0)
    up, down = pltpu.roll(mid, YT - 1, 0), pltpu.roll(mid, 1, 0)
    if yt < NT - 1:
        up = jnp.where(row == YT - 1, ref[x, (yt + 1) * YT:(yt + 1) * YT + 1, :], up)
    if yt > 0:
        down = jnp.where(row == 0, ref[x, yt * YT - 1:yt * YT, :], down)
    return mid, up, down


def coef_kernel(table_ref, hya, hyb, t_hbm, cap_hbm, soil_hbm, *refs):
    outs, (more_ref, halo_ref, ex_ref, ey_ref, half_ref, t_ref, cap, soil), made, (in_sems, out_sems) = (
        refs[:6], refs[6:14], refs[14:20], refs[20:])
    fx_ref, fy_ref, fz_ref, rhs_ref, tn_ref, w_ref = made
    step = CX // PARTS
    spans = [pl.ds(part * step, step) for part in range(PARTS)]
    copies = []
    for k, (src, dst) in enumerate(((soil_hbm, soil), (t_hbm, t_ref), (cap_hbm, cap))):
        copies.append([pltpu.make_async_copy(src.at[span], dst.at[span], in_sems.at[k, part]) for part, span in enumerate(spans)])
        for copy in copies[k]:
            copy.start()
    table = [0.5 * table_ref[k] for k in range(NCLS)]
    gy = lax.axis_index("gy")
    halo = split(hya[...], hyb[...], even("gy"))
    for k, inside in enumerate((gy > 0, gy < NGY - 1)):
        more_ref[k] = lookup(halo[k][CX:].astype(jnp.int32), table) * jnp.where(inside, F32(1.0), F32(0.0))
        halo_ref[k] = halo[k][0:CX]

    def fill(x, carry):
        half_ref[x] = lookup(soil[x], table)
        return carry

    for part in range(PARTS):
        copies[0][part].wait()
        lax.fori_loop(part * step, (part + 1) * step, fill, 0)
    for part in range(PARTS):
        copies[1][part].wait()
        copies[2][part].wait()
    for side, x in enumerate((0, CX - 1)):
        ex_ref[side, 0] = half_ref[x]
        ex_ref[side, 1] = t_ref[x]
    row = lax.broadcasted_iota(jnp.int32, (YT, NZ), 0)
    lane = lax.broadcasted_iota(jnp.int32, (YT, NZ), 1)
    at_end = lane == NZ - 1
    at_ends = jnp.logical_or(at_end, lane == 0)

    def plane(x, first, last):
        for yt in range(NT):
            rows = slice(yt * YT, (yt + 1) * YT)
            low, high = yt == 0, yt == NT - 1
            c, cyp, cym = tile_sides(half_ref, x, yt)
            t, typ, tym = tile_sides(t_ref, x, yt)
            fyp, fym = c + cyp, c + cym
            fz = jnp.where(at_end, F32(0.0), c + pltpu.roll(c, NZ - 1, 1))
            cp = cap[x, rows, :]
            diag = cp + fz + pltpu.roll(fz, 1, 1) + jnp.where(at_ends, c, F32(0.0))
            if high:
                diag = diag + jnp.where(row == YT - 1, c, fyp)
                fyp = jnp.where(row == YT - 1, F32(0.0), fyp)
            else:
                diag = diag + fyp
            if low:
                diag = diag + jnp.where(row == 0, c, fym)
                fym = jnp.where(row == 0, F32(0.0), fym)
            else:
                diag = diag + fym
            rhs = cp * t
            total = rhs + fyp * typ + fym * tym
            if last:
                diag = diag + c
            else:
                fxp = c + half_ref[x + 1, rows, :]
                diag = diag + fxp
                total = total + fxp * t_ref[x + 1, rows, :]
                fx_ref[x, rows, :] = fxp
            if first:
                diag = diag + c
            else:
                fxm = c + half_ref[x - 1, rows, :]
                diag = diag + fxm
                total = total + fxm * t_ref[x - 1, rows, :]
            total = total + fz * pltpu.roll(t, NZ - 1, 1) + pltpu.roll(fz * t, 1, 1)
            rhs_ref[x, rows, :] = rhs
            fy_ref[x, rows, :] = fyp
            fz_ref[x, rows, :] = fz
            if first or last:
                w_ref[x, rows, :] = diag
                tn_ref[x, rows, :] = total
            else:
                w = 0.8 / diag
                w_ref[x, rows, :] = w
                tn_ref[x, rows, :] = (1.0 - 0.8) * t + w * total
            if low or high:
                at = slice(0, 1) if low else slice(YT - 1, YT)
                side = 0 if low else 1
                for k, value in enumerate((total, diag, c, t)):
                    ey_ref[side, k, pl.ds(x, 1), :] = value[at, :]

    def inner(x, carry):
        plane(x, False, False)
        return carry

    leaving = []
    for part in range(PARTS):
        if part == 0:
            plane(0, True, False)
        lax.fori_loop(max(1, part * step), min(CX - 1, (part + 1) * step), inner, 0)
        if part == PARTS - 1:
            fx_ref[CX - 1] = jnp.zeros((CY, NZ), F32)
            plane(CX - 1, False, True)
        for k in range(6):
            leaving.append(pltpu.make_async_copy(made[k].at[spans[part]], outs[k].at[spans[part]], out_sems.at[k, part]))
            leaving[-1].start()
    for copy in leaving:
        copy.wait()


def source_kernel(recv_ref, inj_hbm, rhs_hbm, tn_hbm, w_hbm, ey_in, rhs_ref, tn_ref, w_ref, ey_ref, source, inj, sems):
    pairs = [(inj_hbm, inj), (rhs_hbm, rhs_ref), (tn_hbm, tn_ref), (w_hbm, w_ref)]
    copies = [pltpu.make_async_copy(src, dst, sems.at[k]) for k, (src, dst) in enumerate(pairs)]
    for copy in copies:
        copy.start()
    copies[0].wait()
    add_source(recv_ref, inj, source)
    copies[1].wait()
    copies[2].wait()
    copies[3].wait()

    def plane(x, edge):
        for yt in range(NT):
            rows = slice(yt * YT, (yt + 1) * YT)
            src = source[x, rows, :]
            rhs_ref[x, rows, :] = rhs_ref[x, rows, :] + src
            tn_ref[x, rows, :] = tn_ref[x, rows, :] + (src if edge else w_ref[x, rows, :] * src)
        for side, y in enumerate((0, CY - 1)):
            ey_ref[side, 0, pl.ds(x, 1), :] = ey_in[side, 0, pl.ds(x, 1), :] + source[x, y:y + 1, :]

    def inner(x, carry):
        plane(x, False)
        return carry

    plane(0, True)
    lax.fori_loop(1, CX - 1, inner, 0)
    plane(CX - 1, True)


def at_row(shape, index, value):
    return jnp.where(lax.broadcasted_iota(jnp.int32, shape, 0) == index, value, F32(0.0))


def with_corners(xlo, xhi, ylo, yhi):
    xs, ys = xlo.shape, ylo.shape
    return (xlo + at_row(xs, 0, ylo[0:1]) + at_row(xs, CY - 1, yhi[0:1]),
            xhi + at_row(xs, 0, ylo[CX - 1:CX]) + at_row(xs, CY - 1, yhi[CX - 1:CX]),
            ylo + at_row(ys, 0, xlo[0:1]) + at_row(ys, CX - 1, xhi[0:1]),
            yhi + at_row(ys, 0, xlo[CY - 1:CY]) + at_row(ys, CX - 1, xhi[CY - 1:CY]))


def fix_kernel(table_ref, hxa, hxb, my_ref, ty_ref, w_ref, tn_ref, ex_ref, ey_ref,
               xa, xb, ya, yb, wx_ref, wy_ref, ax_ref, ay_ref):
    table = [0.5 * table_ref[k] for k in range(NCLS)]
    gx, gy = lax.axis_index("gx"), lax.axis_index("gy")
    within = [jnp.where(q, F32(1.0), F32(0.0)) for q in (gx > 0, gx < NGX - 1, gy > 0, gy < NGY - 1)]
    t_halo = split(hxa[0:CY, :], hxb[0:CY, :], even("gx")) + (ty_ref[0], ty_ref[1])
    klass = split(hxa[CY:, :], hxb[CY:, :], even("gx"))
    more = [lookup(k.astype(jnp.int32), table) * q for k, q in zip(klass, within)] + [my_ref[0], my_ref[1]]
    conds = (ex_ref[0, 0], ex_ref[1, 0], ey_ref[0, 2], ey_ref[1, 2])
    face = [(c + m) * q for c, m, q in zip(conds, more, within)]
    diag = with_corners(*more)
    total = with_corners(*[f * t for f, t in zip(face, t_halo)])
    total = [a + b for a, b in zip(total, (tn_ref[0], tn_ref[CX - 1], ey_ref[0, 0], ey_ref[1, 0]))]
    w = [0.8 / (a + b) for a, b in zip(diag, (w_ref[0], w_ref[CX - 1], ey_ref[0, 1], ey_ref[1, 1]))]
    old = (ex_ref[0, 1], ex_ref[1, 1], ey_ref[0, 3], ey_ref[1, 3])
    new = [(1.0 - 0.8) * t + a * b for t, a, b in zip(old, w, total)]
    xa[...], xb[...] = split(new[0], new[1], even("gx"))
    ya[...], yb[...] = split(new[2], new[3], even("gy"))
    for k in range(2):
        wx_ref[k], wy_ref[k] = w[k], w[2 + k]
        ax_ref[k], ay_ref[k] = w[k] * face[k], w[2 + k] * face[2 + k]


def y_term_kernel(ay_ref, hya, hyb, gy_ref):
    lo, hi = split(hya[...], hyb[...], even("gy"))
    gy_ref[0] = ay_ref[0] * lo
    gy_ref[1] = ay_ref[1] * hi


def faces_of(tn_ref, py_ref, ax_ref, gy_ref, hxa, hxb):
    lo, hi = split(hxa[...], hxb[...], even("gx"))
    terms = with_corners(ax_ref[0] * lo, ax_ref[1] * hi, gy_ref[0], gy_ref[1])
    return [a + b for a, b in zip(terms, (tn_ref[0], tn_ref[CX - 1], py_ref[0], py_ref[1]))]


def edge_kernel(tn_ref, py_ref, ax_ref, gy_ref, hxa, hxb, xa, xb, ya, yb):
    new = faces_of(tn_ref, py_ref, ax_ref, gy_ref, hxa, hxb)
    xa[...], xb[...] = split(new[0], new[1], even("gx"))
    ya[...], yb[...] = split(new[2], new[3], even("gy"))


def put_edges(ref, xlo, xhi, ylo, yhi):
    ref[0] = xlo
    ref[CX - 1] = xhi
    for x in range(1, CX - 1):
        ref[x, 0:1, :] = ylo[x:x + 1]
        ref[x, CY - 1:CY, :] = yhi[x:x + 1]


def sweep_plane(x, first, last, t_ref, fx_ref, fy_ref, fz_ref, w_ref, rhs_ref, tn_ref, py_ref):
    row = lax.broadcasted_iota(jnp.int32, (YT, NZ), 0)
    for yt in range(NT):
        rows = slice(yt * YT, (yt + 1) * YT)
        t, typ, tym = tile_sides(t_ref, x, yt)
        fy, _, fym = tile_sides(fy_ref, x, yt)
        if yt == 0:
            fym = jnp.where(row == 0, F32(0.0), fym)
        fz = fz_ref[x, rows, :]
        total = rhs_ref[x, rows, :] + fy * typ + fym * tym
        if not last:
            total = total + fx_ref[x, rows, :] * t_ref[x + 1, rows, :]
        if not first:
            total = total + fx_ref[x - 1, rows, :] * t_ref[x - 1, rows, :]
        total = total + fz * pltpu.roll(t, NZ - 1, 1)
        total = total + pltpu.roll(fz * t, 1, 1)
        tn = (1.0 - 0.8) * t + w_ref[x, rows, :] * total
        tn_ref[x, rows, :] = tn
        if yt == 0:
            py_ref[0, pl.ds(x, 1), :] = tn[0:1, :]
        if yt == NT - 1:
            py_ref[1, pl.ds(x, 1), :] = tn[YT - 1:YT, :]


def sweep_inside(refs, start=1, stop=CX - 1):
    def inner(x, carry):
        sweep_plane(x, False, False, *refs)
        return carry

    lax.fori_loop(start, stop, inner, 0)


def first_sweep_kernel(fx_hbm, fy_hbm, fz_hbm, rhs_ref, xa, xb, ya, yb, wx_ref, wy_ref, w_in, t_in,
                       w_ref, t_ref, tn_ref, py_ref, fx_ref, fy_ref, fz_ref, sems):
    step = CX // PARTS
    pairs = ((fx_hbm, fx_ref), (fy_hbm, fy_ref), (fz_hbm, fz_ref))
    copies = [[pltpu.make_async_copy(src.at[pl.ds(part * step, step)], dst.at[pl.ds(part * step, step)], sems.at[k, part])
               for k, (src, dst) in enumerate(pairs)] for part in range(PARTS)]
    for part in range(PARTS):
        for copy in copies[part]:
            copy.start()
    put_edges(w_ref, wx_ref[0], wx_ref[1], wy_ref[0], wy_ref[1])
    put_edges(t_ref, *split(xa[...], xb[...], even("gx")), *split(ya[...], yb[...], even("gy")))
    refs = (t_ref, fx_ref, fy_ref, fz_ref, w_ref, rhs_ref, tn_ref, py_ref)
    for part in range(PARTS):
        for copy in copies[part]:
            copy.wait()
        if part == 0:
            sweep_plane(0, True, False, *refs)
        sweep_inside(refs, max(1, part * step), min(CX - 1, (part + 1) * step))
    sweep_plane(CX - 1, False, True, *refs)


def sweep(fx_ref, fy_ref, fz_ref, rhs_ref, w_ref, xa, xb, ya, yb, t_ref, tn_ref, py_ref):
    put_edges(t_ref, *split(xa[...], xb[...], even("gx")), *split(ya[...], yb[...], even("gy")))
    refs = (t_ref, fx_ref, fy_ref, fz_ref, w_ref, rhs_ref, tn_ref, py_ref)
    sweep_plane(0, True, False, *refs)
    sweep_inside(refs)
    sweep_plane(CX - 1, False, True, *refs)


def sweep_kernel(fx_ref, fy_ref, fz_ref, rhs_ref, w_ref, xa, xb, ya, yb, t_in, t_ref, tn_ref, py_ref):
    sweep(fx_ref, fy_ref, fz_ref, rhs_ref, w_ref, xa, xb, ya, yb, t_ref, tn_ref, py_ref)


def last_sweep_kernel(fx_ref, fy_ref, fz_ref, rhs_ref, w_ref, xa, xb, ya, yb, t_in, t_ref, tn_ref, py_ref, out_ref, sems):
    put_edges(t_ref, *split(xa[...], xb[...], even("gx")), *split(ya[...], yb[...], even("gy")))
    refs = (t_ref, fx_ref, fy_ref, fz_ref, w_ref, rhs_ref, tn_ref, py_ref)
    bounds = list(range(1, CX - 1, 4)) + [CX - 1]
    copies = []
    for k, (start, stop) in enumerate(zip(bounds[:-1], bounds[1:])):
        sweep_inside(refs, start, stop)
        part = (pl.ds(start, stop - start), pl.ds(YT, CY - 2 * YT))
        copies.append(pltpu.make_async_copy(tn_ref.at[part], out_ref.at[part], sems.at[k]))
        copies[-1].start()
    sweep_plane(0, True, False, *refs)
    sweep_plane(CX - 1, False, True, *refs)
    for copy in copies:
        copy.wait()


def finish_kernel(tn_ref, py_ref, ax_ref, gy_ref, hxa, hxb, out_in, out_ref, x_out, lo_out, hi_out, sems):
    xlo, xhi, ylo, yhi = faces_of(tn_ref, py_ref, ax_ref, gy_ref, hxa, hxb)
    x_out[0] = xlo
    x_out[1] = xhi
    row = lax.broadcasted_iota(jnp.int32, (YT, NZ), 0)
    for x in range(1, CX - 1):
        lo_out[x - 1] = jnp.where(row == 0, ylo[x:x + 1], tn_ref[x, 0:YT, :])
        hi_out[x - 1] = jnp.where(row == YT - 1, yhi[x:x + 1], tn_ref[x, CY - YT:CY, :])
    inside = pl.ds(1, CX - 2)
    load([(x_out.at[0], out_ref.at[0]), (x_out.at[1], out_ref.at[CX - 1]),
          (lo_out, out_ref.at[inside, 0:YT]), (hi_out, out_ref.at[inside, CY - YT:CY])], sems)


def swap(value, partner):
    there = [partner(gx, gy) for gx in range(NGX) for gy in range(NGY)]
    return lax.ppermute(value, ("gx", "gy"), [(i, x * NGY + y) for i, (x, y) in enumerate(there)])


def odd_x(gx, gy):
    if gx in (0, NGX - 1):
        return gx, gy ^ 2
    return (gx + 1 if gx % 2 else gx - 1), gy


def odd_y(gx, gy):
    if gy in (0, NGY - 1):
        return gx ^ 1, gy
    return gx, (gy + 1 if gy % 2 else gy - 1)


def exchange(xa, xb, ya, yb):
    xa, xb = swap(xa, lambda gx, gy: (gx ^ 1, gy)), swap(xb, odd_x)
    ya, yb = swap(ya, lambda gx, gy: (gx, gy ^ 1)), swap(yb, odd_y)
    return near(xa, xb, ya, yb)


def call(kernel, outs, specs, scratch=(), alias={}, mib=1, us=0.1, out_specs=None):
    return pl.pallas_call(
        kernel,
        out_shape=outs,
        in_specs=specs,
        out_specs=out_specs or [VM] * len(outs),
        scratch_shapes=scratch,
        input_output_aliases=alias,
        compiler_params=pltpu.CompilerParams(vmem_limit_bytes=mib * 1024 * 1024),
        cost_estimate=pl.CostEstimate(flops=int(us * 1e9), bytes_accessed=int(us * 3e6), transcendentals=0),
    )


SLAB = local(CX, CY, NZ)
FACES = (local(CY, NZ), local(CY, NZ), local(CX, NZ), local(CX, NZ))
XX, YY = local(2, CY, NZ), local(2, CX, NZ)
DMA = pltpu.SemaphoreType.DMA
I32 = jnp.int32
FIXY, PREP = 20.0, 0.1


def shards(temp_old, capacity, soil_class, cond_table, losses, owner, column, injection):
    rows, rows_int = local(CX, YT, NZ), local(CX, YT, NZ, dtype=I32)
    send, *faces = call(
        start_kernel, (local(NGY * CHUNK, LW),) + (local(2 * CY, NZ),) * 2 + (local(2 * CX, NZ),) * 2, [HB] * 5,
        [rows, rows, rows_int, rows_int, XX, local(2, CY, NZ, dtype=I32), local(SEG, LW), local(1, SEG, dtype=I32),
         local(1, SEG, dtype=I32), DMA((11,))], mib=6)(
        *far(temp_old, soil_class, losses, owner.reshape(1, SEG), column.reshape(1, SEG)))
    recv = lax.all_to_all(send, "gy", 0, 0, tiled=True)
    halo = exchange(*faces)
    hxa, hxb, hya, hyb = halo
    edge_x, edge_y = local(2, 2, CY, NZ), local(2, 4, CX, NZ)
    *stored, my, ty, ex, ey = call(
        coef_kernel, (pltpu.HBM((CX, CY, NZ), F32),) * 6 + (YY, YY, edge_x, edge_y), [SM] + [VM] * 2 + [HB] * 3,
        [SLAB, SLAB, SLAB, local(CX, CY, NZ, dtype=I32)] + [SLAB] * 6 + [DMA((3, PARTS)), DMA((6, PARTS))],
        mib=24, us=FIXY, out_specs=[HB] * 6 + [VM] * 4)(
        cond_table, hya, hyb, *far(temp_old, capacity, soil_class))
    rhs, new, w, ey = call(
        source_kernel, (SLAB,) * 3 + (edge_y,), [VM] + [HB] * 4 + [VM], [SLAB, local(LW, NZ), DMA((4,))],
        alias={5: 3}, mib=8, us=PREP)(*near(recv), *far(injection, *stored[3:]), *near(ey))
    *faces, wx, wy, ax, ay = call(fix_kernel, FACES + (XX, YY, XX, YY), [SM] + [VM] * 8, mib=2)(
        cond_table, hxa, hxb, *near(my, ty, w, new, ex, ey))
    for number in range(1, SWEEPS):
        halo = exchange(*faces)
        if number == 1:
            w, temp, new, py, fx, fy, fz = call(
                first_sweep_kernel, (SLAB, SLAB, SLAB, YY, SLAB, SLAB, SLAB), [HB] * 3 + [VM] * 9, [DMA((3, PARTS))],
                alias={10: 0, 11: 1}, mib=2)(*far(*stored[:3]), *near(rhs, *faces, wx, wy, w, new))
            coefs = near(fx, fy, fz, rhs)
        elif number < SWEEPS - 1:
            temp, new, py = call(sweep_kernel, (SLAB, SLAB, YY), [VM] * 10, alias={9: 0}, mib=2)(
                *coefs, *near(w, *faces, new))
        else:
            temp, new, py, out = call(
                last_sweep_kernel, (SLAB, SLAB, YY, pltpu.HBM((CX, CY, NZ), F32)), [VM] * 10, [DMA((4,))],
                alias={9: 0}, mib=2, out_specs=[VM] * 3 + [HB])(*coefs, *near(w, *faces, new))
        hxa, hxb, hya, hyb = halo
        (gy,) = call(y_term_kernel, (YY,), [VM] * 3, us=8.0)(*near(ay), hya, hyb)
        args = near(new, py, ax, gy) + [hxa, hxb]
        if number < SWEEPS - 1:
            faces = call(edge_kernel, FACES, [VM] * 6, mib=2)(*args)
    return call(finish_kernel, (pltpu.HBM((CX, CY, NZ), F32),), [VM] * 6 + [HB],
                [XX, local(CX - 2, YT, NZ), local(CX - 2, YT, NZ), DMA((4,))], alias={6: 0}, mib=4, out_specs=[HB])(*args, out)[0]


def solution(mesh):
    return jax.shard_map(
        shards,
        mesh=mesh,
        in_specs=(
            P("gx", "gy", None),
            P("gx", "gy", None),
            P("gx", "gy", None),
            P(),
            P(("gx", "gy"), None),
            P(("gx", "gy"), None),
            P(("gx", "gy")),
            P(),
        ),
        out_specs=P("gx", "gy", None),
        check_vma=False,
    )
```

```python
import jax
import jax.numpy as jnp
from jax import lax
from jax.experimental import pallas as pl
from jax.experimental.pallas import tpu as pltpu
from jax.sharding import PartitionSpec as P

SWEEPS = 4
NCLS = 8
CX, CY, NZ = 16, 32, 1024
LW = 128
SEG = 256
CAP = 64
NGX, NGY = 32, 8
CHUNK = CAP + 8
YT = 8
NT = CY // YT
PARTS = 8
F32, BF16 = jnp.float32, jnp.bfloat16
HIGH = lax.Precision.HIGHEST
VM = pl.BlockSpec(memory_space=pltpu.VMEM)
SM = pl.BlockSpec(memory_space=pltpu.SMEM)
HB = pl.BlockSpec(memory_space=pltpu.HBM)


def local(*dims, dtype=F32):
    return pltpu.VMEM(dims, dtype)


def near(*arrays):
    return [pltpu.with_memory_space_constraint(a, pltpu.VMEM) for a in arrays]


def far(*arrays):
    return [pltpu.with_memory_space_constraint(a, pltpu.HBM) for a in arrays]


def lookup(klass, table):
    cond = jnp.where(klass == 0, table[0], F32(0.0))
    for k in range(1, NCLS):
        cond = jnp.where(klass == k, table[k], cond)
    return cond


def load(pairs, sems):
    copies = [pltpu.make_async_copy(src, dst, sems.at[i]) for i, (src, dst) in enumerate(pairs)]
    for copy in copies:
        copy.start()
    for copy in copies:
        copy.wait()


def even(axis):
    return lax.rem(lax.axis_index(axis), 2) == 0


def split(a, b, is_even):
    return jnp.where(is_even, b, a), jnp.where(is_even, a, b)


def start_kernel(t_hbm, soil_hbm, loss_hbm, owner_hbm, col_hbm, send_ref, xa, xb, ya, yb,
                 t_lo, t_hi, s_lo, s_hi, tx, sx, loss_ref, owner_ref, col_ref, sems):
    pairs = [(loss_hbm, loss_ref), (owner_hbm, owner_ref), (col_hbm, col_ref),
             (t_hbm.at[:, 0:YT], t_lo), (t_hbm.at[:, CY - YT:CY], t_hi),
             (soil_hbm.at[:, 0:YT], s_lo), (soil_hbm.at[:, CY - YT:CY], s_hi),
             (t_hbm.at[0], tx.at[0]), (t_hbm.at[CX - 1], tx.at[1]),
             (soil_hbm.at[0], sx.at[0]), (soil_hbm.at[CX - 1], sx.at[1])]
    copies = [pltpu.make_async_copy(src, dst, sems.at[i]) for i, (src, dst) in enumerate(pairs)]
    for copy in copies:
        copy.start()
    for copy in copies[:3]:
        copy.wait()
    own = owner_ref[...]
    mine = lax.broadcasted_iota(jnp.int32, (NGY, SEG), 0) == own
    before = lax.broadcasted_iota(jnp.int32, (SEG, SEG), 0) < lax.broadcasted_iota(jnp.int32, (SEG, SEG), 1)
    count = jnp.dot(mine.astype(F32).astype(BF16), before.astype(F32).astype(BF16), preferred_element_type=F32)
    rank = jnp.sum(jnp.where(mine, count, 0.0), axis=0, keepdims=True).astype(jnp.int32)
    slot = own * CAP + rank
    pick = (lax.broadcasted_iota(jnp.int32, (NGY * CAP, SEG), 0) == slot).astype(F32).astype(BF16)
    loss = loss_ref[...]
    sent = jnp.zeros((NGY * CAP, LW), F32)
    for _ in range(3):
        part = loss.astype(BF16)
        loss = loss - part.astype(F32)
        sent = sent + jnp.dot(pick, part, preferred_element_type=F32)
    col = jnp.broadcast_to(col_ref[...], (8, SEG))
    low = lax.rem(col, 128)
    by_lane = (((1,), (1,)), ((), ()))
    cols = lax.dot_general(low.astype(F32).astype(BF16), pick, by_lane, preferred_element_type=F32)
    cols = cols + lax.dot_general((col - low).astype(F32).astype(BF16), pick, by_lane, preferred_element_type=F32)
    for o in range(NGY):
        send_ref[o * CHUNK:o * CHUNK + CAP, :] = sent[o * CAP:(o + 1) * CAP, :]
        crow = cols[:, o * CAP:(o + 1) * CAP]
        send_ref[o * CHUNK + CAP:(o + 1) * CHUNK, :] = jnp.concatenate([crow, crow], axis=1)
    for copy in copies[3:]:
        copy.wait()
    even_x, even_y = even("gx"), even("gy")
    for x in range(CX):
        ya[x:x + 1, :], yb[x:x + 1, :] = split(t_lo[x, 0:1, :], t_hi[x, YT - 1:YT, :], even_y)
        s_a, s_b = split(s_lo[x, 0:1, :], s_hi[x, YT - 1:YT, :], even_y)
        ya[CX + x:CX + x + 1, :] = s_a.astype(F32)
        yb[CX + x:CX + x + 1, :] = s_b.astype(F32)
    xa[0:CY, :], xb[0:CY, :] = split(tx[0], tx[1], even_x)
    s_a, s_b = split(sx[0], sx[1], even_x)
    xa[CY:, :] = s_a.astype(F32)
    xb[CY:, :] = s_b.astype(F32)


def add_source(recv_ref, inj, out_ref):
    lane = lax.broadcasted_iota(jnp.int32, (1, 2 * CAP), 1)
    cell = lax.broadcasted_iota(jnp.int32, (CX * CY, 2 * CAP), 0)
    pick, loss = [], []
    for g in range(0, NGY, 2):
        a, b = g * CHUNK, (g + 1) * CHUNK
        crow = jnp.where(lane < CAP, recv_ref[a + CAP:a + CAP + 1, :], recv_ref[b + CAP:b + CAP + 1, :])
        pick.append((cell == crow.astype(jnp.int32)).astype(F32).astype(BF16))
        loss += [recv_ref[a:a + CAP, :], recv_ref[b:b + CAP, :]]
    pick = jnp.concatenate(pick, axis=1)
    loss = jnp.concatenate(loss, axis=0)
    gathered = jnp.zeros((CX * CY, LW), F32)
    for _ in range(3):
        part = loss.astype(BF16)
        loss = loss - part.astype(F32)
        gathered = gathered + jnp.dot(pick, part, preferred_element_type=F32)
    high = gathered.astype(BF16)
    low = (gathered - high.astype(F32)).astype(BF16)
    left = jnp.concatenate([high, low, high], axis=1)
    width = 256
    for n in range(0, NZ, width):
        cut = slice(n, n + width)
        both = inj[:, cut]
        top = both.astype(BF16)
        right = jnp.concatenate([top, top, (both - top.astype(F32)).astype(BF16)], axis=0)
        out_ref[:, :, cut] = jnp.dot(left, right, preferred_element_type=F32).reshape(CX, CY, width)


def tile_sides(ref, x, yt):
    mid = ref[x, yt * YT:(yt + 1) * YT, :]
    row = lax.broadcasted_iota(jnp.int32, (YT, NZ), 0)
    up, down = pltpu.roll(mid, YT - 1, 0), pltpu.roll(mid, 1, 0)
    if yt < NT - 1:
        up = jnp.where(row == YT - 1, ref[x, (yt + 1) * YT:(yt + 1) * YT + 1, :], up)
    if yt > 0:
        down = jnp.where(row == 0, ref[x, yt * YT - 1:yt * YT, :], down)
    return mid, up, down


def coef_kernel(table_ref, hyb, hya, t_hbm, cap_hbm, soil_hbm, *refs):
    outs, (more_ref, halo_ref, ex_ref, ey_ref, half_ref, t_ref, cap, soil), made, (in_sems, out_sems) = (
        refs[:6], refs[6:14], refs[14:20], refs[20:])
    fx_ref, fy_ref, fz_ref, rhs_ref, tn_ref, w_ref = made
    step = CX // PARTS
    spans = [pl.ds(part * step, step) for part in range(PARTS)]
    copies = []
    for k, (src, dst) in enumerate(((soil_hbm, soil), (t_hbm, t_ref), (cap_hbm, cap))):
        copies.append([pltpu.make_async_copy(src.at[span], dst.at[span], in_sems.at[k, part]) for part, span in enumerate(spans)])
        for copy in copies[k]:
            copy.start()
    table = [0.5 * table_ref[k] for k in range(NCLS)]
    gy = lax.axis_index("gy")
    halo = split(hya[...], hyb[...], even("gy"))
    for k, inside in enumerate((gy > 0, gy < NGY - 1)):
        more_ref[k] = lookup(halo[k][CX:].astype(jnp.int32), table) * jnp.where(inside, F32(1.0), F32(0.0))
        halo_ref[k] = halo[k][0:CX]

    def fill(x, carry):
        half_ref[x] = lookup(soil[x], table)
        return carry

    for part in range(PARTS):
        copies[0][part].wait()
        lax.fori_loop(part * step, (part + 1) * step, fill, 0)
    for part in range(PARTS):
        copies[1][part].wait()
        copies[2][part].wait()
    for side, x in enumerate((0, CX - 1)):
        ex_ref[side, 0] = half_ref[x]
        ex_ref[side, 1] = t_ref[x]
    row = lax.broadcasted_iota(jnp.int32, (YT, NZ), 0)
    lane = lax.broadcasted_iota(jnp.int32, (YT, NZ), 1)
    at_end = lane == NZ - 1
    at_ends = jnp.logical_or(at_end, lane == 0)

    def plane(x, first, last):
        for yt in range(NT):
            rows = slice(yt * YT, (yt + 1) * YT)
            low, high = yt == 0, yt == NT - 1
            c, cyp, cym = tile_sides(half_ref, x, yt)
            t, typ, tym = tile_sides(t_ref, x, yt)
            fyp, fym = c + cyp, c + cym
            fz = jnp.where(at_end, F32(0.0), c + pltpu.roll(c, NZ - 1, 1))
            cp = cap[x, rows, :]
            diag = cp + fz + pltpu.roll(fz, 1, 1) + jnp.where(at_ends, c, F32(0.0))
            if high:
                diag = diag + jnp.where(row == YT - 1, c, fyp)
                fyp = jnp.where(row == YT - 1, F32(0.0), fyp)
            else:
                diag = diag + fyp
            if low:
                diag = diag + jnp.where(row == 0, c, fym)
                fym = jnp.where(row == 0, F32(0.0), fym)
            else:
                diag = diag + fym
            rhs = cp * t
            total = rhs + fyp * typ + fym * tym
            if last:
                diag = diag + c
            else:
                fxp = c + half_ref[x + 1, rows, :]
                diag = diag + fxp
                total = total + fxp * t_ref[x + 1, rows, :]
                fx_ref[x, rows, :] = fxp
            if first:
                diag = diag + c
            else:
                fxm = c + half_ref[x - 1, rows, :]
                diag = diag + fxm
                total = total + fxm * t_ref[x - 1, rows, :]
            total = total + fz * pltpu.roll(t, NZ - 1, 1) + pltpu.roll(fz * t, 1, 1)
            rhs_ref[x, rows, :] = rhs
            fy_ref[x, rows, :] = fyp
            fz_ref[x, rows, :] = fz
            if first or last:
                w_ref[x, rows, :] = diag
                tn_ref[x, rows, :] = total
            else:
                w = 0.8 / diag
                w_ref[x, rows, :] = w
                tn_ref[x, rows, :] = (1.0 - 0.8) * t + w * total
            if low or high:
                at = slice(0, 1) if low else slice(YT - 1, YT)
                side = 0 if low else 1
                for k, value in enumerate((total, diag, c, t)):
                    ey_ref[side, k, pl.ds(x, 1), :] = value[at, :]

    def inner(x, carry):
        plane(x, False, False)
        return carry

    leaving = []
    for part in range(PARTS):
        if part == 0:
            plane(0, True, False)
        lax.fori_loop(max(1, part * step), min(CX - 1, (part + 1) * step), inner, 0)
        if part == PARTS - 1:
            fx_ref[CX - 1] = jnp.zeros((CY, NZ), F32)
            plane(CX - 1, False, True)
        for k in range(6):
            leaving.append(pltpu.make_async_copy(made[k].at[spans[part]], outs[k].at[spans[part]], out_sems.at[k, part]))
            leaving[-1].start()
    for copy in leaving:
        copy.wait()


def source_kernel(recv_ref, inj_ref, rhs_hbm, tn_hbm, w_hbm, ey_in, rhs_ref, tn_ref, w_ref, ey_ref, source, sems):
    step = CX // 4
    pairs = ((rhs_hbm, rhs_ref), (w_hbm, w_ref), (tn_hbm, tn_ref))
    copies = [[pltpu.make_async_copy(src.at[pl.ds(part * step, step)], dst.at[pl.ds(part * step, step)], sems.at[k, part])
               for k, (src, dst) in enumerate(pairs)] for part in range(4)]
    for part in copies:
        for copy in part:
            copy.start()
    add_source(recv_ref, inj_ref, source)

    def plane(x, edge):
        for yt in range(NT):
            rows = slice(yt * YT, (yt + 1) * YT)
            src = source[x, rows, :]
            rhs_ref[x, rows, :] = rhs_ref[x, rows, :] + src
            tn_ref[x, rows, :] = tn_ref[x, rows, :] + (src if edge else w_ref[x, rows, :] * src)
        for side, y in enumerate((0, CY - 1)):
            ey_ref[side, 0, pl.ds(x, 1), :] = ey_in[side, 0, pl.ds(x, 1), :] + source[x, y:y + 1, :]

    def inner(x, carry):
        plane(x, False)
        return carry

    for part in range(4):
        for copy in copies[part]:
            copy.wait()
        if part == 0:
            plane(0, True)
        lax.fori_loop(max(1, part * step), min(CX - 1, (part + 1) * step), inner, 0)
    plane(CX - 1, True)


def at_row(shape, index, value):
    return jnp.where(lax.broadcasted_iota(jnp.int32, shape, 0) == index, value, F32(0.0))


def with_corners(xlo, xhi, ylo, yhi):
    xs, ys = xlo.shape, ylo.shape
    return (xlo + at_row(xs, 0, ylo[0:1]) + at_row(xs, CY - 1, yhi[0:1]),
            xhi + at_row(xs, 0, ylo[CX - 1:CX]) + at_row(xs, CY - 1, yhi[CX - 1:CX]),
            ylo + at_row(ys, 0, xlo[0:1]) + at_row(ys, CX - 1, xhi[0:1]),
            yhi + at_row(ys, 0, xlo[CY - 1:CY]) + at_row(ys, CX - 1, xhi[CY - 1:CY]))


def fix_kernel(table_ref, hxb, hxa, my_ref, ty_ref, w_ref, tn_ref, ex_ref, ey_ref,
               xa, xb, ya, yb, wx_ref, wy_ref, ax_ref, ay_ref):
    table = [0.5 * table_ref[k] for k in range(NCLS)]
    gx, gy = lax.axis_index("gx"), lax.axis_index("gy")
    within = [jnp.where(q, F32(1.0), F32(0.0)) for q in (gx > 0, gx < NGX - 1, gy > 0, gy < NGY - 1)]
    t_halo = split(hxa[0:CY, :], hxb[0:CY, :], even("gx")) + (ty_ref[0], ty_ref[1])
    klass = split(hxa[CY:, :], hxb[CY:, :], even("gx"))
    more = [lookup(k.astype(jnp.int32), table) * q for k, q in zip(klass, within)] + [my_ref[0], my_ref[1]]
    conds = (ex_ref[0, 0], ex_ref[1, 0], ey_ref[0, 2], ey_ref[1, 2])
    face = [(c + m) * q for c, m, q in zip(conds, more, within)]
    diag = with_corners(*more)
    total = with_corners(*[f * t for f, t in zip(face, t_halo)])
    total = [a + b for a, b in zip(total, (tn_ref[0], tn_ref[CX - 1], ey_ref[0, 0], ey_ref[1, 0]))]
    w = [0.8 / (a + b) for a, b in zip(diag, (w_ref[0], w_ref[CX - 1], ey_ref[0, 1], ey_ref[1, 1]))]
    old = (ex_ref[0, 1], ex_ref[1, 1], ey_ref[0, 3], ey_ref[1, 3])
    new = [(1.0 - 0.8) * t + a * b for t, a, b in zip(old, w, total)]
    xa[...], xb[...] = split(new[0], new[1], even("gx"))
    ya[...], yb[...] = split(new[2], new[3], even("gy"))
    for k in range(2):
        wx_ref[k], wy_ref[k] = w[k], w[2 + k]
        ax_ref[k], ay_ref[k] = w[k] * face[k], w[2 + k] * face[2 + k]


def y_term_kernel(ay_ref, hyb, hya, gy_ref):
    lo, hi = split(hya[...], hyb[...], even("gy"))
    gy_ref[0] = ay_ref[0] * lo
    gy_ref[1] = ay_ref[1] * hi


def faces_of(tn_ref, py_ref, ax_ref, gy_ref, hxb, hxa):
    lo, hi = split(hxa[...], hxb[...], even("gx"))
    terms = with_corners(ax_ref[0] * lo, ax_ref[1] * hi, gy_ref[0], gy_ref[1])
    return [a + b for a, b in zip(terms, (tn_ref[0], tn_ref[CX - 1], py_ref[0], py_ref[1]))]


def edge_kernel(tn_ref, py_ref, ax_ref, gy_ref, hxb, hxa, xa, xb, ya, yb):
    new = faces_of(tn_ref, py_ref, ax_ref, gy_ref, hxb, hxa)
    xa[...], xb[...] = split(new[0], new[1], even("gx"))
    ya[...], yb[...] = split(new[2], new[3], even("gy"))


def put_edges(ref, xlo, xhi, ylo, yhi):
    ref[0] = xlo
    ref[CX - 1] = xhi
    for x in range(1, CX - 1):
        ref[x, 0:1, :] = ylo[x:x + 1]
        ref[x, CY - 1:CY, :] = yhi[x:x + 1]


def sweep_plane(x, first, last, t_ref, fx_ref, fy_ref, fz_ref, w_ref, rhs_ref, tn_ref, py_ref):
    row = lax.broadcasted_iota(jnp.int32, (YT, NZ), 0)
    for yt in range(NT):
        rows = slice(yt * YT, (yt + 1) * YT)
        t, typ, tym = tile_sides(t_ref, x, yt)
        fy, _, fym = tile_sides(fy_ref, x, yt)
        if yt == 0:
            fym = jnp.where(row == 0, F32(0.0), fym)
        fz = fz_ref[x, rows, :]
        total = rhs_ref[x, rows, :] + fy * typ + fym * tym
        if not last:
            total = total + fx_ref[x, rows, :] * t_ref[x + 1, rows, :]
        if not first:
            total = total + fx_ref[x - 1, rows, :] * t_ref[x - 1, rows, :]
        total = total + fz * pltpu.roll(t, NZ - 1, 1)
        total = total + pltpu.roll(fz * t, 1, 1)
        tn = (1.0 - 0.8) * t + w_ref[x, rows, :] * total
        tn_ref[x, rows, :] = tn
        if yt == 0:
            py_ref[0, pl.ds(x, 1), :] = tn[0:1, :]
        if yt == NT - 1:
            py_ref[1, pl.ds(x, 1), :] = tn[YT - 1:YT, :]


def sweep_inside(refs, start=1, stop=CX - 1):
    def inner(x, carry):
        sweep_plane(x, False, False, *refs)
        return carry

    lax.fori_loop(start, stop, inner, 0)


def first_sweep_kernel(fx_hbm, fy_hbm, fz_hbm, rhs_ref, xa, xb, ya, yb, wx_ref, wy_ref, w_in, t_in,
                       w_ref, t_ref, tn_ref, py_ref, fx_ref, fy_ref, fz_ref, sems):
    step = CX // PARTS
    pairs = ((fx_hbm, fx_ref), (fy_hbm, fy_ref), (fz_hbm, fz_ref))
    copies = [[pltpu.make_async_copy(src.at[pl.ds(part * step, step)], dst.at[pl.ds(part * step, step)], sems.at[k, part])
               for k, (src, dst) in enumerate(pairs)] for part in range(PARTS)]
    for part in range(PARTS):
        for copy in copies[part]:
            copy.start()
    put_edges(w_ref, wx_ref[0], wx_ref[1], wy_ref[0], wy_ref[1])
    put_edges(t_ref, *split(xa[...], xb[...], even("gx")), *split(ya[...], yb[...], even("gy")))
    refs = (t_ref, fx_ref, fy_ref, fz_ref, w_ref, rhs_ref, tn_ref, py_ref)
    for part in range(PARTS):
        for copy in copies[part]:
            copy.wait()
        if part == 0:
            sweep_plane(0, True, False, *refs)
        sweep_inside(refs, max(1, part * step), min(CX - 1, (part + 1) * step))
    sweep_plane(CX - 1, False, True, *refs)


def sweep(fx_ref, fy_ref, fz_ref, rhs_ref, w_ref, xa, xb, ya, yb, t_ref, tn_ref, py_ref):
    put_edges(t_ref, *split(xa[...], xb[...], even("gx")), *split(ya[...], yb[...], even("gy")))
    refs = (t_ref, fx_ref, fy_ref, fz_ref, w_ref, rhs_ref, tn_ref, py_ref)
    sweep_plane(0, True, False, *refs)
    sweep_inside(refs)
    sweep_plane(CX - 1, False, True, *refs)


def sweep_kernel(fx_ref, fy_ref, fz_ref, rhs_ref, w_ref, xa, xb, ya, yb, t_in, t_ref, tn_ref, py_ref):
    sweep(fx_ref, fy_ref, fz_ref, rhs_ref, w_ref, xa, xb, ya, yb, t_ref, tn_ref, py_ref)


def last_sweep_kernel(fx_ref, fy_ref, fz_ref, rhs_ref, w_ref, xa, xb, ya, yb, t_in, t_ref, tn_ref, py_ref, out_ref, sems):
    put_edges(t_ref, *split(xa[...], xb[...], even("gx")), *split(ya[...], yb[...], even("gy")))
    refs = (t_ref, fx_ref, fy_ref, fz_ref, w_ref, rhs_ref, tn_ref, py_ref)
    bounds = list(range(1, CX - 1, 4)) + [CX - 1]
    copies = []
    for k, (start, stop) in enumerate(zip(bounds[:-1], bounds[1:])):
        sweep_inside(refs, start, stop)
        part = (pl.ds(start, stop - start), pl.ds(YT, CY - 2 * YT))
        copies.append(pltpu.make_async_copy(tn_ref.at[part], out_ref.at[part], sems.at[k]))
        copies[-1].start()
    sweep_plane(0, True, False, *refs)
    sweep_plane(CX - 1, False, True, *refs)
    for copy in copies:
        copy.wait()


def finish_kernel(tn_ref, py_ref, ax_ref, gy_ref, hxb, hxa, out_in, out_ref, x_out, lo_out, hi_out, sems):
    xlo, xhi, ylo, yhi = faces_of(tn_ref, py_ref, ax_ref, gy_ref, hxb, hxa)
    x_out[0] = xlo
    x_out[1] = xhi
    row = lax.broadcasted_iota(jnp.int32, (YT, NZ), 0)
    for x in range(1, CX - 1):
        lo_out[x - 1] = jnp.where(row == 0, ylo[x:x + 1], tn_ref[x, 0:YT, :])
        hi_out[x - 1] = jnp.where(row == YT - 1, yhi[x:x + 1], tn_ref[x, CY - YT:CY, :])
    inside = pl.ds(1, CX - 2)
    load([(x_out.at[0], out_ref.at[0]), (x_out.at[1], out_ref.at[CX - 1]),
          (lo_out, out_ref.at[inside, 0:YT]), (hi_out, out_ref.at[inside, CY - YT:CY])], sems)


def swap(value, partner):
    there = [partner(gx, gy) for gx in range(NGX) for gy in range(NGY)]
    return lax.ppermute(value, ("gx", "gy"), [(i, x * NGY + y) for i, (x, y) in enumerate(there)])


def odd_x(gx, gy):
    if gx in (0, NGX - 1):
        return gx, gy ^ 2
    return (gx + 1 if gx % 2 else gx - 1), gy


def odd_y(gx, gy):
    if gy in (0, NGY - 1):
        return gx ^ 1, gy
    return gx, (gy + 1 if gy % 2 else gy - 1)


def exchange(xa, xb, ya, yb):
    xb, xa = swap(xb, odd_x), swap(xa, lambda gx, gy: (gx ^ 1, gy))
    yb, ya = swap(yb, odd_y), swap(ya, lambda gx, gy: (gx, gy ^ 1))
    return near(xa, xb, ya, yb)


def call(kernel, outs, specs, scratch=(), alias={}, mib=1, us=0.1, out_specs=None):
    return pl.pallas_call(
        kernel,
        out_shape=outs,
        in_specs=specs,
        out_specs=out_specs or [VM] * len(outs),
        scratch_shapes=scratch,
        input_output_aliases=alias,
        compiler_params=pltpu.CompilerParams(vmem_limit_bytes=mib * 1024 * 1024),
        cost_estimate=pl.CostEstimate(flops=int(us * 1e9), bytes_accessed=int(us * 3e6), transcendentals=0),
    )


SLAB = local(CX, CY, NZ)
FACES = (local(CY, NZ), local(CY, NZ), local(CX, NZ), local(CX, NZ))
XX, YY = local(2, CY, NZ), local(2, CX, NZ)
DMA = pltpu.SemaphoreType.DMA
I32 = jnp.int32
FIXY, PREP = 20.0, 0.1


def shards(temp_old, capacity, soil_class, cond_table, losses, owner, column, injection):
    rows, rows_int = local(CX, YT, NZ), local(CX, YT, NZ, dtype=I32)
    send, *faces = call(
        start_kernel, (local(NGY * CHUNK, LW),) + (local(2 * CY, NZ),) * 2 + (local(2 * CX, NZ),) * 2, [HB] * 5,
        [rows, rows, rows_int, rows_int, XX, local(2, CY, NZ, dtype=I32), local(SEG, LW), local(1, SEG, dtype=I32),
         local(1, SEG, dtype=I32), DMA((11,))], mib=6)(
        *far(temp_old, soil_class, losses, owner.reshape(1, SEG), column.reshape(1, SEG)))
    recv = lax.all_to_all(send, "gy", 0, 0, tiled=True)
    halo = exchange(*faces)
    hxa, hxb, hya, hyb = halo
    edge_x, edge_y = local(2, 2, CY, NZ), local(2, 4, CX, NZ)
    *stored, my, ty, ex, ey = call(
        coef_kernel, (pltpu.HBM((CX, CY, NZ), F32),) * 6 + (YY, YY, edge_x, edge_y), [SM] + [VM] * 2 + [HB] * 3,
        [SLAB, SLAB, SLAB, local(CX, CY, NZ, dtype=I32)] + [SLAB] * 6 + [DMA((3, PARTS)), DMA((6, PARTS))],
        mib=24, us=FIXY, out_specs=[HB] * 6 + [VM] * 4)(
        cond_table, hyb, hya, *far(temp_old, capacity, soil_class))
    rhs, new, w, ey = call(
        source_kernel, (SLAB,) * 3 + (edge_y,), [VM] * 2 + [HB] * 3 + [VM], [SLAB, DMA((3, 4))],
        alias={5: 3}, mib=8, us=PREP)(*near(recv, injection), *far(*stored[3:]), *near(ey))
    *faces, wx, wy, ax, ay = call(fix_kernel, FACES + (XX, YY, XX, YY), [SM] + [VM] * 8, mib=2)(
        cond_table, hxb, hxa, *near(my, ty, w, new, ex, ey))
    for number in range(1, SWEEPS):
        halo = exchange(*faces)
        if number == 1:
            w, temp, new, py, fx, fy, fz = call(
                first_sweep_kernel, (SLAB, SLAB, SLAB, YY, SLAB, SLAB, SLAB), [HB] * 3 + [VM] * 9, [DMA((3, PARTS))],
                alias={10: 0, 11: 1}, mib=2)(*far(*stored[:3]), *near(rhs, *faces, wx, wy, w, new))
            coefs = near(fx, fy, fz, rhs)
        elif number < SWEEPS - 1:
            temp, new, py = call(sweep_kernel, (SLAB, SLAB, YY), [VM] * 10, alias={9: 0}, mib=2)(
                *coefs, *near(w, *faces, new))
        else:
            temp, new, py, out = call(
                last_sweep_kernel, (SLAB, SLAB, YY, pltpu.HBM((CX, CY, NZ), F32)), [VM] * 10, [DMA((4,))],
                alias={9: 0}, mib=2, out_specs=[VM] * 3 + [HB])(*coefs, *near(w, *faces, new))
        hxa, hxb, hya, hyb = halo
        (gy,) = call(y_term_kernel, (YY,), [VM] * 3, us=8.0)(*near(ay), hyb, hya)
        args = near(new, py, ax, gy) + [hxb, hxa]
        if number < SWEEPS - 1:
            faces = call(edge_kernel, FACES, [VM] * 6, mib=2)(*args)
    return call(finish_kernel, (pltpu.HBM((CX, CY, NZ), F32),), [VM] * 6 + [HB],
                [XX, local(CX - 2, YT, NZ), local(CX - 2, YT, NZ), DMA((4,))], alias={6: 0}, mib=4, out_specs=[HB])(*args, out)[0]


def solution(mesh):
    return jax.shard_map(
        shards,
        mesh=mesh,
        in_specs=(
            P("gx", "gy", None),
            P("gx", "gy", None),
            P("gx", "gy", None),
            P(),
            P(("gx", "gy"), None),
            P(("gx", "gy"), None),
            P(("gx", "gy")),
            P(),
        ),
        out_specs=P("gx", "gy", None),
        check_vma=False,
    )
```

```python
import jax
import jax.numpy as jnp
from jax import lax
from jax.experimental import pallas as pl
from jax.experimental.pallas import tpu as pltpu
from jax.sharding import PartitionSpec as P

SWEEPS = 4
NCLS = 8
CX, CY, NZ = 16, 32, 1024
LW = 128
SEG = 256
CAP = 64
NGX, NGY = 32, 8
CHUNK = CAP + 8
YT = 8
NT = CY // YT
PARTS = 8
F32, BF16 = jnp.float32, jnp.bfloat16
HIGH = lax.Precision.HIGHEST
VM = pl.BlockSpec(memory_space=pltpu.VMEM)
SM = pl.BlockSpec(memory_space=pltpu.SMEM)
HB = pl.BlockSpec(memory_space=pltpu.HBM)


def local(*dims, dtype=F32):
    return pltpu.VMEM(dims, dtype)


def near(*arrays):
    return [pltpu.with_memory_space_constraint(a, pltpu.VMEM) for a in arrays]


def far(*arrays):
    return [pltpu.with_memory_space_constraint(a, pltpu.HBM) for a in arrays]


def lookup(klass, table):
    cond = jnp.where(klass == 0, table[0], F32(0.0))
    for k in range(1, NCLS):
        cond = jnp.where(klass == k, table[k], cond)
    return cond


def load(pairs, sems):
    copies = [pltpu.make_async_copy(src, dst, sems.at[i]) for i, (src, dst) in enumerate(pairs)]
    for copy in copies:
        copy.start()
    for copy in copies:
        copy.wait()


def even(axis):
    return lax.rem(lax.axis_index(axis), 2) == 0


def split(a, b, is_even):
    return jnp.where(is_even, b, a), jnp.where(is_even, a, b)


def start_kernel(t_hbm, soil_hbm, loss_hbm, owner_hbm, col_hbm, send_ref, xa, xb, ya, yb,
                 t_lo, t_hi, s_lo, s_hi, tx, sx, loss_ref, owner_ref, col_ref, sems):
    pairs = [(loss_hbm, loss_ref), (owner_hbm, owner_ref), (col_hbm, col_ref),
             (t_hbm.at[:, 0:YT], t_lo), (t_hbm.at[:, CY - YT:CY], t_hi),
             (soil_hbm.at[:, 0:YT], s_lo), (soil_hbm.at[:, CY - YT:CY], s_hi),
             (t_hbm.at[0], tx.at[0]), (t_hbm.at[CX - 1], tx.at[1]),
             (soil_hbm.at[0], sx.at[0]), (soil_hbm.at[CX - 1], sx.at[1])]
    copies = [pltpu.make_async_copy(src, dst, sems.at[i]) for i, (src, dst) in enumerate(pairs)]
    for copy in copies:
        copy.start()
    for copy in copies[:3]:
        copy.wait()
    own = owner_ref[...]
    mine = lax.broadcasted_iota(jnp.int32, (NGY, SEG), 0) == own
    before = lax.broadcasted_iota(jnp.int32, (SEG, SEG), 0) < lax.broadcasted_iota(jnp.int32, (SEG, SEG), 1)
    count = jnp.dot(mine.astype(F32).astype(BF16), before.astype(F32).astype(BF16), preferred_element_type=F32)
    rank = jnp.sum(jnp.where(mine, count, 0.0), axis=0, keepdims=True).astype(jnp.int32)
    slot = own * CAP + rank
    pick = (lax.broadcasted_iota(jnp.int32, (NGY * CAP, SEG), 0) == slot).astype(F32).astype(BF16)
    loss = loss_ref[...]
    sent = jnp.zeros((NGY * CAP, LW), F32)
    for _ in range(3):
        part = loss.astype(BF16)
        loss = loss - part.astype(F32)
        sent = sent + jnp.dot(pick, part, preferred_element_type=F32)
    col = jnp.broadcast_to(col_ref[...], (8, SEG))
    low = lax.rem(col, 128)
    by_lane = (((1,), (1,)), ((), ()))
    cols = lax.dot_general(low.astype(F32).astype(BF16), pick, by_lane, preferred_element_type=F32)
    cols = cols + lax.dot_general((col - low).astype(F32).astype(BF16), pick, by_lane, preferred_element_type=F32)
    for o in range(NGY):
        send_ref[o * CHUNK:o * CHUNK + CAP, :] = sent[o * CAP:(o + 1) * CAP, :]
        crow = cols[:, o * CAP:(o + 1) * CAP]
        send_ref[o * CHUNK + CAP:(o + 1) * CHUNK, :] = jnp.concatenate([crow, crow], axis=1)
    for copy in copies[3:]:
        copy.wait()
    even_x, even_y = even("gx"), even("gy")
    for x in range(CX):
        ya[x:x + 1, :], yb[x:x + 1, :] = split(t_lo[x, 0:1, :], t_hi[x, YT - 1:YT, :], even_y)
        s_a, s_b = split(s_lo[x, 0:1, :], s_hi[x, YT - 1:YT, :], even_y)
        ya[CX + x:CX + x + 1, :] = s_a.astype(F32)
        yb[CX + x:CX + x + 1, :] = s_b.astype(F32)
    xa[0:CY, :], xb[0:CY, :] = split(tx[0], tx[1], even_x)
    s_a, s_b = split(sx[0], sx[1], even_x)
    xa[CY:, :] = s_a.astype(F32)
    xb[CY:, :] = s_b.astype(F32)


def add_source(recv_ref, inj, out_ref):
    lane = lax.broadcasted_iota(jnp.int32, (1, 2 * CAP), 1)
    cell = lax.broadcasted_iota(jnp.int32, (CX * CY, 2 * CAP), 0)
    pick, loss = [], []
    for g in range(0, NGY, 2):
        a, b = g * CHUNK, (g + 1) * CHUNK
        crow = jnp.where(lane < CAP, recv_ref[a + CAP:a + CAP + 1, :], recv_ref[b + CAP:b + CAP + 1, :])
        pick.append((cell == crow.astype(jnp.int32)).astype(F32).astype(BF16))
        loss += [recv_ref[a:a + CAP, :], recv_ref[b:b + CAP, :]]
    pick = jnp.concatenate(pick, axis=1)
    loss = jnp.concatenate(loss, axis=0)
    gathered = jnp.zeros((CX * CY, LW), F32)
    for _ in range(3):
        part = loss.astype(BF16)
        loss = loss - part.astype(F32)
        gathered = gathered + jnp.dot(pick, part, preferred_element_type=F32)
    high = gathered.astype(BF16)
    low = (gathered - high.astype(F32)).astype(BF16)
    left = jnp.concatenate([high, low, high], axis=1)
    width = 256
    for n in range(0, NZ, width):
        cut = slice(n, n + width)
        both = inj[:, cut]
        top = both.astype(BF16)
        right = jnp.concatenate([top, top, (both - top.astype(F32)).astype(BF16)], axis=0)
        out_ref[:, :, cut] = jnp.dot(left, right, preferred_element_type=F32).reshape(CX, CY, width)


def tile_sides(ref, x, yt):
    mid = ref[x, yt * YT:(yt + 1) * YT, :]
    row = lax.broadcasted_iota(jnp.int32, (YT, NZ), 0)
    up, down = pltpu.roll(mid, YT - 1, 0), pltpu.roll(mid, 1, 0)
    if yt < NT - 1:
        up = jnp.where(row == YT - 1, ref[x, (yt + 1) * YT:(yt + 1) * YT + 1, :], up)
    if yt > 0:
        down = jnp.where(row == 0, ref[x, yt * YT - 1:yt * YT, :], down)
    return mid, up, down


def coef_kernel(table_ref, hyb, hya, t_hbm, cap_hbm, soil_hbm, *refs):
    outs, (more_ref, halo_ref, ex_ref, ey_ref, half_ref, t_ref, cap, soil), made, (in_sems, out_sems) = (
        refs[:6], refs[6:14], refs[14:20], refs[20:])
    fx_ref, fy_ref, fz_ref, rhs_ref, tn_ref, w_ref = made
    step = CX // PARTS
    spans = [pl.ds(part * step, step) for part in range(PARTS)]
    copies = []
    for k, (src, dst) in enumerate(((soil_hbm, soil), (t_hbm, t_ref), (cap_hbm, cap))):
        copies.append([pltpu.make_async_copy(src.at[span], dst.at[span], in_sems.at[k, part]) for part, span in enumerate(spans)])
        for copy in copies[k]:
            copy.start()
    table = [0.5 * table_ref[k] for k in range(NCLS)]
    gy = lax.axis_index("gy")
    halo = split(hya[...], hyb[...], even("gy"))
    for k, inside in enumerate((gy > 0, gy < NGY - 1)):
        more_ref[k] = lookup(halo[k][CX:].astype(jnp.int32), table) * jnp.where(inside, F32(1.0), F32(0.0))
        halo_ref[k] = halo[k][0:CX]

    def fill(x, carry):
        half_ref[x] = lookup(soil[x], table)
        return carry

    for part in range(PARTS):
        copies[0][part].wait()
        lax.fori_loop(part * step, (part + 1) * step, fill, 0)
    for part in range(PARTS):
        copies[1][part].wait()
        copies[2][part].wait()
    for side, x in enumerate((0, CX - 1)):
        ex_ref[side, 0] = half_ref[x]
        ex_ref[side, 1] = t_ref[x]
    row = lax.broadcasted_iota(jnp.int32, (YT, NZ), 0)
    lane = lax.broadcasted_iota(jnp.int32, (YT, NZ), 1)
    at_end = lane == NZ - 1
    at_ends = jnp.logical_or(at_end, lane == 0)

    def plane(x, first, last):
        for yt in range(NT):
            rows = slice(yt * YT, (yt + 1) * YT)
            low, high = yt == 0, yt == NT - 1
            c, cyp, cym = tile_sides(half_ref, x, yt)
            t, typ, tym = tile_sides(t_ref, x, yt)
            fyp, fym = c + cyp, c + cym
            fz = jnp.where(at_end, F32(0.0), c + pltpu.roll(c, NZ - 1, 1))
            cp = cap[x, rows, :]
            diag = cp + fz + pltpu.roll(fz, 1, 1) + jnp.where(at_ends, c, F32(0.0))
            if high:
                diag = diag + jnp.where(row == YT - 1, c, fyp)
                fyp = jnp.where(row == YT - 1, F32(0.0), fyp)
            else:
                diag = diag + fyp
            if low:
                diag = diag + jnp.where(row == 0, c, fym)
                fym = jnp.where(row == 0, F32(0.0), fym)
            else:
                diag = diag + fym
            rhs = cp * t
            total = rhs + fyp * typ + fym * tym
            if last:
                diag = diag + c
            else:
                fxp = c + half_ref[x + 1, rows, :]
                diag = diag + fxp
                total = total + fxp * t_ref[x + 1, rows, :]
                fx_ref[x, rows, :] = fxp
            if first:
                diag = diag + c
            else:
                fxm = c + half_ref[x - 1, rows, :]
                diag = diag + fxm
                total = total + fxm * t_ref[x - 1, rows, :]
            total = total + fz * pltpu.roll(t, NZ - 1, 1) + pltpu.roll(fz * t, 1, 1)
            rhs_ref[x, rows, :] = rhs
            fy_ref[x, rows, :] = fyp
            fz_ref[x, rows, :] = fz
            if first or last:
                w_ref[x, rows, :] = diag
                tn_ref[x, rows, :] = total
            else:
                w = 0.8 / diag
                w_ref[x, rows, :] = w
                tn_ref[x, rows, :] = (1.0 - 0.8) * t + w * total
            if low or high:
                at = slice(0, 1) if low else slice(YT - 1, YT)
                side = 0 if low else 1
                for k, value in enumerate((total, diag, c, t)):
                    ey_ref[side, k, pl.ds(x, 1), :] = value[at, :]

    def inner(x, carry):
        plane(x, False, False)
        return carry

    leaving = []
    for part in range(PARTS):
        if part == 0:
            plane(0, True, False)
        lax.fori_loop(max(1, part * step), min(CX - 1, (part + 1) * step), inner, 0)
        if part == PARTS - 1:
            fx_ref[CX - 1] = jnp.zeros((CY, NZ), F32)
            plane(CX - 1, False, True)
        for k in range(6):
            leaving.append(pltpu.make_async_copy(made[k].at[spans[part]], outs[k].at[spans[part]], out_sems.at[k, part]))
            leaving[-1].start()
    for copy in leaving:
        copy.wait()


def source_kernel(recv_ref, inj_ref, rhs_hbm, tn_hbm, w_hbm, ey_in, rhs_ref, tn_ref, w_ref, ey_ref, source, sems):
    step = CX // 4
    pairs = ((rhs_hbm, rhs_ref), (w_hbm, w_ref), (tn_hbm, tn_ref))
    copies = [[pltpu.make_async_copy(src.at[pl.ds(part * step, step)], dst.at[pl.ds(part * step, step)], sems.at[k, part])
               for k, (src, dst) in enumerate(pairs)] for part in range(4)]
    for part in copies:
        for copy in part:
            copy.start()
    add_source(recv_ref, inj_ref, source)

    def plane(x, edge):
        for yt in range(NT):
            rows = slice(yt * YT, (yt + 1) * YT)
            src = source[x, rows, :]
            rhs_ref[x, rows, :] = rhs_ref[x, rows, :] + src
            tn_ref[x, rows, :] = tn_ref[x, rows, :] + (src if edge else w_ref[x, rows, :] * src)
        for side, y in enumerate((0, CY - 1)):
            ey_ref[side, 0, pl.ds(x, 1), :] = ey_in[side, 0, pl.ds(x, 1), :] + source[x, y:y + 1, :]

    def inner(x, carry):
        plane(x, False)
        return carry

    for part in range(4):
        for copy in copies[part]:
            copy.wait()
        if part == 0:
            plane(0, True)
        lax.fori_loop(max(1, part * step), min(CX - 1, (part + 1) * step), inner, 0)
    plane(CX - 1, True)


def at_row(shape, index, value):
    return jnp.where(lax.broadcasted_iota(jnp.int32, shape, 0) == index, value, F32(0.0))


def with_corners(xlo, xhi, ylo, yhi):
    xs, ys = xlo.shape, ylo.shape
    return (xlo + at_row(xs, 0, ylo[0:1]) + at_row(xs, CY - 1, yhi[0:1]),
            xhi + at_row(xs, 0, ylo[CX - 1:CX]) + at_row(xs, CY - 1, yhi[CX - 1:CX]),
            ylo + at_row(ys, 0, xlo[0:1]) + at_row(ys, CX - 1, xhi[0:1]),
            yhi + at_row(ys, 0, xlo[CY - 1:CY]) + at_row(ys, CX - 1, xhi[CY - 1:CY]))


def fix_kernel(table_ref, hxb, hxa, my_ref, ty_ref, w_ref, tn_ref, ex_ref, ey_ref,
               xa, xb, ya, yb, wx_ref, wy_ref, ax_ref, ay_ref):
    table = [0.5 * table_ref[k] for k in range(NCLS)]
    gx, gy = lax.axis_index("gx"), lax.axis_index("gy")
    within = [jnp.where(q, F32(1.0), F32(0.0)) for q in (gx > 0, gx < NGX - 1, gy > 0, gy < NGY - 1)]
    t_halo = split(hxa[0:CY, :], hxb[0:CY, :], even("gx")) + (ty_ref[0], ty_ref[1])
    klass = split(hxa[CY:, :], hxb[CY:, :], even("gx"))
    more = [lookup(k.astype(jnp.int32), table) * q for k, q in zip(klass, within)] + [my_ref[0], my_ref[1]]
    conds = (ex_ref[0, 0], ex_ref[1, 0], ey_ref[0, 2], ey_ref[1, 2])
    face = [(c + m) * q for c, m, q in zip(conds, more, within)]
    diag = with_corners(*more)
    total = with_corners(*[f * t for f, t in zip(face, t_halo)])
    total = [a + b for a, b in zip(total, (tn_ref[0], tn_ref[CX - 1], ey_ref[0, 0], ey_ref[1, 0]))]
    w = [0.8 / (a + b) for a, b in zip(diag, (w_ref[0], w_ref[CX - 1], ey_ref[0, 1], ey_ref[1, 1]))]
    old = (ex_ref[0, 1], ex_ref[1, 1], ey_ref[0, 3], ey_ref[1, 3])
    new = [(1.0 - 0.8) * t + a * b for t, a, b in zip(old, w, total)]
    xa[...], xb[...] = split(new[0], new[1], even("gx"))
    ya[...], yb[...] = split(new[2], new[3], even("gy"))
    for k in range(2):
        wx_ref[k], wy_ref[k] = w[k], w[2 + k]
        ax_ref[k], ay_ref[k] = w[k] * face[k], w[2 + k] * face[2 + k]


def y_term_kernel(ay_ref, hyb, hya, gy_ref):
    lo, hi = split(hya[...], hyb[...], even("gy"))
    gy_ref[0] = ay_ref[0] * lo
    gy_ref[1] = ay_ref[1] * hi


def faces_of(tn_ref, py_ref, ax_ref, gy_ref, hxb, hxa):
    lo, hi = split(hxa[...], hxb[...], even("gx"))
    terms = with_corners(ax_ref[0] * lo, ax_ref[1] * hi, gy_ref[0], gy_ref[1])
    return [a + b for a, b in zip(terms, (tn_ref[0], tn_ref[CX - 1], py_ref[0], py_ref[1]))]


def edge_kernel(tn_ref, py_ref, ax_ref, gy_ref, hxb, hxa, xa, xb, ya, yb):
    new = faces_of(tn_ref, py_ref, ax_ref, gy_ref, hxb, hxa)
    xa[...], xb[...] = split(new[0], new[1], even("gx"))
    ya[...], yb[...] = split(new[2], new[3], even("gy"))


def put_edges(ref, xlo, xhi, ylo, yhi):
    ref[0] = xlo
    ref[CX - 1] = xhi
    for x in range(1, CX - 1):
        ref[x, 0:1, :] = ylo[x:x + 1]
        ref[x, CY - 1:CY, :] = yhi[x:x + 1]


def sweep_plane(x, first, last, t_ref, fx_ref, fy_ref, fz_ref, w_ref, rhs_ref, tn_ref, py_ref):
    row = lax.broadcasted_iota(jnp.int32, (YT, NZ), 0)
    for yt in range(NT):
        rows = slice(yt * YT, (yt + 1) * YT)
        t, typ, tym = tile_sides(t_ref, x, yt)
        fy, _, fym = tile_sides(fy_ref, x, yt)
        if yt == 0:
            fym = jnp.where(row == 0, F32(0.0), fym)
        fz = fz_ref[x, rows, :]
        total = rhs_ref[x, rows, :] + fy * typ + fym * tym
        if not last:
            total = total + fx_ref[x, rows, :] * t_ref[x + 1, rows, :]
        if not first:
            total = total + fx_ref[x - 1, rows, :] * t_ref[x - 1, rows, :]
        total = total + fz * pltpu.roll(t, NZ - 1, 1)
        total = total + pltpu.roll(fz * t, 1, 1)
        tn = (1.0 - 0.8) * t + w_ref[x, rows, :] * total
        tn_ref[x, rows, :] = tn
        if yt == 0:
            py_ref[0, pl.ds(x, 1), :] = tn[0:1, :]
        if yt == NT - 1:
            py_ref[1, pl.ds(x, 1), :] = tn[YT - 1:YT, :]


def sweep_inside(refs, start=1, stop=CX - 1):
    def inner(x, carry):
        sweep_plane(x, False, False, *refs)
        return carry

    lax.fori_loop(start, stop, inner, 0)


def first_sweep_kernel(fx_ref, fy_ref, fz_ref, rhs_ref, xa, xb, ya, yb, wx_ref, wy_ref, w_in, t_in,
                       w_ref, t_ref, tn_ref, py_ref):
    put_edges(w_ref, wx_ref[0], wx_ref[1], wy_ref[0], wy_ref[1])
    sweep(fx_ref, fy_ref, fz_ref, rhs_ref, w_ref, xa, xb, ya, yb, t_ref, tn_ref, py_ref)


def sweep(fx_ref, fy_ref, fz_ref, rhs_ref, w_ref, xa, xb, ya, yb, t_ref, tn_ref, py_ref):
    put_edges(t_ref, *split(xa[...], xb[...], even("gx")), *split(ya[...], yb[...], even("gy")))
    refs = (t_ref, fx_ref, fy_ref, fz_ref, w_ref, rhs_ref, tn_ref, py_ref)
    sweep_plane(0, True, False, *refs)
    sweep_inside(refs)
    sweep_plane(CX - 1, False, True, *refs)


def sweep_kernel(fx_ref, fy_ref, fz_ref, rhs_ref, w_ref, xa, xb, ya, yb, t_in, t_ref, tn_ref, py_ref):
    sweep(fx_ref, fy_ref, fz_ref, rhs_ref, w_ref, xa, xb, ya, yb, t_ref, tn_ref, py_ref)


def last_sweep_kernel(fx_ref, fy_ref, fz_ref, rhs_ref, w_ref, xa, xb, ya, yb, t_in, t_ref, tn_ref, py_ref, out_ref, sems):
    put_edges(t_ref, *split(xa[...], xb[...], even("gx")), *split(ya[...], yb[...], even("gy")))
    refs = (t_ref, fx_ref, fy_ref, fz_ref, w_ref, rhs_ref, tn_ref, py_ref)
    bounds = list(range(1, CX - 1, 4)) + [CX - 1]
    copies = []
    for k, (start, stop) in enumerate(zip(bounds[:-1], bounds[1:])):
        sweep_inside(refs, start, stop)
        part = (pl.ds(start, stop - start), pl.ds(YT, CY - 2 * YT))
        copies.append(pltpu.make_async_copy(tn_ref.at[part], out_ref.at[part], sems.at[k]))
        copies[-1].start()
    sweep_plane(0, True, False, *refs)
    sweep_plane(CX - 1, False, True, *refs)
    for copy in copies:
        copy.wait()


def finish_kernel(tn_ref, py_ref, ax_ref, gy_ref, hxb, hxa, out_in, out_ref, x_out, lo_out, hi_out, sems):
    xlo, xhi, ylo, yhi = faces_of(tn_ref, py_ref, ax_ref, gy_ref, hxb, hxa)
    x_out[0] = xlo
    x_out[1] = xhi
    row = lax.broadcasted_iota(jnp.int32, (YT, NZ), 0)
    for x in range(1, CX - 1):
        lo_out[x - 1] = jnp.where(row == 0, ylo[x:x + 1], tn_ref[x, 0:YT, :])
        hi_out[x - 1] = jnp.where(row == YT - 1, yhi[x:x + 1], tn_ref[x, CY - YT:CY, :])
    inside = pl.ds(1, CX - 2)
    load([(x_out.at[0], out_ref.at[0]), (x_out.at[1], out_ref.at[CX - 1]),
          (lo_out, out_ref.at[inside, 0:YT]), (hi_out, out_ref.at[inside, CY - YT:CY])], sems)


def swap(value, partner):
    there = [partner(gx, gy) for gx in range(NGX) for gy in range(NGY)]
    return lax.ppermute(value, ("gx", "gy"), [(i, x * NGY + y) for i, (x, y) in enumerate(there)])


def odd_x(gx, gy):
    if gx in (0, NGX - 1):
        return gx, gy ^ 2
    return (gx + 1 if gx % 2 else gx - 1), gy


def odd_y(gx, gy):
    if gy in (0, NGY - 1):
        return gx ^ 1, gy
    return gx, (gy + 1 if gy % 2 else gy - 1)


def exchange(xa, xb, ya, yb):
    xb, xa = swap(xb, odd_x), swap(xa, lambda gx, gy: (gx ^ 1, gy))
    yb, ya = swap(yb, odd_y), swap(ya, lambda gx, gy: (gx, gy ^ 1))
    return near(xa, xb, ya, yb)


def call(kernel, outs, specs, scratch=(), alias={}, mib=1, us=0.1, out_specs=None):
    return pl.pallas_call(
        kernel,
        out_shape=outs,
        in_specs=specs,
        out_specs=out_specs or [VM] * len(outs),
        scratch_shapes=scratch,
        input_output_aliases=alias,
        compiler_params=pltpu.CompilerParams(vmem_limit_bytes=mib * 1024 * 1024),
        cost_estimate=pl.CostEstimate(flops=int(us * 1e9), bytes_accessed=int(us * 3e6), transcendentals=0),
    )


SLAB = local(CX, CY, NZ)
FACES = (local(CY, NZ), local(CY, NZ), local(CX, NZ), local(CX, NZ))
XX, YY = local(2, CY, NZ), local(2, CX, NZ)
DMA = pltpu.SemaphoreType.DMA
I32 = jnp.int32
FIXY, PREP = 20.0, 0.1


def shards(temp_old, capacity, soil_class, cond_table, losses, owner, column, injection):
    rows, rows_int = local(CX, YT, NZ), local(CX, YT, NZ, dtype=I32)
    send, *faces = call(
        start_kernel, (local(NGY * CHUNK, LW),) + (local(2 * CY, NZ),) * 2 + (local(2 * CX, NZ),) * 2, [HB] * 5,
        [rows, rows, rows_int, rows_int, XX, local(2, CY, NZ, dtype=I32), local(SEG, LW), local(1, SEG, dtype=I32),
         local(1, SEG, dtype=I32), DMA((11,))], mib=6)(
        *far(temp_old, soil_class, losses, owner.reshape(1, SEG), column.reshape(1, SEG)))
    recv = lax.all_to_all(send, "gy", 0, 0, tiled=True)
    halo = exchange(*faces)
    hxa, hxb, hya, hyb = halo
    edge_x, edge_y = local(2, 2, CY, NZ), local(2, 4, CX, NZ)
    *stored, my, ty, ex, ey = call(
        coef_kernel, (pltpu.HBM((CX, CY, NZ), F32),) * 6 + (YY, YY, edge_x, edge_y), [SM] + [VM] * 2 + [HB] * 3,
        [SLAB, SLAB, SLAB, local(CX, CY, NZ, dtype=I32)] + [SLAB] * 6 + [DMA((3, PARTS)), DMA((6, PARTS))],
        mib=24, us=FIXY, out_specs=[HB] * 6 + [VM] * 4)(
        cond_table, hyb, hya, *far(temp_old, capacity, soil_class))
    rhs, new, w, ey = call(
        source_kernel, (SLAB,) * 3 + (edge_y,), [VM] * 2 + [HB] * 3 + [VM], [SLAB, DMA((3, 4))],
        alias={5: 3}, mib=8, us=PREP)(*near(recv, injection), *far(*stored[3:]), *near(ey))
    *faces, wx, wy, ax, ay = call(fix_kernel, FACES + (XX, YY, XX, YY), [SM] + [VM] * 8, mib=2)(
        cond_table, hxb, hxa, *near(my, ty, w, new, ex, ey))
    for number in range(1, SWEEPS):
        halo = exchange(*faces)
        if number == 1:
            coefs = near(*stored[:3], rhs)
            w, temp, new, py = call(
                first_sweep_kernel, (SLAB, SLAB, SLAB, YY), [VM] * 12, alias={10: 0, 11: 1}, mib=2)(
                *coefs, *near(*faces, wx, wy, w, new))
        elif number < SWEEPS - 1:
            temp, new, py = call(sweep_kernel, (SLAB, SLAB, YY), [VM] * 10, alias={9: 0}, mib=2)(
                *coefs, *near(w, *faces, new))
        else:
            temp, new, py, out = call(
                last_sweep_kernel, (SLAB, SLAB, YY, pltpu.HBM((CX, CY, NZ), F32)), [VM] * 10, [DMA((4,))],
                alias={9: 0}, mib=2, out_specs=[VM] * 3 + [HB])(*coefs, *near(w, *faces, new))
        hxa, hxb, hya, hyb = halo
        (gy,) = call(y_term_kernel, (YY,), [VM] * 3, us=8.0)(*near(ay), hyb, hya)
        args = near(new, py, ax, gy) + [hxb, hxa]
        if number < SWEEPS - 1:
            faces = call(edge_kernel, FACES, [VM] * 6, mib=2)(*args)
    return call(finish_kernel, (pltpu.HBM((CX, CY, NZ), F32),), [VM] * 6 + [HB],
                [XX, local(CX - 2, YT, NZ), local(CX - 2, YT, NZ), DMA((4,))], alias={6: 0}, mib=4, out_specs=[HB])(*args, out)[0]


def solution(mesh):
    return jax.shard_map(
        shards,
        mesh=mesh,
        in_specs=(
            P("gx", "gy", None),
            P("gx", "gy", None),
            P("gx", "gy", None),
            P(),
            P(("gx", "gy"), None),
            P(("gx", "gy"), None),
            P(("gx", "gy")),
            P(),
        ),
        out_specs=P("gx", "gy", None),
        check_vma=False,
    )
```
